32 devices in a mesh: dev: 32 (over z, y, x, core).
Axes of the slice: x: 2, y: 2, z: 4, core: 2. Of those that a mesh axis runs over, the one named last changes fastest.
Arguments:
- master: float32 [2, 3, 1024, 256], P(None, None, 'dev'), may hold values from -0.18 to 0.18
- first_moment: float32 [2, 3, 1024, 256], P(None, None, 'dev'), may hold values from -2 to 2
- second_moment: float32 [2, 3, 1024, 256], P(None, None, 'dev'), may hold values from 0.05 to 2
- old_rows: bfloat16 [32, 256, 1024], P('dev'), may hold values from -6 to 6
- old_cotangent: bfloat16 [32, 256, 1024], P('dev'), may hold values from -0.08984375 to 0.08984375
- new_rows: bfloat16 [32, 256, 1024], P('dev'), may hold values from -6 to 6
- old_slots: int32 [32], replicated, may hold values from 0 to 1
- new_slots: int32 [32], replicated, may hold values from 0 to 1
- live_rows: int32 [32], P('dev'), may hold values from 64 to 256, as said below
Outputs:
- new_master: float32 [2, 3, 1024, 256], P(None, None, 'dev')
- new_first: float32 [2, 3, 1024, 256], P(None, None, 'dev')
- new_second: float32 [2, 3, 1024, 256], P(None, None, 'dev')
- new_outputs: bfloat16 [32, 256, 1024], P('dev')
The draws below stay inside these ranges and needn't reach their ends.
Inputs may be any that keep to these rules, and one draw needn't show every extreme that they name: `live_rows`: some slot has all 256 rows live in every draw.
All inputs are finite; a program needn't handle non-finite values.
Results may differ from the reference program's by a relative error of at most 0.0059.
The reference program's roundings to bfloat16 on the way count: a program that leaves them out, or rounds other values in their place, can miss the bound.
Values may be sent and summed in bfloat16 or wider, within the bound.
No kernel may reach another device: no remote copies, remote signals or barrier semaphores. Data moves between devices by JAX's collectives and lax.ppermute only.
A program may use at most 64 MiB of HBM per device.

```python
import math
import jax
import jax.numpy as jnp
import numpy as np
from jax import lax

D = 1024
HB = 256
ROWS = 256
NB = 2
SLOTS = 32


def draw_live_rows(key, part):
    first_key, second_key = jax.random.split(jax.random.fold_in(key, 71))
    counts = jax.random.randint(first_key, (SLOTS,), ROWS // 4, ROWS + 1).astype(jnp.int32)
    chosen = jax.random.randint(second_key, (), 0, SLOTS)
    return counts.at[chosen].set(ROWS).astype(jnp.int32)


def place_ends(drawn, stream_key, least, top_value):
    longest = drawn.shape.index(max(drawn.shape))
    spots = []
    for shift in (0, 1):
        where = [jax.random.randint(jax.random.fold_in(stream_key, axis), (), 0, length) for axis, length in enumerate(drawn.shape)]
        where[longest] = (where[longest] + shift) % drawn.shape[longest]
        spots.append(tuple(where))
    return drawn.at[spots[0]].set(least).at[spots[1]].set(top_value)


def shard_levels(rng, shape, shards, low, top_value):
    def one(position, blocks):
        draws = jax.random.uniform(jax.random.fold_in(jax.random.fold_in(rng, 6), position), (blocks,), jnp.float32, low / len(shards), top_value / len(shards))
        return jnp.repeat(jnp.exp(draws), shape[position] // blocks).reshape((-1,) + (1,) * (len(shape) - position - 1))

    level = one(*shards[0])
    for cut in shards[1:]:
        level = level * one(*cut)
    return level


def cumulative_ranks(amount, lean):
    weights = [(1 << 20) // math.isqrt(standing ** lean) + 1 for standing in range(1, amount + 1)]
    spread = 1 + sum(weights) // (1 << 30)
    return np.cumsum(np.array([max(1, weight // spread) for weight in weights]))


def ranked_ids(stream_key, extent, number_of, slope):
    grid = cumulative_ranks(number_of, slope)
    pick = jax.random.randint(jax.random.fold_in(stream_key, 1), extent, 0, int(grid[number_of - 1]))
    standing = jnp.searchsorted(jnp.asarray(grid, jnp.int32), pick, side="right")
    return jax.random.permutation(jax.random.fold_in(stream_key, 2), number_of)[standing].astype(jnp.int32)


def noise(rng, extent, scale, limit, cuts=(), kind=jnp.bfloat16):
    gain = shard_levels(rng, extent, cuts, -0.22, 0.18) if cuts else 1.0
    drawn = jax.random.normal(rng, extent, jnp.float32) * scale * gain
    return jnp.minimum(jnp.maximum(drawn, -limit), limit).astype(kind)


def setup_inputs(seed: int = 0) -> dict:
    keys = jax.random.split(jax.random.key(seed), 10)
    return {
        "master": noise(keys[0], (NB, 3, D, HB), 0.03, 0.18, ((2, 32),), jnp.float32),
        "first_moment": noise(keys[1], (NB, 3, D, HB), 0.3, 2.0, ((2, 32),), jnp.float32),
        "second_moment": jnp.clip(jnp.exp(math.log(2.0) - 3.6888794 * jax.random.uniform(keys[2], (NB, 3, D, HB), jnp.float32) ** shard_levels(keys[2], (NB, 3, D, HB), ((2, 32),), -0.2, 0.2)), 0.05, 2.0),
        "old_rows": noise(keys[3], (SLOTS, ROWS, D), 1.0, 6.0, ((0, 32),)),
        "old_cotangent": noise(keys[4], (SLOTS, ROWS, D), 0.015, 0.08984375, ((0, 32),)),
        "new_rows": noise(keys[5], (SLOTS, ROWS, D), 1.0, 6.0, ((0, 32),)),
        "old_slots": place_ends(ranked_ids(keys[6], (SLOTS,), NB, 2), jax.random.fold_in(keys[6], 3), 0, NB - 1).astype(jnp.int32),
        "new_slots": place_ends(ranked_ids(keys[7], (SLOTS,), NB, 2), jax.random.fold_in(keys[7], 3), 0, NB - 1).astype(jnp.int32),
        "live_rows": draw_live_rows(jax.random.fold_in(keys[9], 71), 0),
    }


beta_one = 0.9
beta_two = 0.95
corr_one = 0.9999734386011124
corr_two = 0.994079470779666
adam_eps = 1e-08
learn_rate = 0.003
decay_rate = 0.1

def expert_grads(tokens, cotangent, weights, live):
    positions = jnp.arange(tokens.shape[0], dtype=jnp.int32)
    cotangent = jnp.where((positions < live)[:, None], cotangent, jnp.zeros_like(cotangent))
    gate_pre = jnp.dot(tokens, weights[0], preferred_element_type=jnp.float32)
    up_pre = jnp.dot(tokens, weights[1], preferred_element_type=jnp.float32)
    gate_sig = jax.nn.sigmoid(gate_pre)
    gate_act = gate_pre * gate_sig
    hidden = (gate_act * up_pre).astype(jnp.bfloat16)
    grad_down = lax.dot_general(cotangent, hidden, (((0,), (0,)), ((), ())), preferred_element_type=jnp.float32)
    grad_hidden = jnp.dot(cotangent, weights[2], preferred_element_type=jnp.float32)
    grad_up_pre = (grad_hidden * gate_act).astype(jnp.bfloat16)
    grad_gate_pre = (grad_hidden * up_pre * gate_sig * (1.0 + gate_pre * (1.0 - gate_sig))).astype(jnp.bfloat16)
    grad_gate = lax.dot_general(tokens, grad_gate_pre, (((0,), (0,)), ((), ())), preferred_element_type=jnp.float32)
    grad_up = lax.dot_general(tokens, grad_up_pre, (((0,), (0,)), ((), ())), preferred_element_type=jnp.float32)
    return jnp.stack([grad_gate, grad_up, grad_down])

def adam_update(master, first, second, grad):
    first_new = beta_one * first + (1.0 - beta_one) * grad
    second_new = beta_two * second + (1.0 - beta_two) * grad * grad
    direction = first_new / corr_one / (jnp.sqrt(second_new / corr_two) + adam_eps)
    master_new = master - learn_rate * (direction + decay_rate * master)
    return (master_new, first_new, second_new)

def expert_forward(tokens, weights):
    gate_pre = jnp.dot(tokens, weights[0], preferred_element_type=jnp.float32)
    up_pre = jnp.dot(tokens, weights[1], preferred_element_type=jnp.float32)
    activation = (jax.nn.silu(gate_pre) * up_pre).astype(jnp.bfloat16)
    result = lax.dot_general(activation, weights[2], (((1,), (1,)), ((), ())), preferred_element_type=jnp.float32)
    return result.astype(jnp.bfloat16)

def reference(master, first_moment, second_moment, old_rows, old_cotangent, new_rows, old_slots, new_slots, live_rows):
    old_weights = master.astype(jnp.bfloat16)

    def accumulate(total, item):
        tokens, cotangent, block, live = item
        weights = lax.dynamic_index_in_dim(old_weights, block, 0, keepdims=False)
        grads = expert_grads(tokens, cotangent, weights, live)
        current = lax.dynamic_index_in_dim(total, block, 0, keepdims=False)
        return (lax.dynamic_update_index_in_dim(total, current + grads, block, 0), None)
    total, unused = lax.scan(accumulate, jnp.zeros(master.shape, jnp.float32), (old_rows, old_cotangent, old_slots, live_rows))
    new_master, new_first, new_second = adam_update(master, first_moment, second_moment, total)
    new_weights = new_master.astype(jnp.bfloat16)

    def forward(item):
        tokens, block = item
        weights = lax.dynamic_index_in_dim(new_weights, block, 0, keepdims=False)
        return expert_forward(tokens, weights)
    new_outputs = lax.map(forward, (new_rows, new_slots))
    return (new_master, new_first, new_second, new_outputs)
```

```python
import functools

import jax
import jax.numpy as jnp
from jax import lax
from jax.experimental import pallas as pl
from jax.experimental.pallas import tpu as pltpu
from jax.sharding import PartitionSpec as P

beta_one = 0.9
beta_two = 0.95
corr_one = 0.9999734386011124
corr_two = 0.994079470779666
adam_eps = 1e-08
learn_rate = 0.003
decay_rate = 0.1

CORE, X_STEP, Y_STEP, Z_UNIT = 1, 2, 4, 8
VMEM_LIMIT = 48 * 1024 * 1024


def hop(block, mask):
    count = lax.axis_size("dev")
    return lax.ppermute(block, "dev", [(low, low ^ mask) for low in range(count)])


def adam_update(master, first, second, grad):
    first_new = beta_one * first + (1.0 - beta_one) * grad
    second_new = beta_two * second + (1.0 - beta_two) * grad * grad
    direction = first_new / corr_one / (jnp.sqrt(second_new / corr_two) + adam_eps)
    master_new = master - learn_rate * (direction + decay_rate * master)
    return (master_new, first_new, second_new)


def place_pieces(chip, pieces, weights, sems):
    rows = pieces[0].shape[1]
    copies = []
    for j, piece in enumerate(pieces):
        start = pl.multiple_of(lax.bitwise_xor(chip, j) * rows, rows)
        copies.append(pltpu.make_async_copy(piece, weights.at[:, pl.ds(start, rows), :], sems.at[j]))
    for copy in copies:
        copy.start()
    for copy in copies:
        copy.wait()


def transpose_kernel(chip_ref, own_ref, other_ref, out_ref):
    chip = chip_ref[0]
    tokens, width = own_ref.shape
    count = chip_ref.shape[0] - 1
    rows = width // count
    lanes = max(128, rows)
    for part, ref in enumerate((own_ref, other_ref)):
        for at in range(0, width, lanes):
            turned = ref[:, at : at + lanes].T
            for low in range(0, lanes, rows):
                j = lax.bitwise_xor(chip, (at + low) // rows)
                start = pl.multiple_of(j * rows, rows)
                out_ref[pl.ds(start, rows), part * tokens : (part + 1) * tokens] = turned[low : low + rows]


def backward_kernel(count, chip_ref, *refs):
    pieces = refs[:count]
    own_x, other_x, own_c, other_c, x_turned, c_turned = refs[count : count + 6]
    outs = refs[count + 6 : 2 * count + 6]
    weights, gate_grad, up_grad, hidden_all, sems = refs[2 * count + 6 :]
    place_pieces(chip_ref[0], pieces, weights, sems)
    tokens = own_x.shape[0]
    for part, (x_ref, c_ref) in enumerate(((own_x, own_c), (other_x, other_c))):
        span = slice(part * tokens, (part + 1) * tokens)
        gate_pre = jnp.dot(x_ref[...], weights[0], preferred_element_type=jnp.float32)
        up_pre = jnp.dot(x_ref[...], weights[1], preferred_element_type=jnp.float32)
        grad_hidden = jnp.dot(c_ref[...], weights[2], preferred_element_type=jnp.float32)
        gate_sig = jax.nn.sigmoid(gate_pre)
        gate_act = gate_pre * gate_sig
        hidden_all[span] = (gate_act * up_pre).astype(jnp.bfloat16)
        up_grad[span] = (grad_hidden * gate_act).astype(jnp.bfloat16)
        gate_grad[span] = (grad_hidden * up_pre * gate_sig * (1.0 + gate_pre * (1.0 - gate_sig))).astype(
            jnp.bfloat16
        )
    rows = outs[0].shape[1]
    width = count * rows
    tall = min(width, 256)
    for at in range(0, width, tall):
        for kind, (left, right) in enumerate(
            ((x_turned, gate_grad), (x_turned, up_grad), (c_turned, hidden_all))
        ):
            product = jnp.dot(left[at : at + tall], right[...], preferred_element_type=jnp.float32)
            product = product.astype(jnp.bfloat16)
            for low in range(0, tall, rows):
                outs[(at + low) // rows][kind] = product[low : low + rows]


def forward_kernel(count, chip_ref, *refs):
    pieces = refs[:count]
    own_y, other_y, own_out, other_out, weights, sems = refs[count:]
    place_pieces(chip_ref[0], pieces, weights, sems)
    for y_ref, out_ref in ((other_y, other_out), (own_y, own_out)):
        gate_pre = jnp.dot(y_ref[...], weights[0], preferred_element_type=jnp.float32)
        up_pre = jnp.dot(y_ref[...], weights[1], preferred_element_type=jnp.float32)
        act = (gate_pre * jax.nn.sigmoid(gate_pre) * up_pre).astype(jnp.bfloat16)
        result = lax.dot_general(act, weights[2], (((1,), (1,)), ((), ())), preferred_element_type=jnp.float32)
        out_ref[...] = result.astype(jnp.bfloat16)


VMEM = pl.BlockSpec(memory_space=pltpu.VMEM)
SMEM = pl.BlockSpec(memory_space=pltpu.SMEM)
ANY = pl.BlockSpec(memory_space=pl.ANY)


def params():
    return pltpu.CompilerParams(vmem_limit_bytes=VMEM_LIMIT)


def transposed(chip_ids, own, other):
    tokens, width = own.shape
    return pl.pallas_call(
        transpose_kernel,
        out_shape=jax.ShapeDtypeStruct((width, 2 * tokens), own.dtype),
        in_specs=[SMEM, VMEM, VMEM],
        out_specs=VMEM,
        compiler_params=params(),
        cost_estimate=pl.CostEstimate(flops=0, bytes_accessed=8 * tokens * width, transcendentals=0),
        name="transpose_rows",
    )(chip_ids, own, other)


def backward(chip_ids, pieces, own_x, other_x, own_c, other_c, x_turned, c_turned):
    count = len(pieces)
    kinds, rows, units = pieces[0].shape
    tokens, width = own_x.shape
    return pl.pallas_call(
        functools.partial(backward_kernel, count),
        out_shape=[jax.ShapeDtypeStruct((kinds, rows, units), jnp.bfloat16)] * count,
        in_specs=[SMEM] + [ANY] * count + [VMEM] * 6,
        out_specs=[VMEM] * count,
        scratch_shapes=[
            pltpu.VMEM((kinds, width, units), jnp.bfloat16),
            pltpu.VMEM((2 * tokens, units), jnp.bfloat16),
            pltpu.VMEM((2 * tokens, units), jnp.bfloat16),
            pltpu.VMEM((2 * tokens, units), jnp.bfloat16),
            pltpu.SemaphoreType.DMA((count,)),
        ],
        compiler_params=params(),
        cost_estimate=pl.CostEstimate(
            flops=24 * tokens * width * units,
            bytes_accessed=16 * tokens * width + 12 * width * units,
            transcendentals=2 * tokens * units,
        ),
        name="slot_gradients",
    )(chip_ids, *pieces, own_x, other_x, own_c, other_c, x_turned, c_turned)


def forward(chip_ids, pieces, own_y, other_y):
    count = len(pieces)
    kinds, rows, units = pieces[0].shape
    tokens, width = own_y.shape
    return pl.pallas_call(
        functools.partial(forward_kernel, count),
        out_shape=[jax.ShapeDtypeStruct((tokens, width), jnp.bfloat16)] * 2,
        in_specs=[SMEM] + [ANY] * count + [VMEM] * 2,
        out_specs=[VMEM] * 2,
        scratch_shapes=[
            pltpu.VMEM((kinds, width, units), jnp.bfloat16),
            pltpu.SemaphoreType.DMA((count,)),
        ],
        compiler_params=params(),
        cost_estimate=pl.CostEstimate(
            flops=12 * tokens * width * units,
            bytes_accessed=8 * tokens * width + 6 * width * units,
            transcendentals=2 * tokens * units,
        ),
        name="expert_outputs",
    )(chip_ids, *pieces, own_y, other_y)


def gather_chips(piece):
    depth = lax.axis_size("dev") // Z_UNIT
    column = [piece] + [hop(piece, zj * Z_UNIT) for zj in range(1, depth)]
    pieces = []
    for zj, here in enumerate(column):
        along_x = hop(here, X_STEP)
        along_y = hop(here, Y_STEP)
        across = hop(along_x, Y_STEP) if 2 * zj < depth else hop(along_y, X_STEP)
        pieces += [here, along_x, along_y, across]
    return pieces


def add_pair(one, two):
    return (one.astype(jnp.float32) + two.astype(jnp.float32)).astype(jnp.bfloat16)


def reduce_chips(pieces):
    depth = lax.axis_size("dev") // Z_UNIT
    total = None
    for zj in reversed(range(depth)):
        here, along_x, along_y, across = pieces[4 * zj : 4 * zj + 4]
        if 2 * zj < depth:
            along_y = add_pair(along_y, hop(across, X_STEP))
        else:
            along_x = add_pair(along_x, hop(across, Y_STEP))
        column = (
            here.astype(jnp.float32)
            + hop(along_x, X_STEP).astype(jnp.float32)
            + hop(along_y, Y_STEP).astype(jnp.float32)
        )
        if zj:
            column = hop(column.astype(jnp.bfloat16), zj * Z_UNIT).astype(jnp.float32)
        total = column if total is None else total + column
    return total


def block_a_core(master, first, second, old_rows, old_cotangent, new_rows, own_old, own_new, live):
    local_rows = master.shape[2]
    me_index = lax.axis_index("dev")
    core = me_index & CORE
    chips = lax.axis_size("dev") // 2
    chip_ids = jnp.full((chips + 1,), me_index // 2, jnp.int32)

    def mine(state):
        return lax.dynamic_index_in_dim(state, core, 0, keepdims=False)

    def partners(state):
        return lax.dynamic_index_in_dim(state, 1 - core, 0, keepdims=False)

    def both_rows(own, other):
        return jnp.where(
            core == 0, jnp.concatenate([own, other], axis=-2), jnp.concatenate([other, own], axis=-2)
        )

    master_two = both_rows(mine(master), hop(partners(master), CORE))
    pieces = gather_chips(master_two.astype(jnp.bfloat16))

    positions = jnp.arange(old_rows.shape[0], dtype=jnp.int32)[:, None]
    alive = positions < live
    empty = jnp.zeros_like(old_cotangent)
    own_c = jnp.where(alive & (own_old == core), old_cotangent, empty)
    other_c = hop(jnp.where(alive & (own_old != core), old_cotangent, empty), CORE)
    other_x = hop(old_rows, CORE)
    other_y = hop(new_rows, CORE)
    moments = jnp.stack([first, second], axis=1)
    first_two, second_two = both_rows(mine(moments), hop(partners(moments), CORE))

    x_turned = transposed(chip_ids, old_rows, other_x)
    c_turned = transposed(chip_ids, own_c, other_c)
    grads = backward(chip_ids, pieces, old_rows, other_x, own_c, other_c, x_turned, c_turned)
    grad = reduce_chips(grads)
    updated = adam_update(master_two, first_two, second_two, grad)

    new_pieces = gather_chips(updated[0].astype(jnp.bfloat16))
    updated = jnp.stack(updated)
    own_part = lax.dynamic_slice_in_dim(updated, core * local_rows, local_rows, 2)
    other_part = lax.dynamic_slice_in_dim(updated, (1 - core) * local_rows, local_rows, 2)
    from_other = hop(other_part, CORE)
    state = jnp.where(
        core == 0, jnp.stack([own_part, from_other], axis=1), jnp.stack([from_other, own_part], axis=1)
    )
    own_out, other_out = forward(chip_ids, new_pieces, new_rows, other_y)
    new_outputs = jnp.where(own_new == core, own_out, hop(other_out, CORE))
    return (state[0], state[1], state[2], new_outputs[None])


def hidden_terms(tokens, cotangent, weights, live):
    positions = jnp.arange(tokens.shape[0], dtype=jnp.int32)
    cotangent = jnp.where((positions < live)[:, None], cotangent, jnp.zeros_like(cotangent))
    gate_pre = jnp.dot(tokens, weights[0], preferred_element_type=jnp.float32)
    up_pre = jnp.dot(tokens, weights[1], preferred_element_type=jnp.float32)
    gate_sig = jax.nn.sigmoid(gate_pre)
    gate_act = gate_pre * gate_sig
    hidden = (gate_act * up_pre).astype(jnp.bfloat16)
    grad_down = lax.dot_general(
        cotangent, hidden, (((0,), (0,)), ((), ())), preferred_element_type=jnp.float32
    )
    grad_hidden = jnp.dot(cotangent, weights[2], preferred_element_type=jnp.float32)
    grad_up_pre = (grad_hidden * gate_act).astype(jnp.bfloat16)
    grad_gate_pre = (grad_hidden * up_pre * gate_sig * (1.0 + gate_pre * (1.0 - gate_sig))).astype(
        jnp.bfloat16
    )
    grad_gate = lax.dot_general(
        tokens, grad_gate_pre, (((0,), (0,)), ((), ())), preferred_element_type=jnp.float32
    )
    grad_up = lax.dot_general(
        tokens, grad_up_pre, (((0,), (0,)), ((), ())), preferred_element_type=jnp.float32
    )
    return jnp.stack([grad_gate, grad_up, grad_down])


def expert_forward(tokens, weights):
    gate_pre = jnp.dot(tokens, weights[0], preferred_element_type=jnp.float32)
    up_pre = jnp.dot(tokens, weights[1], preferred_element_type=jnp.float32)
    activation = (jax.nn.silu(gate_pre) * up_pre).astype(jnp.bfloat16)
    result = lax.dot_general(
        activation, weights[2], (((1,), (1,)), ((), ())), preferred_element_type=jnp.float32
    )
    return result.astype(jnp.bfloat16)


def halving(buffer, levels, me_index):
    for step in range(levels):
        count = buffer.shape[2]
        halves = buffer.reshape(buffer.shape[:2] + (count // 2, 2) + buffer.shape[3:])
        own_bit = me_index >> step & 1
        keeping = lax.dynamic_index_in_dim(halves, own_bit, 3, keepdims=False)
        sending = lax.dynamic_index_in_dim(halves, 1 - own_bit, 3, keepdims=False)
        buffer = keeping + hop(sending, 1 << step)
    return buffer


def any_shape(master, first, second, old_rows, old_cotangent, new_rows, own_old, own_new, live):
    blocks, kinds, local_rows, block_width = master.shape
    devices = lax.axis_size("dev")
    me_index = lax.axis_index("dev")
    every_block = lax.all_gather(master.astype(jnp.bfloat16), "dev", axis=2, tiled=True)
    weights = lax.dynamic_index_in_dim(every_block, own_old, 0, keepdims=False)
    slot_grad = hidden_terms(old_rows, old_cotangent, weights, live)
    block_ids = jnp.arange(blocks, dtype=jnp.int32)[:, None, None, None, None]
    dense = slot_grad.reshape(kinds, devices, local_rows, block_width)
    buffer = jnp.where(block_ids == own_old, dense[None], jnp.zeros((), jnp.float32))
    buffer = halving(buffer, devices.bit_length() - 1, me_index)
    grad = buffer.reshape(master.shape)
    new_master, new_first, new_second = adam_update(master, first, second, grad)
    updated_blocks = lax.all_gather(new_master.astype(jnp.bfloat16), "dev", axis=2, tiled=True)
    new_weights = lax.dynamic_index_in_dim(updated_blocks, own_new, 0, keepdims=False)
    return (new_master, new_first, new_second, expert_forward(new_rows, new_weights)[None])


def on_device(
    master,
    first_moment,
    second_moment,
    old_rows,
    old_cotangent,
    new_rows,
    old_slots,
    new_slots,
    live_rows,
):
    blocks, kinds, local_rows, units = master.shape
    devices = lax.axis_size("dev")
    me_index = lax.axis_index("dev")
    own_old = lax.dynamic_index_in_dim(old_slots, me_index, 0, keepdims=False)
    own_new = lax.dynamic_index_in_dim(new_slots, me_index, 0, keepdims=False)
    whole_tiles = local_rows % 16 == 0 and units % 128 == 0 and old_rows.shape[1] % 128 == 0
    form = block_a_core if blocks == 2 and devices % Z_UNIT == 0 and whole_tiles else any_shape
    return form(
        master,
        first_moment,
        second_moment,
        old_rows[0],
        old_cotangent[0],
        new_rows[0],
        own_old,
        own_new,
        live_rows[0],
    )


def solution(mesh):
    return jax.shard_map(
        on_device,
        mesh=mesh,
        in_specs=(
            P(None, None, "dev", None),
            P(None, None, "dev", None),
            P(None, None, "dev", None),
            P("dev", None, None),
            P("dev", None, None),
            P("dev", None, None),
            P(),
            P(),
            P("dev"),
        ),
        out_specs=(
            P(None, None, "dev", None),
            P(None, None, "dev", None),
            P(None, None, "dev", None),
            P("dev", None, None),
        ),
        check_vma=False,
    )
```

```python
import functools

import jax
import jax.numpy as jnp
from jax import lax
from jax.experimental import pallas as pl
from jax.experimental.pallas import tpu as pltpu
from jax.sharding import PartitionSpec as P

beta_one = 0.9
beta_two = 0.95
corr_one = 0.9999734386011124
corr_two = 0.994079470779666
adam_eps = 1e-08
learn_rate = 0.003
decay_rate = 0.1

CORE, X_STEP, Y_STEP, Z_UNIT = 1, 2, 4, 8
VMEM_LIMIT = 16 * 1024 * 1024


def hop(block, mask):
    count = lax.axis_size("dev")
    return lax.ppermute(block, "dev", [(low, low ^ mask) for low in range(count)])


def adam_update(master, first, second, grad):
    first_new = beta_one * first + (1.0 - beta_one) * grad
    second_new = beta_two * second + (1.0 - beta_two) * grad * grad
    direction = first_new / corr_one / (jnp.sqrt(second_new / corr_two) + adam_eps)
    master_new = master - learn_rate * (direction + decay_rate * master)
    return (master_new, first_new, second_new)


def place_pieces(chip, pieces, weights, sems):
    rows = pieces[0].shape[1]
    copies = []
    for j, piece in enumerate(pieces):
        start = pl.multiple_of(lax.bitwise_xor(chip, j) * rows, rows)
        copies.append(pltpu.make_async_copy(piece, weights.at[:, pl.ds(start, rows), :], sems.at[j]))
    for copy in copies:
        copy.start()
    for copy in copies:
        copy.wait()


def transpose_kernel(chip_ref, own_ref, other_ref, out_ref):
    chip = chip_ref[0]
    tokens, width = own_ref.shape
    count = chip_ref.shape[0] - 1
    rows = width // count
    lanes = max(128, rows)
    for part, ref in enumerate((own_ref, other_ref)):
        for at in range(0, width, lanes):
            turned = ref[:, at : at + lanes].T
            for low in range(0, lanes, rows):
                j = lax.bitwise_xor(chip, (at + low) // rows)
                start = pl.multiple_of(j * rows, rows)
                out_ref[pl.ds(start, rows), part * tokens : (part + 1) * tokens] = turned[low : low + rows]


def backward_kernel(count, chip_ref, *refs):
    pieces = refs[:count]
    own_x, other_x, own_c, other_c, x_turned, c_turned = refs[count : count + 6]
    outs = refs[count + 6 : 2 * count + 6]
    weights, gate_grad, up_grad, hidden_all, sems = refs[2 * count + 6 :]
    place_pieces(chip_ref[0], pieces, weights, sems)
    tokens = own_x.shape[0]
    for part, (x_ref, c_ref) in enumerate(((own_x, own_c), (other_x, other_c))):
        span = slice(part * tokens, (part + 1) * tokens)
        gate_pre = jnp.dot(x_ref[...], weights[0], preferred_element_type=jnp.float32)
        up_pre = jnp.dot(x_ref[...], weights[1], preferred_element_type=jnp.float32)
        grad_hidden = jnp.dot(c_ref[...], weights[2], preferred_element_type=jnp.float32)
        gate_sig = jax.nn.sigmoid(gate_pre)
        gate_act = gate_pre * gate_sig
        hidden_all[span] = (gate_act * up_pre).astype(jnp.bfloat16)
        up_grad[span] = (grad_hidden * gate_act).astype(jnp.bfloat16)
        gate_grad[span] = (grad_hidden * up_pre * gate_sig * (1.0 + gate_pre * (1.0 - gate_sig))).astype(
            jnp.bfloat16
        )
    rows = outs[0].shape[1]
    width = count * rows
    tall = min(width, 256)
    for at in range(0, width, tall):
        for kind, (left, right) in enumerate(
            ((x_turned, gate_grad), (x_turned, up_grad), (c_turned, hidden_all))
        ):
            product = jnp.dot(left[at : at + tall], right[...], preferred_element_type=jnp.float32)
            product = product.astype(jnp.bfloat16)
            for low in range(0, tall, rows):
                outs[(at + low) // rows][kind] = product[low : low + rows]


def forward_kernel(count, chip_ref, *refs):
    pieces = refs[:count]
    own_y, other_y, own_out, other_out, weights, sems = refs[count:]
    place_pieces(chip_ref[0], pieces, weights, sems)
    for y_ref, out_ref in ((other_y, other_out), (own_y, own_out)):
        gate_pre = jnp.dot(y_ref[...], weights[0], preferred_element_type=jnp.float32)
        up_pre = jnp.dot(y_ref[...], weights[1], preferred_element_type=jnp.float32)
        act = (gate_pre * jax.nn.sigmoid(gate_pre) * up_pre).astype(jnp.bfloat16)
        result = lax.dot_general(act, weights[2], (((1,), (1,)), ((), ())), preferred_element_type=jnp.float32)
        out_ref[...] = result.astype(jnp.bfloat16)


VMEM = pl.BlockSpec(memory_space=pltpu.VMEM)
SMEM = pl.BlockSpec(memory_space=pltpu.SMEM)
ANY = pl.BlockSpec(memory_space=pl.ANY)


def params():
    return pltpu.CompilerParams(vmem_limit_bytes=VMEM_LIMIT)


def transposed(chip_ids, own, other):
    tokens, width = own.shape
    return pl.pallas_call(
        transpose_kernel,
        out_shape=jax.ShapeDtypeStruct((width, 2 * tokens), own.dtype),
        in_specs=[SMEM, VMEM, VMEM],
        out_specs=VMEM,
        compiler_params=params(),
        cost_estimate=pl.CostEstimate(flops=0, bytes_accessed=8 * tokens * width, transcendentals=0),
        name="transpose_rows",
    )(chip_ids, own, other)


def backward(chip_ids, pieces, own_x, other_x, own_c, other_c, x_turned, c_turned):
    count = len(pieces)
    kinds, rows, units = pieces[0].shape
    tokens, width = own_x.shape
    return pl.pallas_call(
        functools.partial(backward_kernel, count),
        out_shape=[jax.ShapeDtypeStruct((kinds, rows, units), jnp.bfloat16)] * count,
        in_specs=[SMEM] + [ANY] * count + [VMEM] * 6,
        out_specs=[VMEM] * count,
        scratch_shapes=[
            pltpu.VMEM((kinds, width, units), jnp.bfloat16),
            pltpu.VMEM((2 * tokens, units), jnp.bfloat16),
            pltpu.VMEM((2 * tokens, units), jnp.bfloat16),
            pltpu.VMEM((2 * tokens, units), jnp.bfloat16),
            pltpu.SemaphoreType.DMA((count,)),
        ],
        compiler_params=params(),
        cost_estimate=pl.CostEstimate(
            flops=24 * tokens * width * units,
            bytes_accessed=16 * tokens * width + 12 * width * units,
            transcendentals=2 * tokens * units,
        ),
        name="slot_gradients",
    )(chip_ids, *pieces, own_x, other_x, own_c, other_c, x_turned, c_turned)


def forward(chip_ids, pieces, own_y, other_y):
    count = len(pieces)
    kinds, rows, units = pieces[0].shape
    tokens, width = own_y.shape
    return pl.pallas_call(
        functools.partial(forward_kernel, count),
        out_shape=[jax.ShapeDtypeStruct((tokens, width), jnp.bfloat16)] * 2,
        in_specs=[SMEM] + [ANY] * count + [VMEM] * 2,
        out_specs=[VMEM] * 2,
        scratch_shapes=[
            pltpu.VMEM((kinds, width, units), jnp.bfloat16),
            pltpu.SemaphoreType.DMA((count,)),
        ],
        compiler_params=params(),
        cost_estimate=pl.CostEstimate(
            flops=12 * tokens * width * units,
            bytes_accessed=8 * tokens * width + 6 * width * units,
            transcendentals=2 * tokens * units,
        ),
        name="expert_outputs",
    )(chip_ids, *pieces, own_y, other_y)


def after(value, *others):
    return lax.optimization_barrier((value,) + others)[0]


def gather_chips(piece):
    depth = lax.axis_size("dev") // Z_UNIT
    column = [piece] * depth
    for zj in reversed(range(1, depth)):
        top = 1 << zj.bit_length() - 1
        if zj == top:
            column[zj] = hop(piece, zj * Z_UNIT)
    for zj in range(1, depth):
        top = 1 << zj.bit_length() - 1
        if zj != top:
            column[zj] = hop(column[top], (zj - top) * Z_UNIT)
    pieces = []
    for zj, here in enumerate(column):
        along_x = hop(here, X_STEP)
        along_y = hop(here, Y_STEP)
        across = hop(along_y, X_STEP) if zj % 2 else hop(along_x, Y_STEP)
        pieces += [here, along_x, along_y, across]
    return pieces


def add_all(first, *others):
    total = first.astype(jnp.float32)
    for other in others:
        total = total + other.astype(jnp.float32)
    return total


def reduce_chips(pieces):
    depth = lax.axis_size("dev") // Z_UNIT
    column = [None] * depth
    gate = ((), ())
    for upper in reversed(range(1, depth, 2)):
        here, along_x, along_y, across = pieces[4 * upper : 4 * upper + 4]
        below, below_x, below_y, below_across = pieces[4 * upper - 4 : 4 * upper]
        from_x = hop(after(across, *gate[0]), X_STEP)
        from_y = hop(after(below_across, *gate[0]), Y_STEP)
        along_x = hop(after(along_x, *gate[1]), X_STEP)
        below_y = hop(after(below_y, *gate[1]), Y_STEP)
        along_y = hop(add_all(along_y, from_x).astype(jnp.bfloat16), Y_STEP)
        below_x = hop(add_all(below_x, from_y).astype(jnp.bfloat16), X_STEP)
        column[upper] = [here, along_x, along_y]
        column[upper - 1] = [below, below_x, below_y]
        gate = ((from_x, from_y), (along_x, below_y))
    for zj in reversed(range(1, depth)):
        top = 1 << zj.bit_length() - 1
        low = zj - top
        part = add_all(*column[zj]).astype(jnp.bfloat16)
        if low:
            column[top].append(hop(part, low * Z_UNIT))
        else:
            column[0].append(hop(part, top * Z_UNIT))
    return add_all(*column[0])


def block_a_core(master, first, second, old_rows, old_cotangent, new_rows, old_slots, new_slots, live):
    local_rows = master.shape[2]
    me_index = lax.axis_index("dev")
    core = me_index & CORE
    chips = lax.axis_size("dev") // 2
    own_old = lax.dynamic_index_in_dim(old_slots, me_index, 0, keepdims=False)
    own_new = lax.dynamic_index_in_dim(new_slots, me_index, 0, keepdims=False)
    chip_ids = jnp.full((chips + 1,), lax.shift_right_logical(me_index, 1), jnp.int32)

    state = jnp.stack([master, first, second], axis=1)
    mine = lax.dynamic_index_in_dim(state, core, 0, keepdims=False)
    theirs = hop(lax.dynamic_index_in_dim(state, 1 - core, 0, keepdims=False), CORE)

    positions = jnp.arange(old_rows.shape[0], dtype=jnp.int32)[:, None]
    alive = positions < live
    empty = jnp.zeros_like(old_cotangent)
    other_x = hop(old_rows, CORE)
    other_y = hop(new_rows, CORE)
    own_c = jnp.where(alive & (own_old == core), old_cotangent, empty)
    other_c = hop(jnp.where(alive & (own_old != core), old_cotangent, empty), CORE)

    theirs, other_x, other_y, other_c = lax.optimization_barrier((theirs, other_x, other_y, other_c))
    state = jnp.where(
        core == 0, jnp.concatenate([mine, theirs], axis=-2), jnp.concatenate([theirs, mine], axis=-2)
    )
    pieces = gather_chips(state[0].astype(jnp.bfloat16))

    x_turned = transposed(chip_ids, old_rows, other_x)
    c_turned = transposed(chip_ids, own_c, other_c)
    grads = backward(chip_ids, pieces, old_rows, other_x, own_c, other_c, x_turned, c_turned)
    grad = reduce_chips(grads)
    updated = adam_update(state[0], state[1], state[2], grad)

    new_pieces = gather_chips(updated[0].astype(jnp.bfloat16))
    updated = jnp.stack(updated)
    own_part = lax.dynamic_slice_in_dim(updated, core * local_rows, local_rows, 2)
    other_part = lax.dynamic_slice_in_dim(updated, (1 - core) * local_rows, local_rows, 2)
    from_other = hop(other_part, CORE)
    state = jnp.where(
        core == 0, jnp.stack([own_part, from_other], axis=1), jnp.stack([from_other, own_part], axis=1)
    )
    own_out, other_out = forward(chip_ids, new_pieces, new_rows, other_y)
    new_outputs = jnp.where(own_new == core, own_out, hop(other_out, CORE))
    return (state[0], state[1], state[2], new_outputs[None])


def hidden_terms(tokens, cotangent, weights, live):
    positions = jnp.arange(tokens.shape[0], dtype=jnp.int32)
    cotangent = jnp.where((positions < live)[:, None], cotangent, jnp.zeros_like(cotangent))
    gate_pre = jnp.dot(tokens, weights[0], preferred_element_type=jnp.float32)
    up_pre = jnp.dot(tokens, weights[1], preferred_element_type=jnp.float32)
    gate_sig = jax.nn.sigmoid(gate_pre)
    gate_act = gate_pre * gate_sig
    hidden = (gate_act * up_pre).astype(jnp.bfloat16)
    grad_down = lax.dot_general(
        cotangent, hidden, (((0,), (0,)), ((), ())), preferred_element_type=jnp.float32
    )
    grad_hidden = jnp.dot(cotangent, weights[2], preferred_element_type=jnp.float32)
    grad_up_pre = (grad_hidden * gate_act).astype(jnp.bfloat16)
    grad_gate_pre = (grad_hidden * up_pre * gate_sig * (1.0 + gate_pre * (1.0 - gate_sig))).astype(
        jnp.bfloat16
    )
    grad_gate = lax.dot_general(
        tokens, grad_gate_pre, (((0,), (0,)), ((), ())), preferred_element_type=jnp.float32
    )
    grad_up = lax.dot_general(
        tokens, grad_up_pre, (((0,), (0,)), ((), ())), preferred_element_type=jnp.float32
    )
    return jnp.stack([grad_gate, grad_up, grad_down])


def expert_forward(tokens, weights):
    gate_pre = jnp.dot(tokens, weights[0], preferred_element_type=jnp.float32)
    up_pre = jnp.dot(tokens, weights[1], preferred_element_type=jnp.float32)
    activation = (jax.nn.silu(gate_pre) * up_pre).astype(jnp.bfloat16)
    result = lax.dot_general(
        activation, weights[2], (((1,), (1,)), ((), ())), preferred_element_type=jnp.float32
    )
    return result.astype(jnp.bfloat16)


def halving(buffer, levels, me_index):
    for step in range(levels):
        count = buffer.shape[2]
        halves = buffer.reshape(buffer.shape[:2] + (count // 2, 2) + buffer.shape[3:])
        own_bit = me_index >> step & 1
        keeping = lax.dynamic_index_in_dim(halves, own_bit, 3, keepdims=False)
        sending = lax.dynamic_index_in_dim(halves, 1 - own_bit, 3, keepdims=False)
        buffer = keeping + hop(sending, 1 << step)
    return buffer


def any_shape(master, first, second, old_rows, old_cotangent, new_rows, old_slots, new_slots, live):
    blocks, kinds, local_rows, block_width = master.shape
    devices = lax.axis_size("dev")
    me_index = lax.axis_index("dev")
    own_old = lax.dynamic_index_in_dim(old_slots, me_index, 0, keepdims=False)
    own_new = lax.dynamic_index_in_dim(new_slots, me_index, 0, keepdims=False)
    every_block = lax.all_gather(master.astype(jnp.bfloat16), "dev", axis=2, tiled=True)
    weights = lax.dynamic_index_in_dim(every_block, own_old, 0, keepdims=False)
    slot_grad = hidden_terms(old_rows, old_cotangent, weights, live)
    block_ids = jnp.arange(blocks, dtype=jnp.int32)[:, None, None, None, None]
    dense = slot_grad.reshape(kinds, devices, local_rows, block_width)
    buffer = jnp.where(block_ids == own_old, dense[None], jnp.zeros((), jnp.float32))
    buffer = halving(buffer, devices.bit_length() - 1, me_index)
    grad = buffer.reshape(master.shape)
    new_master, new_first, new_second = adam_update(master, first, second, grad)
    updated_blocks = lax.all_gather(new_master.astype(jnp.bfloat16), "dev", axis=2, tiled=True)
    new_weights = lax.dynamic_index_in_dim(updated_blocks, own_new, 0, keepdims=False)
    return (new_master, new_first, new_second, expert_forward(new_rows, new_weights)[None])


def on_device(
    master,
    first_moment,
    second_moment,
    old_rows,
    old_cotangent,
    new_rows,
    old_slots,
    new_slots,
    live_rows,
):
    blocks, kinds, local_rows, units = master.shape
    devices = lax.axis_size("dev")
    whole_tiles = local_rows % 16 == 0 and units % 128 == 0 and old_rows.shape[1] % 128 == 0
    form = block_a_core if blocks == 2 and devices % (2 * Z_UNIT) == 0 and whole_tiles else any_shape
    return form(
        master,
        first_moment,
        second_moment,
        old_rows[0],
        old_cotangent[0],
        new_rows[0],
        old_slots,
        new_slots,
        live_rows[0],
    )


def solution(mesh):
    return jax.shard_map(
        on_device,
        mesh=mesh,
        in_specs=(
            P(None, None, "dev", None),
            P(None, None, "dev", None),
            P(None, None, "dev", None),
            P("dev", None, None),
            P("dev", None, None),
            P("dev", None, None),
            P(),
            P(),
            P("dev"),
        ),
        out_specs=(
            P(None, None, "dev", None),
            P(None, None, "dev", None),
            P(None, None, "dev", None),
            P("dev", None, None),
        ),
        check_vma=False,
    )
```

```python
import functools

import jax
import jax.numpy as jnp
from jax import lax
from jax.experimental import pallas as pl
from jax.experimental.pallas import tpu as pltpu
from jax.sharding import PartitionSpec as P

beta_one = 0.9
beta_two = 0.95
corr_one = 0.9999734386011124
corr_two = 0.994079470779666
adam_eps = 1e-08
learn_rate = 0.003
decay_rate = 0.1

CORE, X_STEP, Y_STEP, Z_UNIT = 1, 2, 4, 8
VMEM_LIMIT = 16 * 1024 * 1024


def hop(block, mask):
    count = lax.axis_size("dev")
    return lax.ppermute(block, "dev", [(low, low ^ mask) for low in range(count)])


def adam_update(master, first, second, grad):
    first_new = beta_one * first + (1.0 - beta_one) * grad
    second_new = beta_two * second + (1.0 - beta_two) * grad * grad
    direction = first_new / corr_one / (jnp.sqrt(second_new / corr_two) + adam_eps)
    master_new = master - learn_rate * (direction + decay_rate * master)
    return (master_new, first_new, second_new)


def place_pieces(chip, pieces, weights, sems):
    rows = pieces[0].shape[1]
    copies = []
    for j, piece in enumerate(pieces):
        start = pl.multiple_of(lax.bitwise_xor(chip, j) * rows, rows)
        copies.append(pltpu.make_async_copy(piece, weights.at[:, pl.ds(start, rows), :], sems.at[j]))
    for copy in copies:
        copy.start()
    for copy in copies:
        copy.wait()


def transpose_kernel(own_x, other_x, own_c, other_c, x_turned, c_turned):
    chip = lax.axis_index("dev") // 2
    tokens, width = own_x.shape
    rows = 2 * width // lax.axis_size("dev")
    lanes = max(128, rows)
    for out, pair in ((x_turned, (own_x, other_x)), (c_turned, (own_c, other_c))):
        for part, ref in enumerate(pair):
            for at in range(0, width, lanes):
                turned = ref[:, at : at + lanes].T
                for low in range(0, lanes, rows):
                    j = lax.bitwise_xor(chip, (at + low) // rows)
                    start = pl.multiple_of(j * rows, rows)
                    out[pl.ds(start, rows), part * tokens : (part + 1) * tokens] = turned[low : low + rows]


def backward_kernel(count, slots, own_live, other_live, *refs):
    pieces = refs[:count]
    own_x, other_x, own_c, other_c, x_turned, c_turned = refs[count : count + 6]
    outs = refs[count + 6 : 2 * count + 6]
    weights, gate_grad, up_grad, hidden_all, sems = refs[2 * count + 6 :]
    me_index = lax.axis_index("dev")
    core = me_index & CORE
    place_pieces(me_index // 2, pieces, weights, sems)
    tokens = own_x.shape[0]
    sides = ((own_x, own_c, me_index, own_live), (other_x, other_c, me_index ^ CORE, other_live))
    for part, (x_ref, c_ref, slot, live) in enumerate(sides):
        span = slice(part * tokens, (part + 1) * tokens)
        gate_pre = jnp.dot(x_ref[...], weights[0], preferred_element_type=jnp.float32)
        up_pre = jnp.dot(x_ref[...], weights[1], preferred_element_type=jnp.float32)
        grad_hidden = jnp.dot(c_ref[...], weights[2], preferred_element_type=jnp.float32)
        gate_sig = jax.nn.sigmoid(gate_pre)
        gate_act = gate_pre * gate_sig
        alive = jnp.where(slots[slot] == core, live[0], 0)
        keep = lax.broadcasted_iota(jnp.int32, gate_pre.shape, 0) < alive
        grad_up = grad_hidden * gate_act
        grad_gate = grad_hidden * up_pre * gate_sig * (1.0 + gate_pre * (1.0 - gate_sig))
        hidden_all[span] = jnp.where(keep, gate_act * up_pre, 0.0).astype(jnp.bfloat16)
        up_grad[span] = jnp.where(keep, grad_up, 0.0).astype(jnp.bfloat16)
        gate_grad[span] = jnp.where(keep, grad_gate, 0.0).astype(jnp.bfloat16)
    rows = outs[0].shape[1]
    width = count * rows
    tall = min(width, 256)
    for at in range(0, width, tall):
        for kind, (left, right) in enumerate(
            ((x_turned, gate_grad), (x_turned, up_grad), (c_turned, hidden_all))
        ):
            product = jnp.dot(left[at : at + tall], right[...], preferred_element_type=jnp.float32)
            product = product.astype(jnp.bfloat16)
            for low in range(0, tall, rows):
                outs[(at + low) // rows][kind] = product[low : low + rows]


def forward_kernel(count, *refs):
    pieces = refs[:count]
    own_y, other_y, own_out, other_out, weights, sems = refs[count:]
    place_pieces(lax.axis_index("dev") // 2, pieces, weights, sems)
    for y_ref, out_ref in ((other_y, other_out), (own_y, own_out)):
        gate_pre = jnp.dot(y_ref[...], weights[0], preferred_element_type=jnp.float32)
        up_pre = jnp.dot(y_ref[...], weights[1], preferred_element_type=jnp.float32)
        act = (gate_pre * jax.nn.sigmoid(gate_pre) * up_pre).astype(jnp.bfloat16)
        result = lax.dot_general(act, weights[2], (((1,), (1,)), ((), ())), preferred_element_type=jnp.float32)
        out_ref[...] = result.astype(jnp.bfloat16)


VMEM = pl.BlockSpec(memory_space=pltpu.VMEM)
SMEM = pl.BlockSpec(memory_space=pltpu.SMEM)
ANY = pl.BlockSpec(memory_space=pl.ANY)


def params():
    return pltpu.CompilerParams(vmem_limit_bytes=VMEM_LIMIT)


def transposed(own_x, other_x, own_c, other_c):
    tokens, width = own_x.shape
    return pl.pallas_call(
        transpose_kernel,
        out_shape=[jax.ShapeDtypeStruct((width, 2 * tokens), own_x.dtype)] * 2,
        in_specs=[VMEM] * 4,
        out_specs=[VMEM] * 2,
        compiler_params=params(),
        cost_estimate=pl.CostEstimate(flops=0, bytes_accessed=16 * tokens * width, transcendentals=0),
        name="transpose_rows",
    )(own_x, other_x, own_c, other_c)


def backward(slots, own_live, other_live, pieces, own_x, other_x, own_c, other_c, x_turned, c_turned):
    count = len(pieces)
    kinds, rows, units = pieces[0].shape
    tokens, width = own_x.shape
    return pl.pallas_call(
        functools.partial(backward_kernel, count),
        out_shape=[jax.ShapeDtypeStruct((kinds, rows, units), jnp.bfloat16)] * count,
        in_specs=[SMEM] * 3 + [ANY] * count + [VMEM] * 6,
        out_specs=[VMEM] * count,
        scratch_shapes=[
            pltpu.VMEM((kinds, width, units), jnp.bfloat16),
            pltpu.VMEM((2 * tokens, units), jnp.bfloat16),
            pltpu.VMEM((2 * tokens, units), jnp.bfloat16),
            pltpu.VMEM((2 * tokens, units), jnp.bfloat16),
            pltpu.SemaphoreType.DMA((count,)),
        ],
        compiler_params=params(),
        cost_estimate=pl.CostEstimate(
            flops=24 * tokens * width * units,
            bytes_accessed=16 * tokens * width + 12 * width * units,
            transcendentals=2 * tokens * units,
        ),
        name="slot_gradients",
    )(slots, own_live, other_live, *pieces, own_x, other_x, own_c, other_c, x_turned, c_turned)


def forward(pieces, own_y, other_y):
    count = len(pieces)
    kinds, rows, units = pieces[0].shape
    tokens, width = own_y.shape
    return pl.pallas_call(
        functools.partial(forward_kernel, count),
        out_shape=[jax.ShapeDtypeStruct((tokens, width), jnp.bfloat16)] * 2,
        in_specs=[ANY] * count + [VMEM] * 2,
        out_specs=[VMEM] * 2,
        scratch_shapes=[
            pltpu.VMEM((kinds, width, units), jnp.bfloat16),
            pltpu.SemaphoreType.DMA((count,)),
        ],
        compiler_params=params(),
        cost_estimate=pl.CostEstimate(
            flops=12 * tokens * width * units,
            bytes_accessed=8 * tokens * width + 6 * width * units,
            transcendentals=2 * tokens * units,
        ),
        name="expert_outputs",
    )(*pieces, own_y, other_y)


def after(value, *others):
    return lax.optimization_barrier((value,) + others)[0]


def gather_chips(piece):
    depth = lax.axis_size("dev") // Z_UNIT
    column = [piece] + [None] * (depth - 1)
    for top in reversed([1 << bit for bit in range(depth.bit_length() - 1)]):
        column[top] = hop(piece, top * Z_UNIT)
    along_x, along_y, across = [None] * depth, [None] * depth, [None] * depth
    along_x[0] = hop(piece, X_STEP)
    along_y[0] = hop(piece, Y_STEP)
    along_x[1] = hop(column[1], X_STEP)
    for zj in range(2, depth):
        top = 1 << zj.bit_length() - 1
        if zj != top:
            column[zj] = hop(column[top], (zj - top) * Z_UNIT)
    along_y[1] = hop(after(column[1], along_x[0]), Y_STEP)
    for zj in range(2, depth, 2):
        along_x[zj] = hop(after(column[zj], along_x[zj - 2], along_y[zj - 2]), X_STEP)
        across[zj - 2] = hop(after(along_x[zj - 2], along_y[zj - 2]), Y_STEP)
        along_x[zj + 1] = hop(after(column[zj + 1], along_x[zj - 1]), X_STEP)
        along_y[zj + 1] = hop(after(column[zj + 1], along_x[zj - 1]), Y_STEP)
        along_y[zj] = hop(after(column[zj], along_y[zj - 1]), Y_STEP)
        across[zj - 1] = hop(after(along_y[zj - 1], along_x[zj]), X_STEP)
    across[-2] = hop(after(along_x[-2], along_x[-1]), Y_STEP)
    across[-1] = hop(along_y[-1], X_STEP)
    return [part for group in zip(column, along_x, along_y, across) for part in group]


def add_all(first, *others):
    total = first.astype(jnp.float32)
    for other in others:
        total = total + other.astype(jnp.float32)
    return total


def reduce_chips(pieces):
    depth = lax.axis_size("dev") // Z_UNIT
    column = [[pieces[4 * zj]] for zj in range(depth)]
    crossed, full, risen = (), (), ()
    for upper in reversed(range(1, depth, 2)):
        along_x, along_y, across = pieces[4 * upper + 1 : 4 * upper + 4]
        below_x, below_y, below_across = pieces[4 * upper - 3 : 4 * upper]
        from_x = hop(after(across, *crossed), X_STEP)
        from_y = hop(after(below_across, *full), Y_STEP)
        along_x = hop(after(along_x, *full), X_STEP)
        along_y = hop(add_all(along_y, from_x).astype(jnp.bfloat16), Y_STEP)
        column[upper] += [along_x, along_y]
        below_x = hop(after(add_all(below_x, from_y).astype(jnp.bfloat16), *risen), X_STEP)
        below_y = hop(after(below_y, from_x, *risen), Y_STEP)
        column[upper - 1] += [below_x, below_y]
        crossed, full = (from_y,), (along_x, along_y)
        for zj in (upper, upper - 1):
            top = 1 << zj.bit_length() - 1 if zj else 0
            low = zj - top
            if zj:
                part = add_all(*column[zj]).astype(jnp.bfloat16)
                risen += (hop(part, low * Z_UNIT if low else top * Z_UNIT),)
                column[top if low else 0].append(risen[-1])
        risen = risen[:1] + (below_x, below_y)
    return add_all(*column[0])


def block_a_core(master, first, second, old_rows, old_cotangent, new_rows, old_slots, new_slots, live):
    local_rows = master.shape[2]
    me_index = lax.axis_index("dev")
    core = me_index & CORE
    own_new = lax.dynamic_index_in_dim(new_slots, me_index, 0, keepdims=False)

    other_x = hop(old_rows, CORE)
    other_c = hop(old_cotangent, CORE)
    state = jnp.stack([master, first, second], axis=1)
    mine = lax.dynamic_index_in_dim(state, core, 0, keepdims=False)
    theirs = hop(lax.dynamic_index_in_dim(state, 1 - core, 0, keepdims=False), CORE)
    other_y = hop(new_rows, CORE)
    other_live = hop(live, CORE)
    x_turned, c_turned = transposed(old_rows, other_x, old_cotangent, other_c)

    theirs, other_y, other_live, x_turned, c_turned, is_own = lax.optimization_barrier(
        (theirs, other_y, other_live, x_turned, c_turned, own_new == core)
    )
    state = jnp.where(
        core == 0, jnp.concatenate([mine, theirs], axis=-2), jnp.concatenate([theirs, mine], axis=-2)
    )
    pieces = gather_chips(state[0].astype(jnp.bfloat16))
    grads = backward(
        old_slots,
        live,
        other_live,
        pieces,
        old_rows,
        other_x,
        old_cotangent,
        other_c,
        x_turned,
        c_turned,
    )
    grad = reduce_chips(grads)
    updated = adam_update(state[0], state[1], state[2], grad)

    new_pieces = gather_chips(updated[0].astype(jnp.bfloat16))
    updated = jnp.stack(updated)
    own_part = lax.dynamic_slice_in_dim(updated, core * local_rows, local_rows, 2)
    other_part = lax.dynamic_slice_in_dim(updated, (1 - core) * local_rows, local_rows, 2)
    from_other = hop(other_part, CORE)
    state = jnp.where(
        core == 0, jnp.stack([own_part, from_other], axis=1), jnp.stack([from_other, own_part], axis=1)
    )
    own_out, other_out = forward(new_pieces, new_rows, other_y)
    new_outputs = jnp.where(is_own, own_out, hop(other_out, CORE))
    return (state[0], state[1], state[2], new_outputs[None])


def hidden_terms(tokens, cotangent, weights, live):
    positions = jnp.arange(tokens.shape[0], dtype=jnp.int32)
    cotangent = jnp.where((positions < live)[:, None], cotangent, jnp.zeros_like(cotangent))
    gate_pre = jnp.dot(tokens, weights[0], preferred_element_type=jnp.float32)
    up_pre = jnp.dot(tokens, weights[1], preferred_element_type=jnp.float32)
    gate_sig = jax.nn.sigmoid(gate_pre)
    gate_act = gate_pre * gate_sig
    hidden = (gate_act * up_pre).astype(jnp.bfloat16)
    grad_down = lax.dot_general(
        cotangent, hidden, (((0,), (0,)), ((), ())), preferred_element_type=jnp.float32
    )
    grad_hidden = jnp.dot(cotangent, weights[2], preferred_element_type=jnp.float32)
    grad_up_pre = (grad_hidden * gate_act).astype(jnp.bfloat16)
    grad_gate_pre = (grad_hidden * up_pre * gate_sig * (1.0 + gate_pre * (1.0 - gate_sig))).astype(
        jnp.bfloat16
    )
    grad_gate = lax.dot_general(
        tokens, grad_gate_pre, (((0,), (0,)), ((), ())), preferred_element_type=jnp.float32
    )
    grad_up = lax.dot_general(
        tokens, grad_up_pre, (((0,), (0,)), ((), ())), preferred_element_type=jnp.float32
    )
    return jnp.stack([grad_gate, grad_up, grad_down])


def expert_forward(tokens, weights):
    gate_pre = jnp.dot(tokens, weights[0], preferred_element_type=jnp.float32)
    up_pre = jnp.dot(tokens, weights[1], preferred_element_type=jnp.float32)
    activation = (jax.nn.silu(gate_pre) * up_pre).astype(jnp.bfloat16)
    result = lax.dot_general(
        activation, weights[2], (((1,), (1,)), ((), ())), preferred_element_type=jnp.float32
    )
    return result.astype(jnp.bfloat16)


def halving(buffer, levels, me_index):
    for step in range(levels):
        count = buffer.shape[2]
        halves = buffer.reshape(buffer.shape[:2] + (count // 2, 2) + buffer.shape[3:])
        own_bit = me_index >> step & 1
        keeping = lax.dynamic_index_in_dim(halves, own_bit, 3, keepdims=False)
        sending = lax.dynamic_index_in_dim(halves, 1 - own_bit, 3, keepdims=False)
        buffer = keeping + hop(sending, 1 << step)
    return buffer


def any_shape(master, first, second, old_rows, old_cotangent, new_rows, old_slots, new_slots, live):
    blocks, kinds, local_rows, block_width = master.shape
    devices = lax.axis_size("dev")
    me_index = lax.axis_index("dev")
    own_old = lax.dynamic_index_in_dim(old_slots, me_index, 0, keepdims=False)
    own_new = lax.dynamic_index_in_dim(new_slots, me_index, 0, keepdims=False)
    every_block = lax.all_gather(master.astype(jnp.bfloat16), "dev", axis=2, tiled=True)
    weights = lax.dynamic_index_in_dim(every_block, own_old, 0, keepdims=False)
    slot_grad = hidden_terms(old_rows, old_cotangent, weights, live[0])
    block_ids = jnp.arange(blocks, dtype=jnp.int32)[:, None, None, None, None]
    dense = slot_grad.reshape(kinds, devices, local_rows, block_width)
    buffer = jnp.where(block_ids == own_old, dense[None], jnp.zeros((), jnp.float32))
    buffer = halving(buffer, devices.bit_length() - 1, me_index)
    grad = buffer.reshape(master.shape)
    new_master, new_first, new_second = adam_update(master, first, second, grad)
    updated_blocks = lax.all_gather(new_master.astype(jnp.bfloat16), "dev", axis=2, tiled=True)
    new_weights = lax.dynamic_index_in_dim(updated_blocks, own_new, 0, keepdims=False)
    return (new_master, new_first, new_second, expert_forward(new_rows, new_weights)[None])


def on_device(
    master,
    first_moment,
    second_moment,
    old_rows,
    old_cotangent,
    new_rows,
    old_slots,
    new_slots,
    live_rows,
):
    blocks, kinds, local_rows, units = master.shape
    devices = lax.axis_size("dev")
    whole_tiles = local_rows % 16 == 0 and units % 128 == 0 and old_rows.shape[1] % 128 == 0
    form = block_a_core if blocks == 2 and devices % (2 * Z_UNIT) == 0 and whole_tiles else any_shape
    return form(
        master,
        first_moment,
        second_moment,
        old_rows[0],
        old_cotangent[0],
        new_rows[0],
        old_slots,
        new_slots,
        live_rows,
    )


def solution(mesh):
    return jax.shard_map(
        on_device,
        mesh=mesh,
        in_specs=(
            P(None, None, "dev", None),
            P(None, None, "dev", None),
            P(None, None, "dev", None),
            P("dev", None, None),
            P("dev", None, None),
            P("dev", None, None),
            P(),
            P(),
            P("dev"),
        ),
        out_specs=(
            P(None, None, "dev", None),
            P(None, None, "dev", None),
            P(None, None, "dev", None),
            P("dev", None, None),
        ),
        check_vma=False,
    )
```

```python
import functools

import jax
import jax.numpy as jnp
from jax import lax
from jax.experimental import pallas as pl
from jax.experimental.pallas import tpu as pltpu
from jax.sharding import PartitionSpec as P

beta_one = 0.9
beta_two = 0.95
corr_one = 0.9999734386011124
corr_two = 0.994079470779666
adam_eps = 1e-08
learn_rate = 0.003
decay_rate = 0.1

CORE, X_STEP, Y_STEP, Z_UNIT = 1, 2, 4, 8
VMEM_LIMIT = 16 * 1024 * 1024


def hop(block, mask):
    count = lax.axis_size("dev")
    return lax.ppermute(block, "dev", [(low, low ^ mask) for low in range(count)])


def adam_update(master, first, second, grad):
    first_new = beta_one * first + (1.0 - beta_one) * grad
    second_new = beta_two * second + (1.0 - beta_two) * grad * grad
    direction = first_new / corr_one / (jnp.sqrt(second_new / corr_two) + adam_eps)
    master_new = master - learn_rate * (direction + decay_rate * master)
    return (master_new, first_new, second_new)


def place_pieces(chip, pieces, weights, sems):
    rows = pieces[0].shape[1]
    copies = []
    for j, piece in enumerate(pieces):
        start = pl.multiple_of(lax.bitwise_xor(chip, j) * rows, rows)
        copies.append(pltpu.make_async_copy(piece, weights.at[:, pl.ds(start, rows), :], sems.at[j]))
    for copy in copies:
        copy.start()
    for copy in copies:
        copy.wait()


def transpose_kernel(own_x, other_x, own_c, other_c, x_turned, c_turned):
    chip = lax.axis_index("dev") // 2
    tokens, width = own_x.shape
    rows = 2 * width // lax.axis_size("dev")
    lanes = max(128, rows)
    for out, pair in ((x_turned, (own_x, other_x)), (c_turned, (own_c, other_c))):
        for part, ref in enumerate(pair):
            for at in range(0, width, lanes):
                turned = ref[:, at : at + lanes].T
                for low in range(0, lanes, rows):
                    j = lax.bitwise_xor(chip, (at + low) // rows)
                    start = pl.multiple_of(j * rows, rows)
                    out[pl.ds(start, rows), part * tokens : (part + 1) * tokens] = turned[low : low + rows]


def places(outs):
    found = []
    for zj in range(len(outs) // 3):
        own, later, pair = outs[3 * zj : 3 * zj + 3]
        by_x, by_y = ((pair, (1,)), (later, ())) if zj % 2 else ((later, ()), (pair, (1,)))
        found += [(own, ()), by_x, by_y, (pair, (0,))]
    return found


def backward_kernel(count, slots, own_live, other_live, *refs):
    pieces = refs[:count]
    own_x, other_x, own_c, other_c, x_turned, c_turned = refs[count : count + 6]
    weights, gate_grad, up_grad, hidden_all, sems = refs[-5:]
    outs = places(refs[count + 6 : -5])
    me_index = lax.axis_index("dev")
    core = me_index & CORE
    place_pieces(me_index // 2, pieces, weights, sems)
    tokens = own_x.shape[0]
    sides = ((own_x, own_c, me_index, own_live), (other_x, other_c, me_index ^ CORE, other_live))
    for part, (x_ref, c_ref, slot, live) in enumerate(sides):
        span = slice(part * tokens, (part + 1) * tokens)
        gate_pre = jnp.dot(x_ref[...], weights[0], preferred_element_type=jnp.float32)
        up_pre = jnp.dot(x_ref[...], weights[1], preferred_element_type=jnp.float32)
        grad_hidden = jnp.dot(c_ref[...], weights[2], preferred_element_type=jnp.float32)
        gate_sig = jax.nn.sigmoid(gate_pre)
        gate_act = gate_pre * gate_sig
        alive = jnp.where(slots[slot] == core, live[0], 0)
        keep = lax.broadcasted_iota(jnp.int32, gate_pre.shape, 0) < alive
        grad_up = grad_hidden * gate_act
        grad_gate = grad_hidden * up_pre * gate_sig * (1.0 + gate_pre * (1.0 - gate_sig))
        hidden_all[span] = jnp.where(keep, gate_act * up_pre, 0.0).astype(jnp.bfloat16)
        up_grad[span] = jnp.where(keep, grad_up, 0.0).astype(jnp.bfloat16)
        gate_grad[span] = jnp.where(keep, grad_gate, 0.0).astype(jnp.bfloat16)
    rows = pieces[0].shape[1]
    width = count * rows
    tall = min(width, 256)
    for at in range(0, width, tall):
        for kind, (left, right) in enumerate(
            ((x_turned, gate_grad), (x_turned, up_grad), (c_turned, hidden_all))
        ):
            product = jnp.dot(left[at : at + tall], right[...], preferred_element_type=jnp.float32)
            product = product.astype(jnp.bfloat16)
            for low in range(0, tall, rows):
                out, before = outs[(at + low) // rows]
                out[before + (kind,)] = product[low : low + rows]


def forward_kernel(count, slots, *refs):
    pieces = refs[:count]
    y_ref, out_ref, matches, weights, sems = refs[count:]
    me_index = lax.axis_index("dev")
    place_pieces(me_index // 2, pieces, weights, sems)
    matches[0] = jnp.where(slots[me_index] == (me_index & CORE), 1, 0)
    gate_pre = jnp.dot(y_ref[...], weights[0], preferred_element_type=jnp.float32)
    up_pre = jnp.dot(y_ref[...], weights[1], preferred_element_type=jnp.float32)
    act = (gate_pre * jax.nn.sigmoid(gate_pre) * up_pre).astype(jnp.bfloat16)
    result = lax.dot_general(act, weights[2], (((1,), (1,)), ((), ())), preferred_element_type=jnp.float32)
    out_ref[...] = result.astype(jnp.bfloat16)


def choose_kernel(matches, own_out, other_out, out, sem):
    for wanted, source in ((1, own_out), (0, other_out)):

        @pl.when(matches[0] == wanted)
        def move():
            copy = pltpu.make_async_copy(source, out, sem)
            copy.start()
            copy.wait()


VMEM = pl.BlockSpec(memory_space=pltpu.VMEM)
SMEM = pl.BlockSpec(memory_space=pltpu.SMEM)
ANY = pl.BlockSpec(memory_space=pl.ANY)


def params():
    return pltpu.CompilerParams(vmem_limit_bytes=VMEM_LIMIT)


def transposed(own_x, other_x, own_c, other_c):
    tokens, width = own_x.shape
    return pl.pallas_call(
        transpose_kernel,
        out_shape=[jax.ShapeDtypeStruct((width, 2 * tokens), own_x.dtype)] * 2,
        in_specs=[VMEM] * 4,
        out_specs=[VMEM] * 2,
        compiler_params=params(),
        cost_estimate=pl.CostEstimate(flops=0, bytes_accessed=16 * tokens * width, transcendentals=0),
        name="transpose_rows",
    )(own_x, other_x, own_c, other_c)


def backward(slots, own_live, other_live, pieces, own_x, other_x, own_c, other_c, x_turned, c_turned):
    count = len(pieces)
    kinds, rows, units = pieces[0].shape
    tokens, width = own_x.shape
    one = jax.ShapeDtypeStruct((kinds, rows, units), jnp.bfloat16)
    two = jax.ShapeDtypeStruct((2, kinds, rows, units), jnp.bfloat16)
    return pl.pallas_call(
        functools.partial(backward_kernel, count),
        out_shape=[one, one, two] * (count // 4),
        in_specs=[SMEM] * 3 + [ANY] * count + [VMEM] * 6,
        out_specs=[VMEM] * (3 * count // 4),
        scratch_shapes=[
            pltpu.VMEM((kinds, width, units), jnp.bfloat16),
            pltpu.VMEM((2 * tokens, units), jnp.bfloat16),
            pltpu.VMEM((2 * tokens, units), jnp.bfloat16),
            pltpu.VMEM((2 * tokens, units), jnp.bfloat16),
            pltpu.SemaphoreType.DMA((count,)),
        ],
        compiler_params=params(),
        cost_estimate=pl.CostEstimate(
            flops=24 * tokens * width * units,
            bytes_accessed=16 * tokens * width + 12 * width * units,
            transcendentals=2 * tokens * units,
        ),
        name="slot_gradients",
    )(slots, own_live, other_live, *pieces, own_x, other_x, own_c, other_c, x_turned, c_turned)


def forward(slots, pieces, rows_in):
    count = len(pieces)
    kinds, rows, units = pieces[0].shape
    tokens, width = rows_in.shape
    return pl.pallas_call(
        functools.partial(forward_kernel, count),
        out_shape=[
            jax.ShapeDtypeStruct((tokens, width), jnp.bfloat16),
            jax.ShapeDtypeStruct((1,), jnp.int32),
        ],
        in_specs=[SMEM] + [ANY] * count + [VMEM],
        out_specs=[VMEM, SMEM],
        scratch_shapes=[
            pltpu.VMEM((kinds, width, units), jnp.bfloat16),
            pltpu.SemaphoreType.DMA((count,)),
        ],
        compiler_params=params(),
        cost_estimate=pl.CostEstimate(
            flops=6 * tokens * width * units,
            bytes_accessed=4 * tokens * width + 6 * width * units,
            transcendentals=tokens * units,
        ),
        name="expert_outputs",
    )(slots, *pieces, rows_in)


def choose(matches, own_out, other_out):
    return pl.pallas_call(
        choose_kernel,
        out_shape=jax.ShapeDtypeStruct(own_out.shape, own_out.dtype),
        in_specs=[SMEM, ANY, ANY],
        out_specs=ANY,
        scratch_shapes=[pltpu.SemaphoreType.DMA],
        compiler_params=params(),
        name="choose_outputs",
    )(matches, own_out, other_out)


def after(value, *others):
    return lax.optimization_barrier((value,) + others)[0]


def gather_chips(piece):
    depth = lax.axis_size("dev") // Z_UNIT
    column = [piece] + [None] * (depth - 1)
    for top in reversed([1 << bit for bit in range(depth.bit_length() - 1)]):
        column[top] = hop(piece, top * Z_UNIT)
    along_x, along_y, across = [None] * depth, [None] * depth, [None] * depth
    along_x[0] = hop(piece, X_STEP)
    along_y[0] = hop(piece, Y_STEP)
    along_x[1] = hop(column[1], X_STEP)
    for zj in range(2, depth):
        top = 1 << zj.bit_length() - 1
        if zj != top:
            column[zj] = hop(column[top], (zj - top) * Z_UNIT)
    along_y[1] = hop(after(column[1], along_x[0]), Y_STEP)
    for zj in range(2, depth, 2):
        along_x[zj] = hop(after(column[zj], along_x[zj - 2], along_y[zj - 2]), X_STEP)
        across[zj - 2] = hop(after(along_x[zj - 2], along_y[zj - 2]), Y_STEP)
        along_x[zj + 1] = hop(after(column[zj + 1], along_x[zj - 1]), X_STEP)
        along_y[zj + 1] = hop(after(column[zj + 1], along_x[zj - 1]), Y_STEP)
        along_y[zj] = hop(after(column[zj], along_y[zj - 1]), Y_STEP)
        across[zj - 1] = hop(after(along_y[zj - 1], along_x[zj]), X_STEP)
    across[-2] = hop(after(along_x[-2], along_x[-1]), Y_STEP)
    across[-1] = hop(along_y[-1], X_STEP)
    return [part for group in zip(column, along_x, along_y, across) for part in group]


def add_all(first, *others):
    total = first.astype(jnp.float32)
    for other in others:
        total = total + other.astype(jnp.float32)
    return total


def reduce_chips(pieces):
    depth = lax.axis_size("dev") // Z_UNIT
    column = [[pieces[3 * zj]] for zj in range(depth)]
    crossed, turned = (), ()
    for upper in reversed(range(1, depth, 2)):
        up_y, pair_x = pieces[3 * upper + 1 : 3 * upper + 3]
        below_x, pair_y = pieces[3 * upper - 2 : 3 * upper]
        got_x = hop(after(pair_x, *crossed), X_STEP)
        got_y = hop(after(pair_y, *turned), Y_STEP)
        column[upper] += [got_x[1], hop(add_all(up_y, got_x[0]).astype(jnp.bfloat16), Y_STEP)]
        column[upper - 1] += [got_y[1], hop(add_all(below_x, got_y[0]).astype(jnp.bfloat16), X_STEP)]
        crossed, turned = (got_x,), (got_y,)
        for zj in (upper, upper - 1):
            top = 1 << zj.bit_length() - 1 if zj else 0
            low = zj - top
            if zj:
                part = add_all(*column[zj]).astype(jnp.bfloat16)
                column[top if low else 0].append(hop(part, (low or top) * Z_UNIT))
    return add_all(*column[0])


def block_a_core(master, first, second, old_rows, old_cotangent, new_rows, old_slots, new_slots, live):
    local_rows = master.shape[2]
    core = lax.axis_index("dev") & CORE

    def mine(state):
        return lax.dynamic_index_in_dim(state, core, 0, keepdims=False)

    def partners(state):
        return lax.dynamic_index_in_dim(state, 1 - core, 0, keepdims=False)

    def both_rows(own, other):
        return jnp.where(
            core == 0, jnp.concatenate([own, other], axis=-2), jnp.concatenate([other, own], axis=-2)
        )

    other_x = hop(old_rows, CORE)
    other_c = hop(old_cotangent, CORE)
    theirs = hop(jnp.stack([partners(master), partners(first), partners(second)]), CORE)
    other_y = hop(new_rows, CORE)
    other_live = hop(live, CORE)
    x_turned, c_turned = transposed(old_rows, other_x, old_cotangent, other_c)
    theirs, other_y, other_live, x_turned, c_turned = lax.optimization_barrier(
        (theirs, other_y, other_live, x_turned, c_turned)
    )
    master_two = both_rows(mine(master), theirs[0])
    pieces = gather_chips(master_two.astype(jnp.bfloat16))
    grads = backward(
        old_slots,
        live,
        other_live,
        pieces,
        old_rows,
        other_x,
        old_cotangent,
        other_c,
        x_turned,
        c_turned,
    )
    theirs = after(theirs, grads[0])
    first_two = both_rows(mine(first), theirs[1])
    second_two = both_rows(mine(second), theirs[2])
    grad = reduce_chips(grads)
    updated = adam_update(master_two, first_two, second_two, grad)

    new_pieces = gather_chips(updated[0].astype(jnp.bfloat16))
    updated = jnp.stack(updated)
    own_part = lax.dynamic_slice_in_dim(updated, core * local_rows, local_rows, 2)
    other_part = lax.dynamic_slice_in_dim(updated, (1 - core) * local_rows, local_rows, 2)
    from_other = hop(after(other_part, new_pieces[-3]), CORE)
    state = jnp.where(
        core == 0, jnp.stack([own_part, from_other], axis=1), jnp.stack([from_other, own_part], axis=1)
    )
    state = (state[0], state[1], state[2])
    other_y, *state = lax.optimization_barrier((other_y,) + state)
    other_out, matches = forward(new_slots, new_pieces, other_y)
    own_out, matches = forward(new_slots, new_pieces, after(new_rows, other_out))
    new_outputs = choose(matches, own_out, hop(other_out, CORE))
    return (*state, new_outputs[None])


def hidden_terms(tokens, cotangent, weights, live):
    positions = jnp.arange(tokens.shape[0], dtype=jnp.int32)
    cotangent = jnp.where((positions < live)[:, None], cotangent, jnp.zeros_like(cotangent))
    gate_pre = jnp.dot(tokens, weights[0], preferred_element_type=jnp.float32)
    up_pre = jnp.dot(tokens, weights[1], preferred_element_type=jnp.float32)
    gate_sig = jax.nn.sigmoid(gate_pre)
    gate_act = gate_pre * gate_sig
    hidden = (gate_act * up_pre).astype(jnp.bfloat16)
    grad_down = lax.dot_general(
        cotangent, hidden, (((0,), (0,)), ((), ())), preferred_element_type=jnp.float32
    )
    grad_hidden = jnp.dot(cotangent, weights[2], preferred_element_type=jnp.float32)
    grad_up_pre = (grad_hidden * gate_act).astype(jnp.bfloat16)
    grad_gate_pre = (grad_hidden * up_pre * gate_sig * (1.0 + gate_pre * (1.0 - gate_sig))).astype(
        jnp.bfloat16
    )
    grad_gate = lax.dot_general(
        tokens, grad_gate_pre, (((0,), (0,)), ((), ())), preferred_element_type=jnp.float32
    )
    grad_up = lax.dot_general(
        tokens, grad_up_pre, (((0,), (0,)), ((), ())), preferred_element_type=jnp.float32
    )
    return jnp.stack([grad_gate, grad_up, grad_down])


def expert_forward(tokens, weights):
    gate_pre = jnp.dot(tokens, weights[0], preferred_element_type=jnp.float32)
    up_pre = jnp.dot(tokens, weights[1], preferred_element_type=jnp.float32)
    activation = (jax.nn.silu(gate_pre) * up_pre).astype(jnp.bfloat16)
    result = lax.dot_general(
        activation, weights[2], (((1,), (1,)), ((), ())), preferred_element_type=jnp.float32
    )
    return result.astype(jnp.bfloat16)


def halving(buffer, levels, me_index):
    for step in range(levels):
        count = buffer.shape[2]
        halves = buffer.reshape(buffer.shape[:2] + (count // 2, 2) + buffer.shape[3:])
        own_bit = me_index >> step & 1
        keeping = lax.dynamic_index_in_dim(halves, own_bit, 3, keepdims=False)
        sending = lax.dynamic_index_in_dim(halves, 1 - own_bit, 3, keepdims=False)
        buffer = keeping + hop(sending, 1 << step)
    return buffer


def any_shape(master, first, second, old_rows, old_cotangent, new_rows, old_slots, new_slots, live):
    blocks, kinds, local_rows, block_width = master.shape
    devices = lax.axis_size("dev")
    me_index = lax.axis_index("dev")
    own_old = lax.dynamic_index_in_dim(old_slots, me_index, 0, keepdims=False)
    own_new = lax.dynamic_index_in_dim(new_slots, me_index, 0, keepdims=False)
    every_block = lax.all_gather(master.astype(jnp.bfloat16), "dev", axis=2, tiled=True)
    weights = lax.dynamic_index_in_dim(every_block, own_old, 0, keepdims=False)
    slot_grad = hidden_terms(old_rows, old_cotangent, weights, live[0])
    block_ids = jnp.arange(blocks, dtype=jnp.int32)[:, None, None, None, None]
    dense = slot_grad.reshape(kinds, devices, local_rows, block_width)
    buffer = jnp.where(block_ids == own_old, dense[None], jnp.zeros((), jnp.float32))
    buffer = halving(buffer, devices.bit_length() - 1, me_index)
    grad = buffer.reshape(master.shape)
    new_master, new_first, new_second = adam_update(master, first, second, grad)
    updated_blocks = lax.all_gather(new_master.astype(jnp.bfloat16), "dev", axis=2, tiled=True)
    new_weights = lax.dynamic_index_in_dim(updated_blocks, own_new, 0, keepdims=False)
    return (new_master, new_first, new_second, expert_forward(new_rows, new_weights)[None])


def on_device(
    master,
    first_moment,
    second_moment,
    old_rows,
    old_cotangent,
    new_rows,
    old_slots,
    new_slots,
    live_rows,
):
    blocks, kinds, local_rows, units = master.shape
    devices = lax.axis_size("dev")
    whole_tiles = local_rows % 16 == 0 and units % 128 == 0 and old_rows.shape[1] % 128 == 0
    form = block_a_core if blocks == 2 and devices % (2 * Z_UNIT) == 0 and whole_tiles else any_shape
    return form(
        master,
        first_moment,
        second_moment,
        old_rows[0],
        old_cotangent[0],
        new_rows[0],
        old_slots,
        new_slots,
        live_rows,
    )


def solution(mesh):
    return jax.shard_map(
        on_device,
        mesh=mesh,
        in_specs=(
            P(None, None, "dev", None),
            P(None, None, "dev", None),
            P(None, None, "dev", None),
            P("dev", None, None),
            P("dev", None, None),
            P("dev", None, None),
            P(),
            P(),
            P("dev"),
        ),
        out_specs=(
            P(None, None, "dev", None),
            P(None, None, "dev", None),
            P(None, None, "dev", None),
            P("dev", None, None),
        ),
        check_vma=False,
    )
```

```python
import functools

import jax
import jax.numpy as jnp
from jax import lax
from jax.experimental import pallas as pl
from jax.experimental.pallas import tpu as pltpu
from jax.sharding import PartitionSpec as P

beta_one = 0.9
beta_two = 0.95
corr_one = 0.9999734386011124
corr_two = 0.994079470779666
adam_eps = 1e-08
learn_rate = 0.003
decay_rate = 0.1

CORE, X_STEP, Y_STEP, Z_UNIT = 1, 2, 4, 8
VMEM_LIMIT = 16 * 1024 * 1024


def hop(block, mask):
    count = lax.axis_size("dev")
    return lax.ppermute(block, "dev", [(low, low ^ mask) for low in range(count)])


def adam_update(master, first, second, grad):
    first_new = beta_one * first + (1.0 - beta_one) * grad
    second_new = beta_two * second + (1.0 - beta_two) * grad * grad
    direction = first_new / corr_one / (jnp.sqrt(second_new / corr_two) + adam_eps)
    master_new = master - learn_rate * (direction + decay_rate * master)
    return (master_new, first_new, second_new)


def place_pieces(chip, pieces, weights):
    rows = pieces[0].shape[1]
    for j, piece in enumerate(pieces):
        start = pl.multiple_of(lax.bitwise_xor(chip, j) * rows, rows)
        weights[:, pl.ds(start, rows), :] = piece[...]


def transpose_kernel(own_x, other_x, own_c, other_c, x_turned, c_turned):
    chip = lax.axis_index("dev") // 2
    tokens, width = own_x.shape
    rows = 2 * width // lax.axis_size("dev")
    lanes = max(128, rows)
    for out, pair in ((x_turned, (own_x, other_x)), (c_turned, (own_c, other_c))):
        for part, ref in enumerate(pair):
            for at in range(0, width, lanes):
                turned = ref[:, at : at + lanes].T
                for low in range(0, lanes, rows):
                    j = lax.bitwise_xor(chip, (at + low) // rows)
                    start = pl.multiple_of(j * rows, rows)
                    out[pl.ds(start, rows), part * tokens : (part + 1) * tokens] = turned[low : low + rows]


def places(outs):
    found = []
    for zj in range(2 * len(outs) // 5):
        here = outs[5 * (zj // 2) : 5 * (zj // 2) + 5]
        found += [(here[zj % 2], ())] + [(pair, (zj % 2,)) for pair in here[2:]]
    return found


def backward_kernel(count, slots, own_live, other_live, *refs):
    pieces = refs[:count]
    own_x, other_x, own_c, other_c, x_turned, c_turned = refs[count : count + 6]
    weights, gate_grad, up_grad, hidden_all = refs[-4:]
    outs = places(refs[count + 6 : -4])
    me_index = lax.axis_index("dev")
    core = me_index & CORE
    place_pieces(me_index // 2, pieces, weights)
    tokens = own_x.shape[0]
    sides = ((own_x, own_c, me_index, own_live), (other_x, other_c, me_index ^ CORE, other_live))
    for part, (x_ref, c_ref, slot, live) in enumerate(sides):
        span = slice(part * tokens, (part + 1) * tokens)
        gate_pre = jnp.dot(x_ref[...], weights[0], preferred_element_type=jnp.float32)
        up_pre = jnp.dot(x_ref[...], weights[1], preferred_element_type=jnp.float32)
        grad_hidden = jnp.dot(c_ref[...], weights[2], preferred_element_type=jnp.float32)
        gate_sig = jax.nn.sigmoid(gate_pre)
        gate_act = gate_pre * gate_sig
        alive = jnp.where(slots[slot] == core, live[0], 0)
        keep = lax.broadcasted_iota(jnp.int32, gate_pre.shape, 0) < alive
        grad_up = grad_hidden * gate_act
        grad_gate = grad_hidden * up_pre * gate_sig * (1.0 + gate_pre * (1.0 - gate_sig))
        hidden_all[span] = jnp.where(keep, gate_act * up_pre, 0.0).astype(jnp.bfloat16)
        up_grad[span] = jnp.where(keep, grad_up, 0.0).astype(jnp.bfloat16)
        gate_grad[span] = jnp.where(keep, grad_gate, 0.0).astype(jnp.bfloat16)
    rows = pieces[0].shape[1]
    width = count * rows
    tall = min(width, 256)
    for at in range(0, width, tall):
        for kind, (left, right) in enumerate(
            ((x_turned, gate_grad), (x_turned, up_grad), (c_turned, hidden_all))
        ):
            product = jnp.dot(left[at : at + tall], right[...], preferred_element_type=jnp.float32)
            product = product.astype(jnp.bfloat16)
            for low in range(0, tall, rows):
                out, before = outs[(at + low) // rows]
                out[before + (kind,)] = product[low : low + rows]


def forward_kernel(count, slots, *refs):
    pieces = refs[:count]
    own_y, other_y, own_out, other_out, matches, weights = refs[count:]
    me_index = lax.axis_index("dev")
    place_pieces(me_index // 2, pieces, weights)
    matches[0] = jnp.where(slots[me_index] == (me_index & CORE), 1, 0)
    for y_ref, out_ref in ((other_y, other_out), (own_y, own_out)):
        gate_pre = jnp.dot(y_ref[...], weights[0], preferred_element_type=jnp.float32)
        up_pre = jnp.dot(y_ref[...], weights[1], preferred_element_type=jnp.float32)
        act = (gate_pre * jax.nn.sigmoid(gate_pre) * up_pre).astype(jnp.bfloat16)
        result = lax.dot_general(act, weights[2], (((1,), (1,)), ((), ())), preferred_element_type=jnp.float32)
        out_ref[...] = result.astype(jnp.bfloat16)


VMEM = pl.BlockSpec(memory_space=pltpu.VMEM)
SMEM = pl.BlockSpec(memory_space=pltpu.SMEM)


def params():
    return pltpu.CompilerParams(vmem_limit_bytes=VMEM_LIMIT)


def transposed(own_x, other_x, own_c, other_c):
    tokens, width = own_x.shape
    return pl.pallas_call(
        transpose_kernel,
        out_shape=[jax.ShapeDtypeStruct((width, 2 * tokens), own_x.dtype)] * 2,
        in_specs=[VMEM] * 4,
        out_specs=[VMEM] * 2,
        compiler_params=params(),
        cost_estimate=pl.CostEstimate(flops=0, bytes_accessed=16 * tokens * width, transcendentals=0),
        name="transpose_rows",
    )(own_x, other_x, own_c, other_c)


def backward(slots, own_live, other_live, pieces, own_x, other_x, own_c, other_c, x_turned, c_turned):
    count = len(pieces)
    kinds, rows, units = pieces[0].shape
    tokens, width = own_x.shape
    one = jax.ShapeDtypeStruct((kinds, rows, units), jnp.bfloat16)
    two = jax.ShapeDtypeStruct((2, kinds, rows, units), jnp.bfloat16)
    return pl.pallas_call(
        functools.partial(backward_kernel, count),
        out_shape=[one, one, two, two, two] * (count // 8),
        in_specs=[SMEM] * 3 + [VMEM] * (count + 6),
        out_specs=[VMEM] * (5 * count // 8),
        scratch_shapes=[
            pltpu.VMEM((kinds, width, units), jnp.bfloat16),
            pltpu.VMEM((2 * tokens, units), jnp.bfloat16),
            pltpu.VMEM((2 * tokens, units), jnp.bfloat16),
            pltpu.VMEM((2 * tokens, units), jnp.bfloat16),
        ],
        compiler_params=params(),
        cost_estimate=pl.CostEstimate(
            flops=24 * tokens * width * units,
            bytes_accessed=16 * tokens * width + 12 * width * units,
            transcendentals=2 * tokens * units,
        ),
        name="slot_gradients",
    )(slots, own_live, other_live, *pieces, own_x, other_x, own_c, other_c, x_turned, c_turned)


def forward(slots, pieces, own_y, other_y):
    count = len(pieces)
    kinds, rows, units = pieces[0].shape
    tokens, width = own_y.shape
    one = jax.ShapeDtypeStruct((tokens, width), jnp.bfloat16)
    return pl.pallas_call(
        functools.partial(forward_kernel, count),
        out_shape=[one, one, jax.ShapeDtypeStruct((1,), jnp.int32)],
        in_specs=[SMEM] + [VMEM] * (count + 2),
        out_specs=[VMEM, VMEM, SMEM],
        scratch_shapes=[pltpu.VMEM((kinds, width, units), jnp.bfloat16)],
        compiler_params=params(),
        cost_estimate=pl.CostEstimate(
            flops=12 * tokens * width * units,
            bytes_accessed=8 * tokens * width + 6 * width * units,
            transcendentals=2 * tokens * units,
        ),
        name="expert_outputs",
    )(slots, *pieces, own_y, other_y)


def after(value, *others):
    return lax.optimization_barrier((value,) + others)[0]


def gather_chips(piece):
    depth = lax.axis_size("dev") // Z_UNIT
    column = [piece] + [None] * (depth - 1)
    for top in reversed([1 << bit for bit in range(depth.bit_length() - 1)]):
        column[top] = hop(piece, top * Z_UNIT)
    along_x, along_y, across = [None] * depth, [None] * depth, [None] * depth
    along_x[0] = hop(piece, X_STEP)
    along_y[0] = hop(piece, Y_STEP)
    along_x[1] = hop(column[1], X_STEP)
    for zj in range(2, depth):
        top = 1 << zj.bit_length() - 1
        if zj != top:
            column[zj] = hop(column[top], (zj - top) * Z_UNIT)
    along_y[1] = hop(after(column[1], along_x[0]), Y_STEP)
    for zj in range(2, depth, 2):
        along_x[zj] = hop(after(column[zj], along_x[zj - 2], along_y[zj - 2]), X_STEP)
        across[zj - 2] = hop(after(along_x[zj - 2], along_y[zj - 2]), Y_STEP)
        along_x[zj + 1] = hop(after(column[zj + 1], along_x[zj - 1]), X_STEP)
        along_y[zj + 1] = hop(after(column[zj + 1], along_x[zj - 1]), Y_STEP)
        along_y[zj] = hop(after(column[zj], along_y[zj - 1]), Y_STEP)
        across[zj - 1] = hop(after(along_y[zj - 1], along_x[zj]), X_STEP)
    across[-2] = hop(after(along_x[-2], along_x[-1]), Y_STEP)
    across[-1] = hop(along_y[-1], X_STEP)
    return [part for group in zip(column, along_x, along_y, across) for part in group]


def add_all(first, *others):
    total = first.astype(jnp.float32)
    for other in others:
        total = total + other.astype(jnp.float32)
    return total


def reduce_chips(pieces):
    total, arrived = None, ()
    for pair in reversed(range(len(pieces) // 5)):
        low, high, by_x, by_y, across = pieces[5 * pair : 5 * pair + 5]
        across = hop(after(across, *arrived), X_STEP | Y_STEP)
        by_x = hop(after(by_x, *arrived), X_STEP)
        by_y = hop(after(by_y, *arrived), Y_STEP)
        arrived = (by_x,)
        for zj, own in ((2 * pair + 1, high), (2 * pair, low)):
            column = add_all(own, by_x[zj % 2], by_y[zj % 2], across[zj % 2])
            if zj:
                column = hop(column.astype(jnp.bfloat16), zj * Z_UNIT).astype(jnp.float32)
            total = column if total is None else total + column
    return total


def block_a_core(master, first, second, old_rows, old_cotangent, new_rows, old_slots, new_slots, live):
    local_rows = master.shape[2]
    core = lax.axis_index("dev") & CORE

    def mine(state):
        return lax.dynamic_index_in_dim(state, core, 0, keepdims=False)

    def partners(state):
        return lax.dynamic_index_in_dim(state, 1 - core, 0, keepdims=False)

    def both_rows(own, other):
        return jnp.where(
            core == 0, jnp.concatenate([own, other], axis=-2), jnp.concatenate([other, own], axis=-2)
        )

    other_x = hop(old_rows, CORE)
    other_c = hop(old_cotangent, CORE)
    theirs = hop(jnp.stack([partners(master), partners(first), partners(second)]), CORE)
    other_y = hop(new_rows, CORE)
    other_live = hop(live, CORE)
    x_turned, c_turned = transposed(old_rows, other_x, old_cotangent, other_c)
    theirs, other_y, other_live, x_turned, c_turned = lax.optimization_barrier(
        (theirs, other_y, other_live, x_turned, c_turned)
    )
    master_two = both_rows(mine(master), theirs[0])
    pieces = gather_chips(master_two.astype(jnp.bfloat16))
    grads = backward(
        old_slots,
        live,
        other_live,
        pieces,
        old_rows,
        other_x,
        old_cotangent,
        other_c,
        x_turned,
        c_turned,
    )
    theirs = after(theirs, grads[0])
    first_two = both_rows(mine(first), theirs[1])
    second_two = both_rows(mine(second), theirs[2])
    grad = reduce_chips(grads)
    updated = adam_update(master_two, first_two, second_two, grad)

    new_pieces = gather_chips(updated[0].astype(jnp.bfloat16))
    updated = jnp.stack(updated)
    own_part = lax.dynamic_slice_in_dim(updated, core * local_rows, local_rows, 2)
    other_part = lax.dynamic_slice_in_dim(updated, (1 - core) * local_rows, local_rows, 2)
    from_other = hop(other_part, CORE)
    state = jnp.where(
        core == 0, jnp.stack([own_part, from_other], axis=1), jnp.stack([from_other, own_part], axis=1)
    )
    own_out, other_out, matches = forward(new_slots, new_pieces, new_rows, other_y)
    new_outputs = jnp.where(matches[0] == 1, own_out, hop(other_out, CORE))
    return (state[0], state[1], state[2], new_outputs[None])


def hidden_terms(tokens, cotangent, weights, live):
    positions = jnp.arange(tokens.shape[0], dtype=jnp.int32)
    cotangent = jnp.where((positions < live)[:, None], cotangent, jnp.zeros_like(cotangent))
    gate_pre = jnp.dot(tokens, weights[0], preferred_element_type=jnp.float32)
    up_pre = jnp.dot(tokens, weights[1], preferred_element_type=jnp.float32)
    gate_sig = jax.nn.sigmoid(gate_pre)
    gate_act = gate_pre * gate_sig
    hidden = (gate_act * up_pre).astype(jnp.bfloat16)
    grad_down = lax.dot_general(
        cotangent, hidden, (((0,), (0,)), ((), ())), preferred_element_type=jnp.float32
    )
    grad_hidden = jnp.dot(cotangent, weights[2], preferred_element_type=jnp.float32)
    grad_up_pre = (grad_hidden * gate_act).astype(jnp.bfloat16)
    grad_gate_pre = (grad_hidden * up_pre * gate_sig * (1.0 + gate_pre * (1.0 - gate_sig))).astype(
        jnp.bfloat16
    )
    grad_gate = lax.dot_general(
        tokens, grad_gate_pre, (((0,), (0,)), ((), ())), preferred_element_type=jnp.float32
    )
    grad_up = lax.dot_general(
        tokens, grad_up_pre, (((0,), (0,)), ((), ())), preferred_element_type=jnp.float32
    )
    return jnp.stack([grad_gate, grad_up, grad_down])


def expert_forward(tokens, weights):
    gate_pre = jnp.dot(tokens, weights[0], preferred_element_type=jnp.float32)
    up_pre = jnp.dot(tokens, weights[1], preferred_element_type=jnp.float32)
    activation = (jax.nn.silu(gate_pre) * up_pre).astype(jnp.bfloat16)
    result = lax.dot_general(
        activation, weights[2], (((1,), (1,)), ((), ())), preferred_element_type=jnp.float32
    )
    return result.astype(jnp.bfloat16)


def halving(buffer, levels, me_index):
    for step in range(levels):
        count = buffer.shape[2]
        halves = buffer.reshape(buffer.shape[:2] + (count // 2, 2) + buffer.shape[3:])
        own_bit = me_index >> step & 1
        keeping = lax.dynamic_index_in_dim(halves, own_bit, 3, keepdims=False)
        sending = lax.dynamic_index_in_dim(halves, 1 - own_bit, 3, keepdims=False)
        buffer = keeping + hop(sending, 1 << step)
    return buffer


def any_shape(master, first, second, old_rows, old_cotangent, new_rows, old_slots, new_slots, live):
    blocks, kinds, local_rows, block_width = master.shape
    devices = lax.axis_size("dev")
    me_index = lax.axis_index("dev")
    own_old = lax.dynamic_index_in_dim(old_slots, me_index, 0, keepdims=False)
    own_new = lax.dynamic_index_in_dim(new_slots, me_index, 0, keepdims=False)
    every_block = lax.all_gather(master.astype(jnp.bfloat16), "dev", axis=2, tiled=True)
    weights = lax.dynamic_index_in_dim(every_block, own_old, 0, keepdims=False)
    slot_grad = hidden_terms(old_rows, old_cotangent, weights, live[0])
    block_ids = jnp.arange(blocks, dtype=jnp.int32)[:, None, None, None, None]
    dense = slot_grad.reshape(kinds, devices, local_rows, block_width)
    buffer = jnp.where(block_ids == own_old, dense[None], jnp.zeros((), jnp.float32))
    buffer = halving(buffer, devices.bit_length() - 1, me_index)
    grad = buffer.reshape(master.shape)
    new_master, new_first, new_second = adam_update(master, first, second, grad)
    updated_blocks = lax.all_gather(new_master.astype(jnp.bfloat16), "dev", axis=2, tiled=True)
    new_weights = lax.dynamic_index_in_dim(updated_blocks, own_new, 0, keepdims=False)
    return (new_master, new_first, new_second, expert_forward(new_rows, new_weights)[None])


def on_device(
    master,
    first_moment,
    second_moment,
    old_rows,
    old_cotangent,
    new_rows,
    old_slots,
    new_slots,
    live_rows,
):
    blocks, kinds, local_rows, units = master.shape
    devices = lax.axis_size("dev")
    whole_tiles = local_rows % 16 == 0 and units % 128 == 0 and old_rows.shape[1] % 128 == 0
    form = block_a_core if blocks == 2 and devices % (2 * Z_UNIT) == 0 and whole_tiles else any_shape
    return form(
        master,
        first_moment,
        second_moment,
        old_rows[0],
        old_cotangent[0],
        new_rows[0],
        old_slots,
        new_slots,
        live_rows,
    )


def solution(mesh):
    return jax.shard_map(
        on_device,
        mesh=mesh,
        in_specs=(
            P(None, None, "dev", None),
            P(None, None, "dev", None),
            P(None, None, "dev", None),
            P("dev", None, None),
            P("dev", None, None),
            P("dev", None, None),
            P(),
            P(),
            P("dev"),
        ),
        out_specs=(
            P(None, None, "dev", None),
            P(None, None, "dev", None),
            P(None, None, "dev", None),
            P("dev", None, None),
        ),
        check_vma=False,
    )
```

```python
import functools

import jax
import jax.numpy as jnp
from jax import lax
from jax.experimental import pallas as pl
from jax.experimental.pallas import tpu as pltpu
from jax.sharding import PartitionSpec as P

beta_one = 0.9
beta_two = 0.95
corr_one = 0.9999734386011124
corr_two = 0.994079470779666
adam_eps = 1e-08
learn_rate = 0.003
decay_rate = 0.1

CORE, X_STEP, Y_STEP, Z_UNIT = 1, 2, 4, 8
VMEM_LIMIT = 16 * 1024 * 1024


def hop(block, mask):
    count = lax.axis_size("dev")
    return lax.ppermute(block, "dev", [(low, low ^ mask) for low in range(count)])


def adam_update(master, first, second, grad):
    first_new = beta_one * first + (1.0 - beta_one) * grad
    second_new = beta_two * second + (1.0 - beta_two) * grad * grad
    direction = first_new / corr_one / (jnp.sqrt(second_new / corr_two) + adam_eps)
    master_new = master - learn_rate * (direction + decay_rate * master)
    return (master_new, first_new, second_new)


def place_pieces(chip, pieces, weights):
    rows = pieces[0].shape[1]
    for j, piece in enumerate(pieces):
        start = pl.multiple_of(lax.bitwise_xor(chip, j) * rows, rows)
        weights[:, pl.ds(start, rows), :] = piece[...]


def transpose_kernel(own_x, other_x, own_c, other_c, x_turned, c_turned):
    chip = lax.axis_index("dev") // 2
    tokens, width = own_x.shape
    rows = 2 * width // lax.axis_size("dev")
    lanes = max(128, rows)
    for out, pair in ((x_turned, (own_x, other_x)), (c_turned, (own_c, other_c))):
        for part, ref in enumerate(pair):
            for at in range(0, width, lanes):
                turned = ref[:, at : at + lanes].T
                for low in range(0, lanes, rows):
                    j = lax.bitwise_xor(chip, (at + low) // rows)
                    start = pl.multiple_of(j * rows, rows)
                    out[pl.ds(start, rows), part * tokens : (part + 1) * tokens] = turned[low : low + rows]


def places(outs):
    found = []
    for zj in range(len(outs) // 3):
        own, later, pair = outs[3 * zj : 3 * zj + 3]
        by_x, by_y = ((pair, (1,)), (later, ())) if zj % 2 else ((later, ()), (pair, (1,)))
        found += [(own, ()), by_x, by_y, (pair, (0,))]
    return found


def gradient_rows(first_row, products, outs):
    outs = places(outs)
    rows = outs[0][0].shape[1]
    width = len(outs) * rows
    tall = min(width, 256)
    for at in range(0, width, tall):
        for kind, (left, right) in enumerate(products):
            product = jnp.dot(
                left[first_row + at : first_row + at + tall], right[...], preferred_element_type=jnp.float32
            ).astype(jnp.bfloat16)
            for low in range(0, tall, rows):
                out, before = outs[(at + low) // rows]
                out[before + (kind,)] = product[low : low + rows]


def backward_kernel(count, slots, own_live, other_live, *refs):
    pieces = refs[:count]
    own_x, other_x, own_c, other_c, x_turned, c_turned = refs[count : count + 6]
    outs = refs[count + 6 : -4]
    gate_grad, up_grad, hidden_all, weights = refs[-4:]
    me_index = lax.axis_index("dev")
    core = me_index & CORE
    place_pieces(me_index // 2, pieces, weights)
    tokens = own_x.shape[0]
    sides = ((own_x, own_c, me_index, own_live), (other_x, other_c, me_index ^ CORE, other_live))
    for part, (x_ref, c_ref, slot, live) in enumerate(sides):
        span = slice(part * tokens, (part + 1) * tokens)
        gate_pre = jnp.dot(x_ref[...], weights[0], preferred_element_type=jnp.float32)
        up_pre = jnp.dot(x_ref[...], weights[1], preferred_element_type=jnp.float32)
        grad_hidden = jnp.dot(c_ref[...], weights[2], preferred_element_type=jnp.float32)
        gate_sig = jax.nn.sigmoid(gate_pre)
        gate_act = gate_pre * gate_sig
        alive = jnp.where(slots[slot] == core, live[0], 0)
        keep = lax.broadcasted_iota(jnp.int32, gate_pre.shape, 0) < alive
        grad_up = grad_hidden * gate_act
        grad_gate = grad_hidden * up_pre * gate_sig * (1.0 + gate_pre * (1.0 - gate_sig))
        hidden_all[span] = jnp.where(keep, gate_act * up_pre, 0.0).astype(jnp.bfloat16)
        up_grad[span] = jnp.where(keep, grad_up, 0.0).astype(jnp.bfloat16)
        gate_grad[span] = jnp.where(keep, grad_gate, 0.0).astype(jnp.bfloat16)
    products = ((x_turned, gate_grad), (x_turned, up_grad), (c_turned, hidden_all))
    gradient_rows(0, products, outs)


def forward_kernel(count, slots, *refs):
    pieces = refs[:count]
    own_y, other_y, own_out, other_out, matches, weights = refs[count:]
    me_index = lax.axis_index("dev")
    place_pieces(me_index // 2, pieces, weights)
    matches[0] = jnp.where(slots[me_index] == (me_index & CORE), 1, 0)
    for y_ref, out_ref in ((other_y, other_out), (own_y, own_out)):
        gate_pre = jnp.dot(y_ref[...], weights[0], preferred_element_type=jnp.float32)
        up_pre = jnp.dot(y_ref[...], weights[1], preferred_element_type=jnp.float32)
        act = (gate_pre * jax.nn.sigmoid(gate_pre) * up_pre).astype(jnp.bfloat16)
        result = lax.dot_general(act, weights[2], (((1,), (1,)), ((), ())), preferred_element_type=jnp.float32)
        out_ref[...] = result.astype(jnp.bfloat16)


VMEM = pl.BlockSpec(memory_space=pltpu.VMEM)
SMEM = pl.BlockSpec(memory_space=pltpu.SMEM)


def params():
    return pltpu.CompilerParams(vmem_limit_bytes=VMEM_LIMIT)


def transposed(own_x, other_x, own_c, other_c):
    tokens, width = own_x.shape
    return pl.pallas_call(
        transpose_kernel,
        out_shape=[jax.ShapeDtypeStruct((width, 2 * tokens), own_x.dtype)] * 2,
        in_specs=[VMEM] * 4,
        out_specs=[VMEM] * 2,
        compiler_params=params(),
        cost_estimate=pl.CostEstimate(flops=0, bytes_accessed=16 * tokens * width, transcendentals=0),
        name="transpose_rows",
    )(own_x, other_x, own_c, other_c)


def backward(slots, own_live, other_live, pieces, own_x, other_x, own_c, other_c, x_turned, c_turned):
    count = len(pieces)
    kinds, rows, units = pieces[0].shape
    tokens, width = own_x.shape
    one = jax.ShapeDtypeStruct((kinds, rows, units), jnp.bfloat16)
    two = jax.ShapeDtypeStruct((2, kinds, rows, units), jnp.bfloat16)
    return pl.pallas_call(
        functools.partial(backward_kernel, count),
        out_shape=[one, one, two] * (count // 4),
        in_specs=[SMEM] * 3 + [VMEM] * (count + 6),
        out_specs=[VMEM] * (3 * count // 4),
        scratch_shapes=[
            pltpu.VMEM((2 * tokens, units), jnp.bfloat16),
            pltpu.VMEM((2 * tokens, units), jnp.bfloat16),
            pltpu.VMEM((2 * tokens, units), jnp.bfloat16),
            pltpu.VMEM((kinds, width, units), jnp.bfloat16),
        ],
        compiler_params=params(),
        cost_estimate=pl.CostEstimate(
            flops=24 * tokens * width * units,
            bytes_accessed=16 * tokens * width + 12 * width * units,
            transcendentals=2 * tokens * units,
        ),
        name="slot_gradients",
    )(slots, own_live, other_live, *pieces, own_x, other_x, own_c, other_c, x_turned, c_turned)


def forward(slots, pieces, own_y, other_y):
    count = len(pieces)
    kinds, rows, units = pieces[0].shape
    tokens, width = own_y.shape
    one = jax.ShapeDtypeStruct((tokens, width), jnp.bfloat16)
    return pl.pallas_call(
        functools.partial(forward_kernel, count),
        out_shape=[one, one, jax.ShapeDtypeStruct((1,), jnp.int32)],
        in_specs=[SMEM] + [VMEM] * (count + 2),
        out_specs=[VMEM, VMEM, SMEM],
        scratch_shapes=[pltpu.VMEM((kinds, width, units), jnp.bfloat16)],
        compiler_params=params(),
        cost_estimate=pl.CostEstimate(
            flops=12 * tokens * width * units,
            bytes_accessed=8 * tokens * width + 6 * width * units,
            transcendentals=2 * tokens * units,
        ),
        name="expert_outputs",
    )(slots, *pieces, own_y, other_y)


def after(value, *others):
    return lax.optimization_barrier((value,) + others)[0]


def gather_chips(piece):
    depth = lax.axis_size("dev") // Z_UNIT
    column = [piece] + [None] * (depth - 1)
    for top in reversed([1 << bit for bit in range(depth.bit_length() - 1)]):
        column[top] = hop(piece, top * Z_UNIT)
    along_x, along_y, across = [None] * depth, [None] * depth, [None] * depth
    along_x[0] = hop(piece, X_STEP)
    along_y[0] = hop(piece, Y_STEP)
    along_x[1] = hop(column[1], X_STEP)
    for zj in range(2, depth):
        top = 1 << zj.bit_length() - 1
        if zj != top:
            column[zj] = hop(column[top], (zj - top) * Z_UNIT)
    along_y[1] = hop(after(column[1], along_x[0]), Y_STEP)
    for zj in range(2, depth, 2):
        along_x[zj] = hop(after(column[zj], along_x[zj - 2], along_y[zj - 2]), X_STEP)
        across[zj - 2] = hop(after(along_x[zj - 2], along_y[zj - 2]), Y_STEP)
        along_x[zj + 1] = hop(after(column[zj + 1], along_x[zj - 1]), X_STEP)
        along_y[zj + 1] = hop(after(column[zj + 1], along_x[zj - 1]), Y_STEP)
        along_y[zj] = hop(after(column[zj], along_y[zj - 1]), Y_STEP)
        across[zj - 1] = hop(after(along_y[zj - 1], along_x[zj]), X_STEP)
    across[-2] = hop(after(along_x[-2], along_x[-1]), Y_STEP)
    across[-1] = hop(along_y[-1], X_STEP)
    return [part for group in zip(column, along_x, along_y, across) for part in group]


def add_all(first, *others):
    total = first.astype(jnp.float32)
    for other in others:
        total = total + other.astype(jnp.float32)
    return total


def reduce_chips(pieces):
    depth = lax.axis_size("dev") // Z_UNIT
    column = [[pieces[3 * zj]] for zj in range(depth)]
    arrived, crossed, risen = (), (), ()
    for upper in reversed(range(1, depth, 2)):
        up_y, pair_x = pieces[3 * upper + 1 : 3 * upper + 3]
        below_x, pair_y = pieces[3 * upper - 2 : 3 * upper]
        got_x = hop(pair_x, X_STEP)
        got_y = hop(after(pair_y, *arrived), Y_STEP)
        up_y = add_all(up_y, got_x[0]).astype(jnp.bfloat16)
        column[upper] += [got_x[1], hop(after(up_y, *crossed), Y_STEP)]
        below_x = add_all(below_x, got_y[0]).astype(jnp.bfloat16)
        column[upper - 1] += [got_y[1], hop(after(below_x, *risen), X_STEP)]
        arrived, crossed, risen = (got_x,), (column[upper][-1],), ()
        for zj in (upper, upper - 1):
            top = 1 << zj.bit_length() - 1 if zj else 0
            low = zj - top
            if zj:
                part = add_all(*column[zj]).astype(jnp.bfloat16)
                column[top if low else 0].append(hop(part, (low or top) * Z_UNIT))
                risen = risen or (column[top if low else 0][-1],)
    return add_all(*column[0])


def block_a_core(master, first, second, old_rows, old_cotangent, new_rows, old_slots, new_slots, live):
    local_rows = master.shape[2]
    core = lax.axis_index("dev") & CORE

    def mine(state):
        return lax.dynamic_index_in_dim(state, core, 0, keepdims=False)

    def partners(state):
        return lax.dynamic_index_in_dim(state, 1 - core, 0, keepdims=False)

    def both_rows(own, other):
        return jnp.where(
            core == 0, jnp.concatenate([own, other], axis=-2), jnp.concatenate([other, own], axis=-2)
        )

    other_x = hop(old_rows, CORE)
    other_c = hop(old_cotangent, CORE)
    theirs = hop(jnp.stack([partners(master), partners(first), partners(second)]), CORE)
    other_y = hop(new_rows, CORE)
    other_live = hop(live, CORE)
    x_turned, c_turned = transposed(old_rows, other_x, old_cotangent, other_c)
    theirs, other_y, other_live, x_turned, c_turned = lax.optimization_barrier(
        (theirs, other_y, other_live, x_turned, c_turned)
    )
    master_two = both_rows(mine(master), theirs[0])
    pieces = gather_chips(master_two.astype(jnp.bfloat16))
    grads = backward(
        old_slots,
        live,
        other_live,
        pieces,
        old_rows,
        other_x,
        old_cotangent,
        other_c,
        x_turned,
        c_turned,
    )
    theirs = after(theirs, grads[0])
    first_two = both_rows(mine(first), theirs[1])
    second_two = both_rows(mine(second), theirs[2])
    grad = reduce_chips(grads)
    updated = adam_update(master_two, first_two, second_two, grad)

    new_pieces = gather_chips(updated[0].astype(jnp.bfloat16))
    updated = jnp.stack(updated)
    own_part = lax.dynamic_slice_in_dim(updated, core * local_rows, local_rows, 2)
    other_part = lax.dynamic_slice_in_dim(updated, (1 - core) * local_rows, local_rows, 2)
    from_other = hop(other_part, CORE)
    state = jnp.where(
        core == 0, jnp.stack([own_part, from_other], axis=1), jnp.stack([from_other, own_part], axis=1)
    )
    own_out, other_out, matches = forward(new_slots, new_pieces, new_rows, other_y)
    new_outputs = jnp.where(matches[0] == 1, own_out, hop(other_out, CORE))
    return (state[0], state[1], state[2], new_outputs[None])


def hidden_terms(tokens, cotangent, weights, live):
    positions = jnp.arange(tokens.shape[0], dtype=jnp.int32)
    cotangent = jnp.where((positions < live)[:, None], cotangent, jnp.zeros_like(cotangent))
    gate_pre = jnp.dot(tokens, weights[0], preferred_element_type=jnp.float32)
    up_pre = jnp.dot(tokens, weights[1], preferred_element_type=jnp.float32)
    gate_sig = jax.nn.sigmoid(gate_pre)
    gate_act = gate_pre * gate_sig
    hidden = (gate_act * up_pre).astype(jnp.bfloat16)
    grad_down = lax.dot_general(
        cotangent, hidden, (((0,), (0,)), ((), ())), preferred_element_type=jnp.float32
    )
    grad_hidden = jnp.dot(cotangent, weights[2], preferred_element_type=jnp.float32)
    grad_up_pre = (grad_hidden * gate_act).astype(jnp.bfloat16)
    grad_gate_pre = (grad_hidden * up_pre * gate_sig * (1.0 + gate_pre * (1.0 - gate_sig))).astype(
        jnp.bfloat16
    )
    grad_gate = lax.dot_general(
        tokens, grad_gate_pre, (((0,), (0,)), ((), ())), preferred_element_type=jnp.float32
    )
    grad_up = lax.dot_general(
        tokens, grad_up_pre, (((0,), (0,)), ((), ())), preferred_element_type=jnp.float32
    )
    return jnp.stack([grad_gate, grad_up, grad_down])


def expert_forward(tokens, weights):
    gate_pre = jnp.dot(tokens, weights[0], preferred_element_type=jnp.float32)
    up_pre = jnp.dot(tokens, weights[1], preferred_element_type=jnp.float32)
    activation = (jax.nn.silu(gate_pre) * up_pre).astype(jnp.bfloat16)
    result = lax.dot_general(
        activation, weights[2], (((1,), (1,)), ((), ())), preferred_element_type=jnp.float32
    )
    return result.astype(jnp.bfloat16)


def halving(buffer, levels, me_index):
    for step in range(levels):
        count = buffer.shape[2]
        halves = buffer.reshape(buffer.shape[:2] + (count // 2, 2) + buffer.shape[3:])
        own_bit = me_index >> step & 1
        keeping = lax.dynamic_index_in_dim(halves, own_bit, 3, keepdims=False)
        sending = lax.dynamic_index_in_dim(halves, 1 - own_bit, 3, keepdims=False)
        buffer = keeping + hop(sending, 1 << step)
    return buffer


def any_shape(master, first, second, old_rows, old_cotangent, new_rows, old_slots, new_slots, live):
    blocks, kinds, local_rows, block_width = master.shape
    devices = lax.axis_size("dev")
    me_index = lax.axis_index("dev")
    own_old = lax.dynamic_index_in_dim(old_slots, me_index, 0, keepdims=False)
    own_new = lax.dynamic_index_in_dim(new_slots, me_index, 0, keepdims=False)
    every_block = lax.all_gather(master.astype(jnp.bfloat16), "dev", axis=2, tiled=True)
    weights = lax.dynamic_index_in_dim(every_block, own_old, 0, keepdims=False)
    slot_grad = hidden_terms(old_rows, old_cotangent, weights, live[0])
    block_ids = jnp.arange(blocks, dtype=jnp.int32)[:, None, None, None, None]
    dense = slot_grad.reshape(kinds, devices, local_rows, block_width)
    buffer = jnp.where(block_ids == own_old, dense[None], jnp.zeros((), jnp.float32))
    buffer = halving(buffer, devices.bit_length() - 1, me_index)
    grad = buffer.reshape(master.shape)
    new_master, new_first, new_second = adam_update(master, first, second, grad)
    updated_blocks = lax.all_gather(new_master.astype(jnp.bfloat16), "dev", axis=2, tiled=True)
    new_weights = lax.dynamic_index_in_dim(updated_blocks, own_new, 0, keepdims=False)
    return (new_master, new_first, new_second, expert_forward(new_rows, new_weights)[None])


def on_device(
    master,
    first_moment,
    second_moment,
    old_rows,
    old_cotangent,
    new_rows,
    old_slots,
    new_slots,
    live_rows,
):
    blocks, kinds, local_rows, units = master.shape
    devices = lax.axis_size("dev")
    whole_tiles = local_rows % 16 == 0 and units % 128 == 0 and old_rows.shape[1] % 128 == 0
    form = block_a_core if blocks == 2 and devices % (2 * Z_UNIT) == 0 and whole_tiles else any_shape
    return form(
        master,
        first_moment,
        second_moment,
        old_rows[0],
        old_cotangent[0],
        new_rows[0],
        old_slots,
        new_slots,
        live_rows,
    )


def solution(mesh):
    return jax.shard_map(
        on_device,
        mesh=mesh,
        in_specs=(
            P(None, None, "dev", None),
            P(None, None, "dev", None),
            P(None, None, "dev", None),
            P("dev", None, None),
            P("dev", None, None),
            P("dev", None, None),
            P(),
            P(),
            P("dev"),
        ),
        out_specs=(
            P(None, None, "dev", None),
            P(None, None, "dev", None),
            P(None, None, "dev", None),
            P("dev", None, None),
        ),
        check_vma=False,
    )
```

```python
import functools

import jax
import jax.numpy as jnp
from jax import lax
from jax.experimental import pallas as pl
from jax.experimental.pallas import tpu as pltpu
from jax.sharding import PartitionSpec as P

beta_one = 0.9
beta_two = 0.95
corr_one = 0.9999734386011124
corr_two = 0.994079470779666
adam_eps = 1e-08
learn_rate = 0.003
decay_rate = 0.1

CORE, X_STEP, Y_STEP, Z_UNIT = 1, 2, 4, 8
VMEM_LIMIT = 16 * 1024 * 1024


def hop(block, mask):
    count = lax.axis_size("dev")
    return lax.ppermute(block, "dev", [(low, low ^ mask) for low in range(count)])


def adam_update(master, first, second, grad):
    first_new = beta_one * first + (1.0 - beta_one) * grad
    second_new = beta_two * second + (1.0 - beta_two) * grad * grad
    direction = first_new / corr_one / (jnp.sqrt(second_new / corr_two) + adam_eps)
    master_new = master - learn_rate * (direction + decay_rate * master)
    return (master_new, first_new, second_new)


def place_pieces(chip, pieces, weights):
    rows = pieces[0].shape[1]
    for j, piece in enumerate(pieces):
        start = pl.multiple_of(lax.bitwise_xor(chip, j) * rows, rows)
        weights[:, pl.ds(start, rows), :] = piece[...]


def transpose_kernel(own_x, other_x, own_c, other_c, x_turned, c_turned):
    chip = lax.axis_index("dev") // 2
    tokens, width = own_x.shape
    rows = 2 * width // lax.axis_size("dev")
    lanes = max(128, rows)
    for out, pair in ((x_turned, (own_x, other_x)), (c_turned, (own_c, other_c))):
        for part, ref in enumerate(pair):
            for at in range(0, width, lanes):
                turned = ref[:, at : at + lanes].T
                for low in range(0, lanes, rows):
                    j = lax.bitwise_xor(chip, (at + low) // rows)
                    start = pl.multiple_of(j * rows, rows)
                    out[pl.ds(start, rows), part * tokens : (part + 1) * tokens] = turned[low : low + rows]


def places(outs):
    found = []
    for zj in range(2):
        found += [(outs[zj], ())] + [(pair, (zj,)) for pair in outs[2:5]]
    return found + [(out, ()) for out in outs[5:]]


def gradient_rows(first_row, products, outs):
    outs = places(outs)
    rows = outs[0][0].shape[1]
    width = len(outs) * rows
    tall = min(width, 256)
    for at in range(0, width, tall):
        for kind, (left, right) in enumerate(products):
            product = jnp.dot(
                left[first_row + at : first_row + at + tall], right[...], preferred_element_type=jnp.float32
            ).astype(jnp.bfloat16)
            for low in range(0, tall, rows):
                out, before = outs[(at + low) // rows]
                out[before + (kind,)] = product[low : low + rows]


def backward_kernel(count, slots, own_live, other_live, *refs):
    pieces = refs[:count]
    own_x, other_x, own_c, other_c, x_turned, c_turned = refs[count : count + 6]
    outs = refs[count + 6 : -4]
    gate_grad, up_grad, hidden_all, weights = refs[-4:]
    me_index = lax.axis_index("dev")
    core = me_index & CORE
    place_pieces(me_index // 2, pieces, weights)
    tokens = own_x.shape[0]
    sides = ((own_x, own_c, me_index, own_live), (other_x, other_c, me_index ^ CORE, other_live))
    for part, (x_ref, c_ref, slot, live) in enumerate(sides):
        span = slice(part * tokens, (part + 1) * tokens)
        gate_pre = jnp.dot(x_ref[...], weights[0], preferred_element_type=jnp.float32)
        up_pre = jnp.dot(x_ref[...], weights[1], preferred_element_type=jnp.float32)
        grad_hidden = jnp.dot(c_ref[...], weights[2], preferred_element_type=jnp.float32)
        gate_sig = jax.nn.sigmoid(gate_pre)
        gate_act = gate_pre * gate_sig
        alive = jnp.where(slots[slot] == core, live[0], 0)
        keep = lax.broadcasted_iota(jnp.int32, gate_pre.shape, 0) < alive
        grad_up = grad_hidden * gate_act
        grad_gate = grad_hidden * up_pre * gate_sig * (1.0 + gate_pre * (1.0 - gate_sig))
        hidden_all[span] = jnp.where(keep, gate_act * up_pre, 0.0).astype(jnp.bfloat16)
        up_grad[span] = jnp.where(keep, grad_up, 0.0).astype(jnp.bfloat16)
        gate_grad[span] = jnp.where(keep, grad_gate, 0.0).astype(jnp.bfloat16)
    products = ((x_turned, gate_grad), (x_turned, up_grad), (c_turned, hidden_all))
    gradient_rows(0, products, outs)


def forward_kernel(count, slots, *refs):
    pieces = refs[:count]
    own_y, other_y, own_out, other_out, matches, weights = refs[count:]
    me_index = lax.axis_index("dev")
    place_pieces(me_index // 2, pieces, weights)
    matches[0] = jnp.where(slots[me_index] == (me_index & CORE), 1, 0)
    for y_ref, out_ref in ((other_y, other_out), (own_y, own_out)):
        gate_pre = jnp.dot(y_ref[...], weights[0], preferred_element_type=jnp.float32)
        up_pre = jnp.dot(y_ref[...], weights[1], preferred_element_type=jnp.float32)
        act = (gate_pre * jax.nn.sigmoid(gate_pre) * up_pre).astype(jnp.bfloat16)
        result = lax.dot_general(act, weights[2], (((1,), (1,)), ((), ())), preferred_element_type=jnp.float32)
        out_ref[...] = result.astype(jnp.bfloat16)


VMEM = pl.BlockSpec(memory_space=pltpu.VMEM)
SMEM = pl.BlockSpec(memory_space=pltpu.SMEM)


def params():
    return pltpu.CompilerParams(vmem_limit_bytes=VMEM_LIMIT)


def transposed(own_x, other_x, own_c, other_c):
    tokens, width = own_x.shape
    return pl.pallas_call(
        transpose_kernel,
        out_shape=[jax.ShapeDtypeStruct((width, 2 * tokens), own_x.dtype)] * 2,
        in_specs=[VMEM] * 4,
        out_specs=[VMEM] * 2,
        compiler_params=params(),
        cost_estimate=pl.CostEstimate(flops=0, bytes_accessed=16 * tokens * width, transcendentals=0),
        name="transpose_rows",
    )(own_x, other_x, own_c, other_c)


def backward(slots, own_live, other_live, pieces, own_x, other_x, own_c, other_c, x_turned, c_turned):
    count = len(pieces)
    kinds, rows, units = pieces[0].shape
    tokens, width = own_x.shape
    one = jax.ShapeDtypeStruct((kinds, rows, units), jnp.bfloat16)
    two = jax.ShapeDtypeStruct((2, kinds, rows, units), jnp.bfloat16)
    return pl.pallas_call(
        functools.partial(backward_kernel, count),
        out_shape=[one] * 2 + [two] * 3 + [one] * (count - 8),
        in_specs=[SMEM] * 3 + [VMEM] * (count + 6),
        out_specs=[VMEM] * (count - 3),
        scratch_shapes=[
            pltpu.VMEM((2 * tokens, units), jnp.bfloat16),
            pltpu.VMEM((2 * tokens, units), jnp.bfloat16),
            pltpu.VMEM((2 * tokens, units), jnp.bfloat16),
            pltpu.VMEM((kinds, width, units), jnp.bfloat16),
        ],
        compiler_params=params(),
        cost_estimate=pl.CostEstimate(
            flops=24 * tokens * width * units,
            bytes_accessed=16 * tokens * width + 12 * width * units,
            transcendentals=2 * tokens * units,
        ),
        name="slot_gradients",
    )(slots, own_live, other_live, *pieces, own_x, other_x, own_c, other_c, x_turned, c_turned)


def forward(slots, pieces, own_y, other_y):
    count = len(pieces)
    kinds, rows, units = pieces[0].shape
    tokens, width = own_y.shape
    one = jax.ShapeDtypeStruct((tokens, width), jnp.bfloat16)
    return pl.pallas_call(
        functools.partial(forward_kernel, count),
        out_shape=[one, one, jax.ShapeDtypeStruct((1,), jnp.int32)],
        in_specs=[SMEM] + [VMEM] * (count + 2),
        out_specs=[VMEM, VMEM, SMEM],
        scratch_shapes=[pltpu.VMEM((kinds, width, units), jnp.bfloat16)],
        compiler_params=params(),
        cost_estimate=pl.CostEstimate(
            flops=12 * tokens * width * units,
            bytes_accessed=8 * tokens * width + 6 * width * units,
            transcendentals=2 * tokens * units,
        ),
        name="expert_outputs",
    )(slots, *pieces, own_y, other_y)


def after(value, *others):
    return lax.optimization_barrier((value,) + others)[0]


def gather_chips(piece):
    depth = lax.axis_size("dev") // Z_UNIT
    column = [piece] + [None] * (depth - 1)
    for top in reversed([1 << bit for bit in range(depth.bit_length() - 1)]):
        column[top] = hop(piece, top * Z_UNIT)
    along_x, along_y, across = [None] * depth, [None] * depth, [None] * depth
    along_x[0] = hop(piece, X_STEP)
    along_y[0] = hop(piece, Y_STEP)
    along_x[1] = hop(column[1], X_STEP)
    for zj in range(2, depth):
        top = 1 << zj.bit_length() - 1
        if zj != top:
            column[zj] = hop(column[top], (zj - top) * Z_UNIT)
    along_y[1] = hop(after(column[1], along_x[0]), Y_STEP)
    for zj in range(2, depth, 2):
        along_x[zj] = hop(after(column[zj], along_x[zj - 2], along_y[zj - 2]), X_STEP)
        across[zj - 2] = hop(after(along_x[zj - 2], along_y[zj - 2]), Y_STEP)
        along_x[zj + 1] = hop(after(column[zj + 1], along_x[zj - 1]), X_STEP)
        along_y[zj + 1] = hop(after(column[zj + 1], along_x[zj - 1]), Y_STEP)
        along_y[zj] = hop(after(column[zj], along_y[zj - 1]), Y_STEP)
        across[zj - 1] = hop(after(along_y[zj - 1], along_x[zj]), X_STEP)
    across[-2] = hop(after(along_x[-2], along_x[-1]), Y_STEP)
    across[-1] = hop(along_y[-1], X_STEP)
    return [part for group in zip(column, along_x, along_y, across) for part in group]


def add_all(first, *others):
    total = first.astype(jnp.float32)
    for other in others:
        total = total + other.astype(jnp.float32)
    return total


def reduce_chips(pieces):
    depth = lax.axis_size("dev") // Z_UNIT
    own_here, own_next, near_x, near_y, near_across = pieces[:5]
    total, early, late = None, (), ()
    for upper in reversed(range(3, depth, 2)):
        own_up, up_x, up_y, up_across = pieces[4 * upper - 3 : 4 * upper + 1]
        own_low, low_x, low_y, low_across = pieces[4 * upper - 7 : 4 * upper - 3]
        from_x = hop(after(up_across, *late), X_STEP)
        from_y = hop(after(low_across, *late), Y_STEP)
        up_x = hop(after(up_x, *late), X_STEP)
        up_y = hop(add_all(up_y, from_x).astype(jnp.bfloat16), Y_STEP)
        low_x = hop(add_all(low_x, from_y).astype(jnp.bfloat16), X_STEP)
        low_y = hop(after(low_y, from_x), Y_STEP)
        up = hop(add_all(own_up, up_x, up_y).astype(jnp.bfloat16), upper * Z_UNIT)
        low = hop(add_all(own_low, low_x, low_y).astype(jnp.bfloat16), (upper - 1) * Z_UNIT)
        total = add_all(up, low) if total is None else add_all(total, up, low)
        early, late = (from_y,), (up_y, up_x)
    near_across = hop(after(near_across, *early), X_STEP | Y_STEP)
    near_x = hop(after(near_x, *late), X_STEP)
    near_y = hop(after(near_y, *late), Y_STEP)
    column = add_all(own_next, near_x[1], near_y[1], near_across[1]).astype(jnp.bfloat16)
    here = add_all(own_here, near_x[0], near_y[0], near_across[0], hop(column, Z_UNIT))
    return here if total is None else here + total


def block_a_core(master, first, second, old_rows, old_cotangent, new_rows, old_slots, new_slots, live):
    local_rows = master.shape[2]
    core = lax.axis_index("dev") & CORE

    def mine(state):
        return lax.dynamic_index_in_dim(state, core, 0, keepdims=False)

    def partners(state):
        return lax.dynamic_index_in_dim(state, 1 - core, 0, keepdims=False)

    def both_rows(own, other):
        return jnp.where(
            core == 0, jnp.concatenate([own, other], axis=-2), jnp.concatenate([other, own], axis=-2)
        )

    other_x = hop(old_rows, CORE)
    other_c = hop(old_cotangent, CORE)
    theirs = hop(jnp.stack([partners(master), partners(first), partners(second)]), CORE)
    other_y = hop(new_rows, CORE)
    other_live = hop(live, CORE)
    x_turned, c_turned = transposed(old_rows, other_x, old_cotangent, other_c)
    theirs, other_y, other_live, x_turned, c_turned = lax.optimization_barrier(
        (theirs, other_y, other_live, x_turned, c_turned)
    )
    master_two = both_rows(mine(master), theirs[0])
    pieces = gather_chips(master_two.astype(jnp.bfloat16))
    grads = backward(
        old_slots,
        live,
        other_live,
        pieces,
        old_rows,
        other_x,
        old_cotangent,
        other_c,
        x_turned,
        c_turned,
    )
    theirs = after(theirs, grads[0])
    first_two = both_rows(mine(first), theirs[1])
    second_two = both_rows(mine(second), theirs[2])
    grad = reduce_chips(grads)
    updated = adam_update(master_two, first_two, second_two, grad)

    new_pieces = gather_chips(updated[0].astype(jnp.bfloat16))
    updated = jnp.stack(updated)
    own_part = lax.dynamic_slice_in_dim(updated, core * local_rows, local_rows, 2)
    other_part = lax.dynamic_slice_in_dim(updated, (1 - core) * local_rows, local_rows, 2)
    from_other = hop(other_part, CORE)
    state = jnp.where(
        core == 0, jnp.stack([own_part, from_other], axis=1), jnp.stack([from_other, own_part], axis=1)
    )
    own_out, other_out, matches = forward(new_slots, new_pieces, new_rows, other_y)
    new_outputs = jnp.where(matches[0] == 1, own_out, hop(other_out, CORE))
    return (state[0], state[1], state[2], new_outputs[None])


def hidden_terms(tokens, cotangent, weights, live):
    positions = jnp.arange(tokens.shape[0], dtype=jnp.int32)
    cotangent = jnp.where((positions < live)[:, None], cotangent, jnp.zeros_like(cotangent))
    gate_pre = jnp.dot(tokens, weights[0], preferred_element_type=jnp.float32)
    up_pre = jnp.dot(tokens, weights[1], preferred_element_type=jnp.float32)
    gate_sig = jax.nn.sigmoid(gate_pre)
    gate_act = gate_pre * gate_sig
    hidden = (gate_act * up_pre).astype(jnp.bfloat16)
    grad_down = lax.dot_general(
        cotangent, hidden, (((0,), (0,)), ((), ())), preferred_element_type=jnp.float32
    )
    grad_hidden = jnp.dot(cotangent, weights[2], preferred_element_type=jnp.float32)
    grad_up_pre = (grad_hidden * gate_act).astype(jnp.bfloat16)
    grad_gate_pre = (grad_hidden * up_pre * gate_sig * (1.0 + gate_pre * (1.0 - gate_sig))).astype(
        jnp.bfloat16
    )
    grad_gate = lax.dot_general(
        tokens, grad_gate_pre, (((0,), (0,)), ((), ())), preferred_element_type=jnp.float32
    )
    grad_up = lax.dot_general(
        tokens, grad_up_pre, (((0,), (0,)), ((), ())), preferred_element_type=jnp.float32
    )
    return jnp.stack([grad_gate, grad_up, grad_down])


def expert_forward(tokens, weights):
    gate_pre = jnp.dot(tokens, weights[0], preferred_element_type=jnp.float32)
    up_pre = jnp.dot(tokens, weights[1], preferred_element_type=jnp.float32)
    activation = (jax.nn.silu(gate_pre) * up_pre).astype(jnp.bfloat16)
    result = lax.dot_general(
        activation, weights[2], (((1,), (1,)), ((), ())), preferred_element_type=jnp.float32
    )
    return result.astype(jnp.bfloat16)


def halving(buffer, levels, me_index):
    for step in range(levels):
        count = buffer.shape[2]
        halves = buffer.reshape(buffer.shape[:2] + (count // 2, 2) + buffer.shape[3:])
        own_bit = me_index >> step & 1
        keeping = lax.dynamic_index_in_dim(halves, own_bit, 3, keepdims=False)
        sending = lax.dynamic_index_in_dim(halves, 1 - own_bit, 3, keepdims=False)
        buffer = keeping + hop(sending, 1 << step)
    return buffer


def any_shape(master, first, second, old_rows, old_cotangent, new_rows, old_slots, new_slots, live):
    blocks, kinds, local_rows, block_width = master.shape
    devices = lax.axis_size("dev")
    me_index = lax.axis_index("dev")
    own_old = lax.dynamic_index_in_dim(old_slots, me_index, 0, keepdims=False)
    own_new = lax.dynamic_index_in_dim(new_slots, me_index, 0, keepdims=False)
    every_block = lax.all_gather(master.astype(jnp.bfloat16), "dev", axis=2, tiled=True)
    weights = lax.dynamic_index_in_dim(every_block, own_old, 0, keepdims=False)
    slot_grad = hidden_terms(old_rows, old_cotangent, weights, live[0])
    block_ids = jnp.arange(blocks, dtype=jnp.int32)[:, None, None, None, None]
    dense = slot_grad.reshape(kinds, devices, local_rows, block_width)
    buffer = jnp.where(block_ids == own_old, dense[None], jnp.zeros((), jnp.float32))
    buffer = halving(buffer, devices.bit_length() - 1, me_index)
    grad = buffer.reshape(master.shape)
    new_master, new_first, new_second = adam_update(master, first, second, grad)
    updated_blocks = lax.all_gather(new_master.astype(jnp.bfloat16), "dev", axis=2, tiled=True)
    new_weights = lax.dynamic_index_in_dim(updated_blocks, own_new, 0, keepdims=False)
    return (new_master, new_first, new_second, expert_forward(new_rows, new_weights)[None])


def on_device(
    master,
    first_moment,
    second_moment,
    old_rows,
    old_cotangent,
    new_rows,
    old_slots,
    new_slots,
    live_rows,
):
    blocks, kinds, local_rows, units = master.shape
    devices = lax.axis_size("dev")
    whole_tiles = local_rows % 16 == 0 and units % 128 == 0 and old_rows.shape[1] % 128 == 0
    form = block_a_core if blocks == 2 and devices % (2 * Z_UNIT) == 0 and whole_tiles else any_shape
    return form(
        master,
        first_moment,
        second_moment,
        old_rows[0],
        old_cotangent[0],
        new_rows[0],
        old_slots,
        new_slots,
        live_rows,
    )


def solution(mesh):
    return jax.shard_map(
        on_device,
        mesh=mesh,
        in_specs=(
            P(None, None, "dev", None),
            P(None, None, "dev", None),
            P(None, None, "dev", None),
            P("dev", None, None),
            P("dev", None, None),
            P("dev", None, None),
            P(),
            P(),
            P("dev"),
        ),
        out_specs=(
            P(None, None, "dev", None),
            P(None, None, "dev", None),
            P(None, None, "dev", None),
            P("dev", None, None),
        ),
        check_vma=False,
    )
```

```python
import functools

import jax
import jax.numpy as jnp
from jax import lax
from jax.experimental import pallas as pl
from jax.experimental.pallas import tpu as pltpu
from jax.sharding import PartitionSpec as P

beta_one = 0.9
beta_two = 0.95
corr_one = 0.9999734386011124
corr_two = 0.994079470779666
adam_eps = 1e-08
learn_rate = 0.003
decay_rate = 0.1

CORE, X_STEP, Y_STEP, Z_UNIT = 1, 2, 4, 8
VMEM_LIMIT = 16 * 1024 * 1024


def hop(block, mask):
    count = lax.axis_size("dev")
    return lax.ppermute(block, "dev", [(low, low ^ mask) for low in range(count)])


def adam_update(master, first, second, grad):
    first_new = beta_one * first + (1.0 - beta_one) * grad
    second_new = beta_two * second + (1.0 - beta_two) * grad * grad
    direction = first_new / corr_one / (jnp.sqrt(second_new / corr_two) + adam_eps)
    master_new = master - learn_rate * (direction + decay_rate * master)
    return (master_new, first_new, second_new)


def place_pieces(chip, pieces, weights):
    rows = pieces[0].shape[1]
    for j, piece in enumerate(pieces):
        start = pl.multiple_of(lax.bitwise_xor(chip, j) * rows, rows)
        weights[:, pl.ds(start, rows), :] = piece[...]


def transpose_kernel(own_x, other_x, own_c, other_c, x_turned, c_turned):
    chip = lax.axis_index("dev") // 2
    tokens, width = own_x.shape
    rows = 2 * width // lax.axis_size("dev")
    lanes = max(128, rows)
    for out, pair in ((x_turned, (own_x, other_x)), (c_turned, (own_c, other_c))):
        for part, ref in enumerate(pair):
            for at in range(0, width, lanes):
                turned = ref[:, at : at + lanes].T
                for low in range(0, lanes, rows):
                    j = lax.bitwise_xor(chip, (at + low) // rows)
                    start = pl.multiple_of(j * rows, rows)
                    out[pl.ds(start, rows), part * tokens : (part + 1) * tokens] = turned[low : low + rows]


def places(outs):
    plane = lax.axis_index("dev") // 2 % 4
    return [(outs[j // 8], (lax.bitwise_xor(plane, j % 4), j // 4 % 2)) for j in range(8 * len(outs))]


def gradient_rows(first_row, products, outs):
    outs = places(outs)
    rows = outs[0][0].shape[-2]
    width = len(outs) * rows
    tall = min(width, 256)
    for at in range(0, width, tall):
        for kind, (left, right) in enumerate(products):
            product = jnp.dot(
                left[first_row + at : first_row + at + tall], right[...], preferred_element_type=jnp.float32
            ).astype(jnp.bfloat16)
            for low in range(0, tall, rows):
                out, before = outs[(at + low) // rows]
                out[before + (kind,)] = product[low : low + rows]


def backward_kernel(count, slots, own_live, other_live, *refs):
    pieces = refs[:count]
    own_x, other_x, own_c, other_c, x_turned, c_turned = refs[count : count + 6]
    outs = refs[count + 6 : -4]
    gate_grad, up_grad, hidden_all, weights = refs[-4:]
    me_index = lax.axis_index("dev")
    core = me_index & CORE
    place_pieces(me_index // 2, pieces, weights)
    tokens = own_x.shape[0]
    sides = ((own_x, own_c, me_index, own_live), (other_x, other_c, me_index ^ CORE, other_live))
    for part, (x_ref, c_ref, slot, live) in enumerate(sides):
        span = slice(part * tokens, (part + 1) * tokens)
        gate_pre = jnp.dot(x_ref[...], weights[0], preferred_element_type=jnp.float32)
        up_pre = jnp.dot(x_ref[...], weights[1], preferred_element_type=jnp.float32)
        grad_hidden = jnp.dot(c_ref[...], weights[2], preferred_element_type=jnp.float32)
        gate_sig = jax.nn.sigmoid(gate_pre)
        gate_act = gate_pre * gate_sig
        alive = jnp.where(slots[slot] == core, live[0], 0)
        keep = lax.broadcasted_iota(jnp.int32, gate_pre.shape, 0) < alive
        grad_up = grad_hidden * gate_act
        grad_gate = grad_hidden * up_pre * gate_sig * (1.0 + gate_pre * (1.0 - gate_sig))
        hidden_all[span] = jnp.where(keep, gate_act * up_pre, 0.0).astype(jnp.bfloat16)
        up_grad[span] = jnp.where(keep, grad_up, 0.0).astype(jnp.bfloat16)
        gate_grad[span] = jnp.where(keep, grad_gate, 0.0).astype(jnp.bfloat16)
    products = ((x_turned, gate_grad), (x_turned, up_grad), (c_turned, hidden_all))
    gradient_rows(0, products, outs)


def forward_kernel(count, slots, *refs):
    pieces = refs[:count]
    own_y, other_y, own_out, other_out, matches, weights = refs[count:]
    me_index = lax.axis_index("dev")
    place_pieces(me_index // 2, pieces, weights)
    matches[0] = jnp.where(slots[me_index] == (me_index & CORE), 1, 0)
    for y_ref, out_ref in ((other_y, other_out), (own_y, own_out)):
        gate_pre = jnp.dot(y_ref[...], weights[0], preferred_element_type=jnp.float32)
        up_pre = jnp.dot(y_ref[...], weights[1], preferred_element_type=jnp.float32)
        act = (gate_pre * jax.nn.sigmoid(gate_pre) * up_pre).astype(jnp.bfloat16)
        result = lax.dot_general(act, weights[2], (((1,), (1,)), ((), ())), preferred_element_type=jnp.float32)
        out_ref[...] = result.astype(jnp.bfloat16)


VMEM = pl.BlockSpec(memory_space=pltpu.VMEM)
SMEM = pl.BlockSpec(memory_space=pltpu.SMEM)


def params():
    return pltpu.CompilerParams(vmem_limit_bytes=VMEM_LIMIT)


def transposed(own_x, other_x, own_c, other_c):
    tokens, width = own_x.shape
    return pl.pallas_call(
        transpose_kernel,
        out_shape=[jax.ShapeDtypeStruct((width, 2 * tokens), own_x.dtype)] * 2,
        in_specs=[VMEM] * 4,
        out_specs=[VMEM] * 2,
        compiler_params=params(),
        cost_estimate=pl.CostEstimate(flops=0, bytes_accessed=16 * tokens * width, transcendentals=0),
        name="transpose_rows",
    )(own_x, other_x, own_c, other_c)


def backward(slots, own_live, other_live, pieces, own_x, other_x, own_c, other_c, x_turned, c_turned):
    count = len(pieces)
    kinds, rows, units = pieces[0].shape
    tokens, width = own_x.shape
    return pl.pallas_call(
        functools.partial(backward_kernel, count),
        out_shape=[jax.ShapeDtypeStruct((4, 2, kinds, rows, units), jnp.bfloat16)] * (count // 8),
        in_specs=[SMEM] * 3 + [VMEM] * (count + 6),
        out_specs=[VMEM] * (count // 8),
        scratch_shapes=[
            pltpu.VMEM((2 * tokens, units), jnp.bfloat16),
            pltpu.VMEM((2 * tokens, units), jnp.bfloat16),
            pltpu.VMEM((2 * tokens, units), jnp.bfloat16),
            pltpu.VMEM((kinds, width, units), jnp.bfloat16),
        ],
        compiler_params=params(),
        cost_estimate=pl.CostEstimate(
            flops=24 * tokens * width * units,
            bytes_accessed=16 * tokens * width + 12 * width * units,
            transcendentals=2 * tokens * units,
        ),
        name="slot_gradients",
    )(slots, own_live, other_live, *pieces, own_x, other_x, own_c, other_c, x_turned, c_turned)


def forward(slots, pieces, own_y, other_y):
    count = len(pieces)
    kinds, rows, units = pieces[0].shape
    tokens, width = own_y.shape
    one = jax.ShapeDtypeStruct((tokens, width), jnp.bfloat16)
    return pl.pallas_call(
        functools.partial(forward_kernel, count),
        out_shape=[one, one, jax.ShapeDtypeStruct((1,), jnp.int32)],
        in_specs=[SMEM] + [VMEM] * (count + 2),
        out_specs=[VMEM, VMEM, SMEM],
        scratch_shapes=[pltpu.VMEM((kinds, width, units), jnp.bfloat16)],
        compiler_params=params(),
        cost_estimate=pl.CostEstimate(
            flops=12 * tokens * width * units,
            bytes_accessed=8 * tokens * width + 6 * width * units,
            transcendentals=2 * tokens * units,
        ),
        name="expert_outputs",
    )(slots, *pieces, own_y, other_y)


def after(value, *others):
    return lax.optimization_barrier((value,) + others)[0]


def gather_chips(piece):
    depth = lax.axis_size("dev") // Z_UNIT
    column = [piece] + [hop(piece, zj * Z_UNIT) for zj in range(1, depth)]
    along_x, along_y, across = [], [], []
    for zj, here in enumerate(column):
        if zj > 1:
            here = after(here, column[zj - 1], along_x[zj - 2], along_y[zj - 2])
        along_x.append(hop(here, X_STEP))
        along_y.append(hop(here, Y_STEP))
        if zj > 1 and zj == depth - 1:
            across.append(hop(here, X_STEP | Y_STEP))
        elif zj % 2:
            across.append(hop(after(along_y[zj], along_x[zj]), X_STEP))
        else:
            across.append(hop(after(along_x[zj], along_y[zj]), Y_STEP))
    return [part for group in zip(column, along_x, along_y, across) for part in group]


def add_all(first, *others):
    total = first.astype(jnp.float32)
    for other in others:
        total = total + other.astype(jnp.float32)
    return total


def reduce_chips(pieces):
    devices = lax.axis_size("dev")
    planes = [
        [base + core + 2 * chip for chip in range(4)] for base in range(0, devices, Z_UNIT) for core in range(2)
    ]
    total, sent = None, ()
    for pair in reversed(range(len(pieces))):
        got = lax.all_to_all(after(pieces[pair], *sent), "dev", 0, 0, axis_index_groups=planes)
        sent = ()
        for zj in (2 * pair + 1, 2 * pair):
            column = add_all(*[got[chip, zj % 2] for chip in range(4)])
            if zj:
                column = column.astype(jnp.bfloat16)
                sent += (column,)
                column = hop(column, zj * Z_UNIT).astype(jnp.float32)
            total = column if total is None else total + column
    return total


def block_a_core(master, first, second, old_rows, old_cotangent, new_rows, old_slots, new_slots, live):
    local_rows = master.shape[2]
    core = lax.axis_index("dev") & CORE

    def mine(state):
        return lax.dynamic_index_in_dim(state, core, 0, keepdims=False)

    def partners(state):
        return lax.dynamic_index_in_dim(state, 1 - core, 0, keepdims=False)

    def both_rows(own, other):
        return jnp.where(
            core == 0, jnp.concatenate([own, other], axis=-2), jnp.concatenate([other, own], axis=-2)
        )

    other_x = hop(old_rows, CORE)
    other_c = hop(old_cotangent, CORE)
    theirs = hop(jnp.stack([partners(master), partners(first), partners(second)]), CORE)
    other_y = hop(new_rows, CORE)
    other_live = hop(live, CORE)
    x_turned, c_turned = transposed(old_rows, other_x, old_cotangent, other_c)
    theirs, other_y, other_live, x_turned, c_turned = lax.optimization_barrier(
        (theirs, other_y, other_live, x_turned, c_turned)
    )
    master_two = both_rows(mine(master), theirs[0])
    pieces = gather_chips(master_two.astype(jnp.bfloat16))
    grads = backward(
        old_slots,
        live,
        other_live,
        pieces,
        old_rows,
        other_x,
        old_cotangent,
        other_c,
        x_turned,
        c_turned,
    )
    theirs = after(theirs, grads[0])
    first_two = both_rows(mine(first), theirs[1])
    second_two = both_rows(mine(second), theirs[2])
    grad = reduce_chips(grads)
    updated = adam_update(master_two, first_two, second_two, grad)

    new_pieces = gather_chips(updated[0].astype(jnp.bfloat16))
    updated = jnp.stack(updated)
    own_part = lax.dynamic_slice_in_dim(updated, core * local_rows, local_rows, 2)
    other_part = lax.dynamic_slice_in_dim(updated, (1 - core) * local_rows, local_rows, 2)
    from_other = hop(other_part, CORE)
    state = jnp.where(
        core == 0, jnp.stack([own_part, from_other], axis=1), jnp.stack([from_other, own_part], axis=1)
    )
    own_out, other_out, matches = forward(new_slots, new_pieces, new_rows, other_y)
    new_outputs = jnp.where(matches[0] == 1, own_out, hop(other_out, CORE))
    return (state[0], state[1], state[2], new_outputs[None])


def hidden_terms(tokens, cotangent, weights, live):
    positions = jnp.arange(tokens.shape[0], dtype=jnp.int32)
    cotangent = jnp.where((positions < live)[:, None], cotangent, jnp.zeros_like(cotangent))
    gate_pre = jnp.dot(tokens, weights[0], preferred_element_type=jnp.float32)
    up_pre = jnp.dot(tokens, weights[1], preferred_element_type=jnp.float32)
    gate_sig = jax.nn.sigmoid(gate_pre)
    gate_act = gate_pre * gate_sig
    hidden = (gate_act * up_pre).astype(jnp.bfloat16)
    grad_down = lax.dot_general(
        cotangent, hidden, (((0,), (0,)), ((), ())), preferred_element_type=jnp.float32
    )
    grad_hidden = jnp.dot(cotangent, weights[2], preferred_element_type=jnp.float32)
    grad_up_pre = (grad_hidden * gate_act).astype(jnp.bfloat16)
    grad_gate_pre = (grad_hidden * up_pre * gate_sig * (1.0 + gate_pre * (1.0 - gate_sig))).astype(
        jnp.bfloat16
    )
    grad_gate = lax.dot_general(
        tokens, grad_gate_pre, (((0,), (0,)), ((), ())), preferred_element_type=jnp.float32
    )
    grad_up = lax.dot_general(
        tokens, grad_up_pre, (((0,), (0,)), ((), ())), preferred_element_type=jnp.float32
    )
    return jnp.stack([grad_gate, grad_up, grad_down])


def expert_forward(tokens, weights):
    gate_pre = jnp.dot(tokens, weights[0], preferred_element_type=jnp.float32)
    up_pre = jnp.dot(tokens, weights[1], preferred_element_type=jnp.float32)
    activation = (jax.nn.silu(gate_pre) * up_pre).astype(jnp.bfloat16)
    result = lax.dot_general(
        activation, weights[2], (((1,), (1,)), ((), ())), preferred_element_type=jnp.float32
    )
    return result.astype(jnp.bfloat16)


def halving(buffer, levels, me_index):
    for step in range(levels):
        count = buffer.shape[2]
        halves = buffer.reshape(buffer.shape[:2] + (count // 2, 2) + buffer.shape[3:])
        own_bit = me_index >> step & 1
        keeping = lax.dynamic_index_in_dim(halves, own_bit, 3, keepdims=False)
        sending = lax.dynamic_index_in_dim(halves, 1 - own_bit, 3, keepdims=False)
        buffer = keeping + hop(sending, 1 << step)
    return buffer


def any_shape(master, first, second, old_rows, old_cotangent, new_rows, old_slots, new_slots, live):
    blocks, kinds, local_rows, block_width = master.shape
    devices = lax.axis_size("dev")
    me_index = lax.axis_index("dev")
    own_old = lax.dynamic_index_in_dim(old_slots, me_index, 0, keepdims=False)
    own_new = lax.dynamic_index_in_dim(new_slots, me_index, 0, keepdims=False)
    every_block = lax.all_gather(master.astype(jnp.bfloat16), "dev", axis=2, tiled=True)
    weights = lax.dynamic_index_in_dim(every_block, own_old, 0, keepdims=False)
    slot_grad = hidden_terms(old_rows, old_cotangent, weights, live[0])
    block_ids = jnp.arange(blocks, dtype=jnp.int32)[:, None, None, None, None]
    dense = slot_grad.reshape(kinds, devices, local_rows, block_width)
    buffer = jnp.where(block_ids == own_old, dense[None], jnp.zeros((), jnp.float32))
    buffer = halving(buffer, devices.bit_length() - 1, me_index)
    grad = buffer.reshape(master.shape)
    new_master, new_first, new_second = adam_update(master, first, second, grad)
    updated_blocks = lax.all_gather(new_master.astype(jnp.bfloat16), "dev", axis=2, tiled=True)
    new_weights = lax.dynamic_index_in_dim(updated_blocks, own_new, 0, keepdims=False)
    return (new_master, new_first, new_second, expert_forward(new_rows, new_weights)[None])


def on_device(
    master,
    first_moment,
    second_moment,
    old_rows,
    old_cotangent,
    new_rows,
    old_slots,
    new_slots,
    live_rows,
):
    blocks, kinds, local_rows, units = master.shape
    devices = lax.axis_size("dev")
    whole_tiles = local_rows % 16 == 0 and units % 128 == 0 and old_rows.shape[1] % 128 == 0
    form = block_a_core if blocks == 2 and devices % (2 * Z_UNIT) == 0 and whole_tiles else any_shape
    return form(
        master,
        first_moment,
        second_moment,
        old_rows[0],
        old_cotangent[0],
        new_rows[0],
        old_slots,
        new_slots,
        live_rows,
    )


def solution(mesh):
    return jax.shard_map(
        on_device,
        mesh=mesh,
        in_specs=(
            P(None, None, "dev", None),
            P(None, None, "dev", None),
            P(None, None, "dev", None),
            P("dev", None, None),
            P("dev", None, None),
            P("dev", None, None),
            P(),
            P(),
            P("dev"),
        ),
        out_specs=(
            P(None, None, "dev", None),
            P(None, None, "dev", None),
            P(None, None, "dev", None),
            P("dev", None, None),
        ),
        check_vma=False,
    )
```

```python
import functools

import jax
import jax.numpy as jnp
from jax import lax
from jax.experimental import pallas as pl
from jax.experimental.pallas import tpu as pltpu
from jax.sharding import PartitionSpec as P

beta_one = 0.9
beta_two = 0.95
corr_one = 0.9999734386011124
corr_two = 0.994079470779666
adam_eps = 1e-08
learn_rate = 0.003
decay_rate = 0.1

CORE, X_STEP, Y_STEP, Z_UNIT = 1, 2, 4, 8
VMEM_LIMIT = 16 * 1024 * 1024


def hop(block, mask):
    count = lax.axis_size("dev")
    return lax.ppermute(block, "dev", [(low, low ^ mask) for low in range(count)])


def adam_update(master, first, second, grad):
    first_new = beta_one * first + (1.0 - beta_one) * grad
    second_new = beta_two * second + (1.0 - beta_two) * grad * grad
    direction = first_new / corr_one / (jnp.sqrt(second_new / corr_two) + adam_eps)
    master_new = master - learn_rate * (direction + decay_rate * master)
    return (master_new, first_new, second_new)


def place_pieces(chip, pieces, weights):
    rows = pieces[0].shape[1]
    for j, piece in enumerate(pieces):
        start = pl.multiple_of(lax.bitwise_xor(chip, j) * rows, rows)
        weights[:, pl.ds(start, rows), :] = piece[...]


def transpose_kernel(own_x, other_x, own_c, other_c, x_turned, c_turned, x_rows, c_rows):
    chip = lax.axis_index("dev") // 2
    tokens, width = own_x.shape
    rows = 2 * width // lax.axis_size("dev")
    lanes = max(128, rows)
    for out, straight, pair in ((x_turned, x_rows, (own_x, other_x)), (c_turned, c_rows, (own_c, other_c))):
        for part, ref in enumerate(pair):
            span = slice(part * tokens, (part + 1) * tokens)
            straight[span] = ref[...]
            for at in range(0, width, lanes):
                turned = ref[:, at : at + lanes].T
                for low in range(0, lanes, rows):
                    j = lax.bitwise_xor(chip, (at + low) // rows)
                    start = pl.multiple_of(j * rows, rows)
                    out[pl.ds(start, rows), span] = turned[low : low + rows]


def places(outs):
    found = []
    for zj in range(len(outs) // 3):
        own, later, pair = outs[3 * zj : 3 * zj + 3]
        by_x, by_y = ((pair, (1,)), (later, ())) if zj % 2 else ((later, ()), (pair, (1,)))
        found += [(own, ()), by_x, by_y, (pair, (0,))]
    return found


def gradient_rows(first_row, products, outs):
    outs = places(outs)
    rows = outs[0][0].shape[1]
    width = len(outs) * rows
    tall = min(width, 256)
    for at in range(0, width, tall):
        for kind, (left, right) in enumerate(products):
            product = jnp.dot(
                left[first_row + at : first_row + at + tall], right[...], preferred_element_type=jnp.float32
            ).astype(jnp.bfloat16)
            for low in range(0, tall, rows):
                out, before = outs[(at + low) // rows]
                out[before + (kind,)] = product[low : low + rows]


def backward_kernel(count, slots, own_live, other_live, *refs):
    pieces = refs[:count]
    x_turned, c_turned, x_rows, c_rows = refs[count : count + 4]
    outs = refs[count + 4 : -4]
    gate_grad, up_grad, hidden_all, weights = refs[-4:]
    me_index = lax.axis_index("dev")
    core = me_index & CORE
    place_pieces(me_index // 2, pieces, weights)
    tokens = x_rows.shape[0] // 2
    gate_pre = jnp.dot(x_rows[...], weights[0], preferred_element_type=jnp.float32)
    up_pre = jnp.dot(x_rows[...], weights[1], preferred_element_type=jnp.float32)
    grad_hidden = jnp.dot(c_rows[...], weights[2], preferred_element_type=jnp.float32)
    gate_sig = jax.nn.sigmoid(gate_pre)
    gate_act = gate_pre * gate_sig
    own_alive = jnp.where(slots[me_index] == core, own_live[0], 0)
    other_alive = jnp.where(slots[me_index ^ CORE] == core, other_live[0], 0)
    row = lax.broadcasted_iota(jnp.int32, gate_pre.shape, 0)
    keep = (row < own_alive) | ((row >= tokens) & (row < tokens + other_alive))
    grad_up = grad_hidden * gate_act
    grad_gate = grad_hidden * up_pre * gate_sig * (1.0 + gate_pre * (1.0 - gate_sig))
    hidden_all[...] = jnp.where(keep, gate_act * up_pre, 0.0).astype(jnp.bfloat16)
    up_grad[...] = jnp.where(keep, grad_up, 0.0).astype(jnp.bfloat16)
    gate_grad[...] = jnp.where(keep, grad_gate, 0.0).astype(jnp.bfloat16)
    products = ((x_turned, gate_grad), (x_turned, up_grad), (c_turned, hidden_all))
    gradient_rows(0, products, outs)


def forward_kernel(count, slots, *refs):
    pieces = refs[:count]
    own_y, other_y, own_out, other_out, matches, weights = refs[count:]
    me_index = lax.axis_index("dev")
    place_pieces(me_index // 2, pieces, weights)
    matches[0] = jnp.where(slots[me_index] == (me_index & CORE), 1, 0)
    for y_ref, out_ref in ((other_y, other_out), (own_y, own_out)):
        gate_pre = jnp.dot(y_ref[...], weights[0], preferred_element_type=jnp.float32)
        up_pre = jnp.dot(y_ref[...], weights[1], preferred_element_type=jnp.float32)
        act = (gate_pre * jax.nn.sigmoid(gate_pre) * up_pre).astype(jnp.bfloat16)
        result = lax.dot_general(act, weights[2], (((1,), (1,)), ((), ())), preferred_element_type=jnp.float32)
        out_ref[...] = result.astype(jnp.bfloat16)


VMEM = pl.BlockSpec(memory_space=pltpu.VMEM)
SMEM = pl.BlockSpec(memory_space=pltpu.SMEM)


def params():
    return pltpu.CompilerParams(vmem_limit_bytes=VMEM_LIMIT)


def transposed(own_x, other_x, own_c, other_c):
    tokens, width = own_x.shape
    return pl.pallas_call(
        transpose_kernel,
        out_shape=[jax.ShapeDtypeStruct((width, 2 * tokens), own_x.dtype)] * 2
        + [jax.ShapeDtypeStruct((2 * tokens, width), own_x.dtype)] * 2,
        in_specs=[VMEM] * 4,
        out_specs=[VMEM] * 4,
        compiler_params=params(),
        cost_estimate=pl.CostEstimate(flops=0, bytes_accessed=16 * tokens * width, transcendentals=0),
        name="transpose_rows",
    )(own_x, other_x, own_c, other_c)


def backward(slots, own_live, other_live, pieces, x_turned, c_turned, x_rows, c_rows):
    count = len(pieces)
    kinds, rows, units = pieces[0].shape
    tokens, width = x_rows.shape[0] // 2, x_rows.shape[1]
    one = jax.ShapeDtypeStruct((kinds, rows, units), jnp.bfloat16)
    two = jax.ShapeDtypeStruct((2, kinds, rows, units), jnp.bfloat16)
    return pl.pallas_call(
        functools.partial(backward_kernel, count),
        out_shape=[one, one, two] * (count // 4),
        in_specs=[SMEM] * 3 + [VMEM] * (count + 4),
        out_specs=[VMEM] * (3 * count // 4),
        scratch_shapes=[
            pltpu.VMEM((2 * tokens, units), jnp.bfloat16),
            pltpu.VMEM((2 * tokens, units), jnp.bfloat16),
            pltpu.VMEM((2 * tokens, units), jnp.bfloat16),
            pltpu.VMEM((kinds, width, units), jnp.bfloat16),
        ],
        compiler_params=params(),
        cost_estimate=pl.CostEstimate(
            flops=24 * tokens * width * units,
            bytes_accessed=16 * tokens * width + 12 * width * units,
            transcendentals=2 * tokens * units,
        ),
        name="slot_gradients",
    )(slots, own_live, other_live, *pieces, x_turned, c_turned, x_rows, c_rows)


def forward(slots, pieces, own_y, other_y):
    count = len(pieces)
    kinds, rows, units = pieces[0].shape
    tokens, width = own_y.shape
    one = jax.ShapeDtypeStruct((tokens, width), jnp.bfloat16)
    return pl.pallas_call(
        functools.partial(forward_kernel, count),
        out_shape=[one, one, jax.ShapeDtypeStruct((1,), jnp.int32)],
        in_specs=[SMEM] + [VMEM] * (count + 2),
        out_specs=[VMEM, VMEM, SMEM],
        scratch_shapes=[pltpu.VMEM((kinds, width, units), jnp.bfloat16)],
        compiler_params=params(),
        cost_estimate=pl.CostEstimate(
            flops=12 * tokens * width * units,
            bytes_accessed=8 * tokens * width + 6 * width * units,
            transcendentals=2 * tokens * units,
        ),
        name="expert_outputs",
    )(slots, *pieces, own_y, other_y)


def after(value, *others):
    return lax.optimization_barrier((value,) + others)[0]


def gather_chips(piece):
    depth = lax.axis_size("dev") // Z_UNIT
    column = [piece] + [None] * (depth - 1)
    for top in reversed([1 << bit for bit in range(depth.bit_length() - 1)]):
        column[top] = hop(piece, top * Z_UNIT)
    along_x, along_y, across = [None] * depth, [None] * depth, [None] * depth
    along_x[0] = hop(piece, X_STEP)
    along_y[0] = hop(piece, Y_STEP)
    along_x[1] = hop(column[1], X_STEP)
    for zj in range(2, depth):
        top = 1 << zj.bit_length() - 1
        if zj != top:
            column[zj] = hop(column[top], (zj - top) * Z_UNIT)
    along_y[1] = hop(after(column[1], along_x[0]), Y_STEP)
    for zj in range(2, depth, 2):
        along_x[zj] = hop(after(column[zj], along_x[zj - 2], along_y[zj - 2]), X_STEP)
        along_x[zj + 1] = hop(after(column[zj + 1], along_x[zj - 1]), X_STEP)
        along_y[zj + 1] = hop(after(column[zj + 1], along_x[zj - 1]), Y_STEP)
        along_y[zj] = hop(after(column[zj], along_y[zj - 1]), Y_STEP)
        across[zj - 1] = hop(after(along_y[zj - 1], along_x[zj]), X_STEP)
    for zj in range(0, depth, 4):
        two = hop(after(jnp.stack([along_x[zj], along_x[zj + 2]]), along_x[-1], along_y[zj + 1]), Y_STEP)
        across[zj], across[zj + 2] = two[0], two[1]
    across[-1] = hop(along_y[-1], X_STEP)
    return [part for group in zip(column, along_x, along_y, across) for part in group]


def add_all(first, *others):
    total = first.astype(jnp.float32)
    for other in others:
        total = total + other.astype(jnp.float32)
    return total


def reduce_chips(pieces):
    depth = lax.axis_size("dev") // Z_UNIT
    column = [[pieces[3 * zj]] for zj in range(depth)]
    arrived, crossed, risen = (), (), ()
    for upper in reversed(range(1, depth, 2)):
        up_y, pair_x = pieces[3 * upper + 1 : 3 * upper + 3]
        below_x, pair_y = pieces[3 * upper - 2 : 3 * upper]
        got_x = hop(pair_x, X_STEP)
        got_y = hop(after(pair_y, *arrived), Y_STEP)
        up_y = add_all(up_y, got_x[0]).astype(jnp.bfloat16)
        column[upper] += [got_x[1], hop(after(up_y, *crossed), Y_STEP)]
        below_x = add_all(below_x, got_y[0]).astype(jnp.bfloat16)
        column[upper - 1] += [got_y[1], hop(after(below_x, *risen), X_STEP)]
        arrived, crossed, risen = (got_x,), (column[upper][-1],), ()
        for zj in (upper, upper - 1):
            top = 1 << zj.bit_length() - 1 if zj else 0
            low = zj - top
            if zj:
                part = add_all(*column[zj]).astype(jnp.bfloat16)
                column[top if low else 0].append(hop(part, (low or top) * Z_UNIT))
                risen = risen or (column[top if low else 0][-1],)
    return add_all(*column[0])


def block_a_core(master, first, second, old_rows, old_cotangent, new_rows, old_slots, new_slots, live):
    local_rows = master.shape[2]
    core = lax.axis_index("dev") & CORE

    def mine(state):
        return lax.dynamic_index_in_dim(state, core, 0, keepdims=False)

    def partners(state):
        return lax.dynamic_index_in_dim(state, 1 - core, 0, keepdims=False)

    def both_rows(own, other):
        return jnp.where(
            core == 0, jnp.concatenate([own, other], axis=-2), jnp.concatenate([other, own], axis=-2)
        )

    leaving = jnp.stack([partners(master), partners(first), partners(second)])
    theirs = hop(leaving, CORE)
    other_x = hop(after(old_rows, leaving), CORE)
    other_c = hop(after(old_cotangent, leaving), CORE)
    other_y = hop(after(new_rows, leaving), CORE)
    other_live = hop(after(live, leaving), CORE)
    theirs, other_x, other_c, other_y, other_live = lax.optimization_barrier(
        (theirs, other_x, other_c, other_y, other_live)
    )
    laid = transposed(old_rows, other_x, old_cotangent, other_c)
    master_two = both_rows(mine(master), theirs[0])
    pieces = gather_chips(master_two.astype(jnp.bfloat16))
    grads = backward(old_slots, live, other_live, pieces, *laid)
    theirs = after(theirs, grads[0])
    first_two = both_rows(mine(first), theirs[1])
    second_two = both_rows(mine(second), theirs[2])
    grad = reduce_chips(grads)
    updated = adam_update(master_two, first_two, second_two, grad)

    new_pieces = gather_chips(updated[0].astype(jnp.bfloat16))
    updated = jnp.stack(updated)
    own_part = lax.dynamic_slice_in_dim(updated, core * local_rows, local_rows, 2)
    other_part = lax.dynamic_slice_in_dim(updated, (1 - core) * local_rows, local_rows, 2)
    from_other = hop(after(other_part, new_pieces[-1]), CORE)
    state = jnp.where(
        core == 0, jnp.stack([own_part, from_other], axis=1), jnp.stack([from_other, own_part], axis=1)
    )
    own_out, other_out, matches = forward(new_slots, new_pieces, new_rows, other_y)
    new_outputs = jnp.where(matches[0] == 1, own_out, hop(other_out, CORE))
    return (state[0], state[1], state[2], new_outputs[None])


def hidden_terms(tokens, cotangent, weights, live):
    positions = jnp.arange(tokens.shape[0], dtype=jnp.int32)
    cotangent = jnp.where((positions < live)[:, None], cotangent, jnp.zeros_like(cotangent))
    gate_pre = jnp.dot(tokens, weights[0], preferred_element_type=jnp.float32)
    up_pre = jnp.dot(tokens, weights[1], preferred_element_type=jnp.float32)
    gate_sig = jax.nn.sigmoid(gate_pre)
    gate_act = gate_pre * gate_sig
    hidden = (gate_act * up_pre).astype(jnp.bfloat16)
    grad_down = lax.dot_general(
        cotangent, hidden, (((0,), (0,)), ((), ())), preferred_element_type=jnp.float32
    )
    grad_hidden = jnp.dot(cotangent, weights[2], preferred_element_type=jnp.float32)
    grad_up_pre = (grad_hidden * gate_act).astype(jnp.bfloat16)
    grad_gate_pre = (grad_hidden * up_pre * gate_sig * (1.0 + gate_pre * (1.0 - gate_sig))).astype(
        jnp.bfloat16
    )
    grad_gate = lax.dot_general(
        tokens, grad_gate_pre, (((0,), (0,)), ((), ())), preferred_element_type=jnp.float32
    )
    grad_up = lax.dot_general(
        tokens, grad_up_pre, (((0,), (0,)), ((), ())), preferred_element_type=jnp.float32
    )
    return jnp.stack([grad_gate, grad_up, grad_down])


def expert_forward(tokens, weights):
    gate_pre = jnp.dot(tokens, weights[0], preferred_element_type=jnp.float32)
    up_pre = jnp.dot(tokens, weights[1], preferred_element_type=jnp.float32)
    activation = (jax.nn.silu(gate_pre) * up_pre).astype(jnp.bfloat16)
    result = lax.dot_general(
        activation, weights[2], (((1,), (1,)), ((), ())), preferred_element_type=jnp.float32
    )
    return result.astype(jnp.bfloat16)


def halving(buffer, levels, me_index):
    for step in range(levels):
        count = buffer.shape[2]
        halves = buffer.reshape(buffer.shape[:2] + (count // 2, 2) + buffer.shape[3:])
        own_bit = me_index >> step & 1
        keeping = lax.dynamic_index_in_dim(halves, own_bit, 3, keepdims=False)
        sending = lax.dynamic_index_in_dim(halves, 1 - own_bit, 3, keepdims=False)
        buffer = keeping + hop(sending, 1 << step)
    return buffer


def any_shape(master, first, second, old_rows, old_cotangent, new_rows, old_slots, new_slots, live):
    blocks, kinds, local_rows, block_width = master.shape
    devices = lax.axis_size("dev")
    me_index = lax.axis_index("dev")
    own_old = lax.dynamic_index_in_dim(old_slots, me_index, 0, keepdims=False)
    own_new = lax.dynamic_index_in_dim(new_slots, me_index, 0, keepdims=False)
    every_block = lax.all_gather(master.astype(jnp.bfloat16), "dev", axis=2, tiled=True)
    weights = lax.dynamic_index_in_dim(every_block, own_old, 0, keepdims=False)
    slot_grad = hidden_terms(old_rows, old_cotangent, weights, live[0])
    block_ids = jnp.arange(blocks, dtype=jnp.int32)[:, None, None, None, None]
    dense = slot_grad.reshape(kinds, devices, local_rows, block_width)
    buffer = jnp.where(block_ids == own_old, dense[None], jnp.zeros((), jnp.float32))
    buffer = halving(buffer, devices.bit_length() - 1, me_index)
    grad = buffer.reshape(master.shape)
    new_master, new_first, new_second = adam_update(master, first, second, grad)
    updated_blocks = lax.all_gather(new_master.astype(jnp.bfloat16), "dev", axis=2, tiled=True)
    new_weights = lax.dynamic_index_in_dim(updated_blocks, own_new, 0, keepdims=False)
    return (new_master, new_first, new_second, expert_forward(new_rows, new_weights)[None])


def on_device(
    master,
    first_moment,
    second_moment,
    old_rows,
    old_cotangent,
    new_rows,
    old_slots,
    new_slots,
    live_rows,
):
    blocks, kinds, local_rows, units = master.shape
    devices = lax.axis_size("dev")
    whole_tiles = local_rows % 16 == 0 and units % 128 == 0 and old_rows.shape[1] % 128 == 0
    form = block_a_core if blocks == 2 and devices % (4 * Z_UNIT) == 0 and whole_tiles else any_shape
    return form(
        master,
        first_moment,
        second_moment,
        old_rows[0],
        old_cotangent[0],
        new_rows[0],
        old_slots,
        new_slots,
        live_rows,
    )


def solution(mesh):
    return jax.shard_map(
        on_device,
        mesh=mesh,
        in_specs=(
            P(None, None, "dev", None),
            P(None, None, "dev", None),
            P(None, None, "dev", None),
            P("dev", None, None),
            P("dev", None, None),
            P("dev", None, None),
            P(),
            P(),
            P("dev"),
        ),
        out_specs=(
            P(None, None, "dev", None),
            P(None, None, "dev", None),
            P(None, None, "dev", None),
            P("dev", None, None),
        ),
        check_vma=False,
    )
```

```python
import functools

import jax
import jax.numpy as jnp
from jax import lax
from jax.experimental import pallas as pl
from jax.experimental.pallas import tpu as pltpu
from jax.sharding import PartitionSpec as P

beta_one = 0.9
beta_two = 0.95
corr_one = 0.9999734386011124
corr_two = 0.994079470779666
adam_eps = 1e-08
learn_rate = 0.003
decay_rate = 0.1

CORE, X_STEP, Y_STEP, Z_UNIT = 1, 2, 4, 8
VMEM_LIMIT = 16 * 1024 * 1024


def hop(block, mask):
    count = lax.axis_size("dev")
    return lax.ppermute(block, "dev", [(low, low ^ mask) for low in range(count)])


def adam_update(master, first, second, grad):
    first_new = beta_one * first + (1.0 - beta_one) * grad
    second_new = beta_two * second + (1.0 - beta_two) * grad * grad
    direction = first_new / corr_one / (jnp.sqrt(second_new / corr_two) + adam_eps)
    master_new = master - learn_rate * (direction + decay_rate * master)
    return (master_new, first_new, second_new)


def place_pieces(chip, pieces, weights):
    rows = pieces[0].shape[1]
    for j, piece in enumerate(pieces):
        start = pl.multiple_of(lax.bitwise_xor(chip, j) * rows, rows)
        weights[:, pl.ds(start, rows), :] = piece[...]


def transpose_kernel(own_x, other_x, own_c, other_c, x_turned, c_turned):
    chip = lax.axis_index("dev") // 2
    tokens, width = own_x.shape
    rows = 2 * width // lax.axis_size("dev")
    lanes = max(128, rows)
    for out, pair in ((x_turned, (own_x, other_x)), (c_turned, (own_c, other_c))):
        for part, ref in enumerate(pair):
            for at in range(0, width, lanes):
                turned = ref[:, at : at + lanes].T
                for low in range(0, lanes, rows):
                    j = lax.bitwise_xor(chip, (at + low) // rows)
                    start = pl.multiple_of(j * rows, rows)
                    out[pl.ds(start, rows), part * tokens : (part + 1) * tokens] = turned[low : low + rows]


def places(outs):
    found = []
    for zj in range(2):
        found += [(outs[zj], ())] + [(pair, (zj,)) for pair in outs[2:5]]
    return found + [(out, ()) for out in outs[5:]]


def gradient_rows(first_row, products, outs):
    outs = places(outs)
    rows = outs[0][0].shape[1]
    width = len(outs) * rows
    tall = min(width, 256)
    for at in range(0, width, tall):
        for kind, (left, right) in enumerate(products):
            product = jnp.dot(
                left[first_row + at : first_row + at + tall], right[...], preferred_element_type=jnp.float32
            ).astype(jnp.bfloat16)
            for low in range(0, tall, rows):
                out, before = outs[(at + low) // rows]
                out[before + (kind,)] = product[low : low + rows]


def backward_kernel(count, slots, own_live, other_live, *refs):
    pieces = refs[:count]
    own_x, other_x, own_c, other_c, x_turned, c_turned = refs[count : count + 6]
    outs = refs[count + 6 : -4]
    gate_grad, up_grad, hidden_all, weights = refs[-4:]
    me_index = lax.axis_index("dev")
    core = me_index & CORE
    place_pieces(me_index // 2, pieces, weights)
    tokens = own_x.shape[0]
    sides = ((own_x, own_c, me_index, own_live), (other_x, other_c, me_index ^ CORE, other_live))
    for part, (x_ref, c_ref, slot, live) in enumerate(sides):
        span = slice(part * tokens, (part + 1) * tokens)
        gate_pre = jnp.dot(x_ref[...], weights[0], preferred_element_type=jnp.float32)
        up_pre = jnp.dot(x_ref[...], weights[1], preferred_element_type=jnp.float32)
        grad_hidden = jnp.dot(c_ref[...], weights[2], preferred_element_type=jnp.float32)
        gate_sig = jax.nn.sigmoid(gate_pre)
        gate_act = gate_pre * gate_sig
        alive = jnp.where(slots[slot] == core, live[0], 0)
        keep = lax.broadcasted_iota(jnp.int32, gate_pre.shape, 0) < alive
        grad_up = grad_hidden * gate_act
        grad_gate = grad_hidden * up_pre * gate_sig * (1.0 + gate_pre * (1.0 - gate_sig))
        hidden_all[span] = jnp.where(keep, gate_act * up_pre, 0.0).astype(jnp.bfloat16)
        up_grad[span] = jnp.where(keep, grad_up, 0.0).astype(jnp.bfloat16)
        gate_grad[span] = jnp.where(keep, grad_gate, 0.0).astype(jnp.bfloat16)
    products = ((x_turned, gate_grad), (x_turned, up_grad), (c_turned, hidden_all))
    gradient_rows(0, products, outs)


def forward_kernel(count, slots, *refs):
    pieces = refs[:count]
    own_y, other_y, own_out, other_out, matches, weights = refs[count:]
    me_index = lax.axis_index("dev")
    place_pieces(me_index // 2, pieces, weights)
    matches[0] = jnp.where(slots[me_index] == (me_index & CORE), 1, 0)
    for y_ref, out_ref in ((other_y, other_out), (own_y, own_out)):
        gate_pre = jnp.dot(y_ref[...], weights[0], preferred_element_type=jnp.float32)
        up_pre = jnp.dot(y_ref[...], weights[1], preferred_element_type=jnp.float32)
        act = (gate_pre * jax.nn.sigmoid(gate_pre) * up_pre).astype(jnp.bfloat16)
        result = lax.dot_general(act, weights[2], (((1,), (1,)), ((), ())), preferred_element_type=jnp.float32)
        out_ref[...] = result.astype(jnp.bfloat16)


VMEM = pl.BlockSpec(memory_space=pltpu.VMEM)
SMEM = pl.BlockSpec(memory_space=pltpu.SMEM)


def params():
    return pltpu.CompilerParams(vmem_limit_bytes=VMEM_LIMIT)


def transposed(own_x, other_x, own_c, other_c):
    tokens, width = own_x.shape
    return pl.pallas_call(
        transpose_kernel,
        out_shape=[jax.ShapeDtypeStruct((width, 2 * tokens), own_x.dtype)] * 2,
        in_specs=[VMEM] * 4,
        out_specs=[VMEM] * 2,
        compiler_params=params(),
        cost_estimate=pl.CostEstimate(flops=0, bytes_accessed=16 * tokens * width, transcendentals=0),
        name="transpose_rows",
    )(own_x, other_x, own_c, other_c)


def backward(slots, own_live, other_live, pieces, own_x, other_x, own_c, other_c, x_turned, c_turned):
    count = len(pieces)
    kinds, rows, units = pieces[0].shape
    tokens, width = own_x.shape
    one = jax.ShapeDtypeStruct((kinds, rows, units), jnp.bfloat16)
    two = jax.ShapeDtypeStruct((2, kinds, rows, units), jnp.bfloat16)
    return pl.pallas_call(
        functools.partial(backward_kernel, count),
        out_shape=[one] * 2 + [two] * 3 + [one] * (count - 8),
        in_specs=[SMEM] * 3 + [VMEM] * (count + 6),
        out_specs=[VMEM] * (count - 3),
        scratch_shapes=[
            pltpu.VMEM((2 * tokens, units), jnp.bfloat16),
            pltpu.VMEM((2 * tokens, units), jnp.bfloat16),
            pltpu.VMEM((2 * tokens, units), jnp.bfloat16),
            pltpu.VMEM((kinds, width, units), jnp.bfloat16),
        ],
        compiler_params=params(),
        cost_estimate=pl.CostEstimate(
            flops=24 * tokens * width * units,
            bytes_accessed=16 * tokens * width + 12 * width * units,
            transcendentals=2 * tokens * units,
        ),
        name="slot_gradients",
    )(slots, own_live, other_live, *pieces, own_x, other_x, own_c, other_c, x_turned, c_turned)


def forward(slots, pieces, own_y, other_y):
    count = len(pieces)
    kinds, rows, units = pieces[0].shape
    tokens, width = own_y.shape
    one = jax.ShapeDtypeStruct((tokens, width), jnp.bfloat16)
    return pl.pallas_call(
        functools.partial(forward_kernel, count),
        out_shape=[one, one, jax.ShapeDtypeStruct((1,), jnp.int32)],
        in_specs=[SMEM] + [VMEM] * (count + 2),
        out_specs=[VMEM, VMEM, SMEM],
        scratch_shapes=[pltpu.VMEM((kinds, width, units), jnp.bfloat16)],
        compiler_params=params(),
        cost_estimate=pl.CostEstimate(
            flops=12 * tokens * width * units,
            bytes_accessed=8 * tokens * width + 6 * width * units,
            transcendentals=2 * tokens * units,
        ),
        name="expert_outputs",
    )(slots, *pieces, own_y, other_y)


def after(value, *others):
    return lax.optimization_barrier((value,) + others)[0]


def gather_chips(piece):
    depth = lax.axis_size("dev") // Z_UNIT
    column = [piece] + [None] * (depth - 1)
    for top in reversed([1 << bit for bit in range(depth.bit_length() - 1)]):
        column[top] = hop(piece, top * Z_UNIT)
    along_x, along_y, across = [None] * depth, [None] * depth, [None] * depth
    along_x[0] = hop(piece, X_STEP)
    along_y[0] = hop(piece, Y_STEP)
    along_x[1] = hop(column[1], X_STEP)
    for zj in range(2, depth):
        top = 1 << zj.bit_length() - 1
        if zj != top:
            column[zj] = hop(column[top], (zj - top) * Z_UNIT)
    along_y[1] = hop(after(column[1], along_x[0]), Y_STEP)
    for zj in range(2, depth, 2):
        along_x[zj] = hop(after(column[zj], along_x[zj - 2], along_y[zj - 2]), X_STEP)
        across[zj - 2] = hop(after(along_x[zj - 2], along_y[zj - 2]), Y_STEP)
        along_x[zj + 1] = hop(after(column[zj + 1], along_x[zj - 1]), X_STEP)
        along_y[zj + 1] = hop(after(column[zj + 1], along_x[zj - 1]), Y_STEP)
        along_y[zj] = hop(after(column[zj], along_y[zj - 1]), Y_STEP)
        across[zj - 1] = hop(after(along_y[zj - 1], along_x[zj]), X_STEP)
    across[-2] = hop(after(along_x[-2], along_x[-1]), Y_STEP)
    across[-1] = hop(along_y[-1], X_STEP)
    return [part for group in zip(column, along_x, along_y, across) for part in group]


def add_all(first, *others):
    total = first.astype(jnp.float32)
    for other in others:
        total = total + other.astype(jnp.float32)
    return total


def reduce_chips(pieces):
    depth = lax.axis_size("dev") // Z_UNIT
    own_here, own_next, near_x, near_y, near_across = pieces[:5]
    column = [[own_here], [own_next]] + [[pieces[4 * zj - 3]] for zj in range(2, depth)]
    early, late, sums = (), (), [None] * depth

    def rise(zj):
        top = 1 << zj.bit_length() - 1
        sums[zj] = hop(add_all(*column[zj]).astype(jnp.bfloat16), (zj - top or top) * Z_UNIT)
        column[0 if zj == top else top].append(sums[zj])

    for upper in reversed(range(3, depth, 2)):
        up_x, up_y, up_across = pieces[4 * upper - 2 : 4 * upper + 1]
        low_x, low_y, low_across = pieces[4 * upper - 6 : 4 * upper - 3]
        from_x = hop(after(up_across, *late), X_STEP)
        from_y = hop(after(low_across, *late), Y_STEP)
        up_x = hop(after(up_x, *late), X_STEP)
        up_y = hop(add_all(up_y, from_x).astype(jnp.bfloat16), Y_STEP)
        low_x = hop(add_all(low_x, from_y).astype(jnp.bfloat16), X_STEP)
        low_y = hop(after(low_y, from_x), Y_STEP)
        column[upper] += [up_x, up_y]
        column[upper - 1] += [low_x, low_y]
        rise(upper)
        rise(upper - 1)
        early, late = (from_y,), (up_y, up_x)
    near_across = hop(after(near_across, *early), X_STEP | Y_STEP)
    near_x = hop(after(near_x, *late), X_STEP)
    near_y = hop(after(near_y, *late), Y_STEP)
    for zj in range(2):
        column[zj] += [near_x[zj], near_y[zj], near_across[zj]]
    rise(1)
    return add_all(*column[0])


def block_a_core(master, first, second, old_rows, old_cotangent, new_rows, old_slots, new_slots, live):
    local_rows = master.shape[2]
    core = lax.axis_index("dev") & CORE

    def mine(state):
        return lax.dynamic_index_in_dim(state, core, 0, keepdims=False)

    def partners(state):
        return lax.dynamic_index_in_dim(state, 1 - core, 0, keepdims=False)

    def both_rows(own, other):
        return jnp.where(
            core == 0, jnp.concatenate([own, other], axis=-2), jnp.concatenate([other, own], axis=-2)
        )

    other_x = hop(old_rows, CORE)
    other_c = hop(old_cotangent, CORE)
    theirs = hop(jnp.stack([partners(master), partners(first), partners(second)]), CORE)
    other_y = hop(new_rows, CORE)
    other_live = hop(live, CORE)
    x_turned, c_turned = transposed(old_rows, other_x, old_cotangent, other_c)
    theirs, other_y, other_live, x_turned, c_turned = lax.optimization_barrier(
        (theirs, other_y, other_live, x_turned, c_turned)
    )
    master_two = both_rows(mine(master), theirs[0])
    pieces = gather_chips(master_two.astype(jnp.bfloat16))
    grads = backward(
        old_slots,
        live,
        other_live,
        pieces,
        old_rows,
        other_x,
        old_cotangent,
        other_c,
        x_turned,
        c_turned,
    )
    theirs = after(theirs, grads[0])
    first_two = both_rows(mine(first), theirs[1])
    second_two = both_rows(mine(second), theirs[2])
    grad = reduce_chips(grads)
    updated = adam_update(master_two, first_two, second_two, grad)

    new_pieces = gather_chips(updated[0].astype(jnp.bfloat16))
    updated = jnp.stack(updated)
    own_part = lax.dynamic_slice_in_dim(updated, core * local_rows, local_rows, 2)
    other_part = lax.dynamic_slice_in_dim(updated, (1 - core) * local_rows, local_rows, 2)
    from_other = hop(other_part, CORE)
    state = jnp.where(
        core == 0, jnp.stack([own_part, from_other], axis=1), jnp.stack([from_other, own_part], axis=1)
    )
    own_out, other_out, matches = forward(new_slots, new_pieces, new_rows, other_y)
    new_outputs = jnp.where(matches[0] == 1, own_out, hop(other_out, CORE))
    return (state[0], state[1], state[2], new_outputs[None])


def hidden_terms(tokens, cotangent, weights, live):
    positions = jnp.arange(tokens.shape[0], dtype=jnp.int32)
    cotangent = jnp.where((positions < live)[:, None], cotangent, jnp.zeros_like(cotangent))
    gate_pre = jnp.dot(tokens, weights[0], preferred_element_type=jnp.float32)
    up_pre = jnp.dot(tokens, weights[1], preferred_element_type=jnp.float32)
    gate_sig = jax.nn.sigmoid(gate_pre)
    gate_act = gate_pre * gate_sig
    hidden = (gate_act * up_pre).astype(jnp.bfloat16)
    grad_down = lax.dot_general(
        cotangent, hidden, (((0,), (0,)), ((), ())), preferred_element_type=jnp.float32
    )
    grad_hidden = jnp.dot(cotangent, weights[2], preferred_element_type=jnp.float32)
    grad_up_pre = (grad_hidden * gate_act).astype(jnp.bfloat16)
    grad_gate_pre = (grad_hidden * up_pre * gate_sig * (1.0 + gate_pre * (1.0 - gate_sig))).astype(
        jnp.bfloat16
    )
    grad_gate = lax.dot_general(
        tokens, grad_gate_pre, (((0,), (0,)), ((), ())), preferred_element_type=jnp.float32
    )
    grad_up = lax.dot_general(
        tokens, grad_up_pre, (((0,), (0,)), ((), ())), preferred_element_type=jnp.float32
    )
    return jnp.stack([grad_gate, grad_up, grad_down])


def expert_forward(tokens, weights):
    gate_pre = jnp.dot(tokens, weights[0], preferred_element_type=jnp.float32)
    up_pre = jnp.dot(tokens, weights[1], preferred_element_type=jnp.float32)
    activation = (jax.nn.silu(gate_pre) * up_pre).astype(jnp.bfloat16)
    result = lax.dot_general(
        activation, weights[2], (((1,), (1,)), ((), ())), preferred_element_type=jnp.float32
    )
    return result.astype(jnp.bfloat16)


def halving(buffer, levels, me_index):
    for step in range(levels):
        count = buffer.shape[2]
        halves = buffer.reshape(buffer.shape[:2] + (count // 2, 2) + buffer.shape[3:])
        own_bit = me_index >> step & 1
        keeping = lax.dynamic_index_in_dim(halves, own_bit, 3, keepdims=False)
        sending = lax.dynamic_index_in_dim(halves, 1 - own_bit, 3, keepdims=False)
        buffer = keeping + hop(sending, 1 << step)
    return buffer


def any_shape(master, first, second, old_rows, old_cotangent, new_rows, old_slots, new_slots, live):
    blocks, kinds, local_rows, block_width = master.shape
    devices = lax.axis_size("dev")
    me_index = lax.axis_index("dev")
    own_old = lax.dynamic_index_in_dim(old_slots, me_index, 0, keepdims=False)
    own_new = lax.dynamic_index_in_dim(new_slots, me_index, 0, keepdims=False)
    every_block = lax.all_gather(master.astype(jnp.bfloat16), "dev", axis=2, tiled=True)
    weights = lax.dynamic_index_in_dim(every_block, own_old, 0, keepdims=False)
    slot_grad = hidden_terms(old_rows, old_cotangent, weights, live[0])
    block_ids = jnp.arange(blocks, dtype=jnp.int32)[:, None, None, None, None]
    dense = slot_grad.reshape(kinds, devices, local_rows, block_width)
    buffer = jnp.where(block_ids == own_old, dense[None], jnp.zeros((), jnp.float32))
    buffer = halving(buffer, devices.bit_length() - 1, me_index)
    grad = buffer.reshape(master.shape)
    new_master, new_first, new_second = adam_update(master, first, second, grad)
    updated_blocks = lax.all_gather(new_master.astype(jnp.bfloat16), "dev", axis=2, tiled=True)
    new_weights = lax.dynamic_index_in_dim(updated_blocks, own_new, 0, keepdims=False)
    return (new_master, new_first, new_second, expert_forward(new_rows, new_weights)[None])


def on_device(
    master,
    first_moment,
    second_moment,
    old_rows,
    old_cotangent,
    new_rows,
    old_slots,
    new_slots,
    live_rows,
):
    blocks, kinds, local_rows, units = master.shape
    devices = lax.axis_size("dev")
    whole_tiles = local_rows % 16 == 0 and units % 128 == 0 and old_rows.shape[1] % 128 == 0
    form = block_a_core if blocks == 2 and devices % (2 * Z_UNIT) == 0 and whole_tiles else any_shape
    return form(
        master,
        first_moment,
        second_moment,
        old_rows[0],
        old_cotangent[0],
        new_rows[0],
        old_slots,
        new_slots,
        live_rows,
    )


def solution(mesh):
    return jax.shard_map(
        on_device,
        mesh=mesh,
        in_specs=(
            P(None, None, "dev", None),
            P(None, None, "dev", None),
            P(None, None, "dev", None),
            P("dev", None, None),
            P("dev", None, None),
            P("dev", None, None),
            P(),
            P(),
            P("dev"),
        ),
        out_specs=(
            P(None, None, "dev", None),
            P(None, None, "dev", None),
            P(None, None, "dev", None),
            P("dev", None, None),
        ),
        check_vma=False,
    )
```

```python
import functools

import jax
import jax.numpy as jnp
from jax import lax
from jax.experimental import pallas as pl
from jax.experimental.pallas import tpu as pltpu
from jax.sharding import PartitionSpec as P

beta_one = 0.9
beta_two = 0.95
corr_one = 0.9999734386011124
corr_two = 0.994079470779666
adam_eps = 1e-08
learn_rate = 0.003
decay_rate = 0.1

CORE, X_STEP, Y_STEP, Z_UNIT = 1, 2, 4, 8
VMEM_LIMIT = 16 * 1024 * 1024


def hop(block, mask):
    count = lax.axis_size("dev")
    return lax.ppermute(block, "dev", [(low, low ^ mask) for low in range(count)])


def adam_update(master, first, second, grad):
    first_new = beta_one * first + (1.0 - beta_one) * grad
    second_new = beta_two * second + (1.0 - beta_two) * grad * grad
    direction = first_new / corr_one / (jnp.sqrt(second_new / corr_two) + adam_eps)
    master_new = master - learn_rate * (direction + decay_rate * master)
    return (master_new, first_new, second_new)


def place_pieces(chip, pieces, weights):
    rows = pieces[0].shape[1]
    for j, piece in enumerate(pieces):
        start = pl.multiple_of(lax.bitwise_xor(chip, j) * rows, rows)
        weights[:, pl.ds(start, rows), :] = piece[...]


def transpose_kernel(own_x, other_x, own_c, other_c, x_turned, c_turned):
    chip = lax.axis_index("dev") // 2
    tokens, width = own_x.shape
    rows = 2 * width // lax.axis_size("dev")
    lanes = max(128, rows)
    for out, pair in ((x_turned, (own_x, other_x)), (c_turned, (own_c, other_c))):
        for part, ref in enumerate(pair):
            for at in range(0, width, lanes):
                turned = ref[:, at : at + lanes].T
                for low in range(0, lanes, rows):
                    j = lax.bitwise_xor(chip, (at + low) // rows)
                    start = pl.multiple_of(j * rows, rows)
                    out[pl.ds(start, rows), part * tokens : (part + 1) * tokens] = turned[low : low + rows]


def places(outs):
    found = []
    for zj in range(len(outs) // 3):
        own, later, pair = outs[3 * zj : 3 * zj + 3]
        by_x, by_y = ((pair, (1,)), (later, ())) if zj % 2 else ((later, ()), (pair, (1,)))
        found += [(own, ()), by_x, by_y, (pair, (0,))]
    return found


def gradient_rows(first_row, products, outs):
    outs = places(outs)
    rows = outs[0][0].shape[1]
    width = len(outs) * rows
    tall = min(width, 256)
    for at in range(0, width, tall):
        for kind, (left, right) in enumerate(products):
            product = jnp.dot(
                left[first_row + at : first_row + at + tall], right[...], preferred_element_type=jnp.float32
            ).astype(jnp.bfloat16)
            for low in range(0, tall, rows):
                out, before = outs[(at + low) // rows]
                out[before + (kind,)] = product[low : low + rows]


def backward_kernel(count, slots, own_live, other_live, *refs):
    pieces = refs[:count]
    own_x, other_x, own_c, other_c, x_turned, c_turned = refs[count : count + 6]
    outs = refs[count + 6 : -4]
    gate_grad, up_grad, hidden_all, weights = refs[-4:]
    me_index = lax.axis_index("dev")
    core = me_index & CORE
    place_pieces(me_index // 2, pieces, weights)
    tokens = own_x.shape[0]
    sides = ((own_x, own_c, me_index, own_live), (other_x, other_c, me_index ^ CORE, other_live))
    for part, (x_ref, c_ref, slot, live) in enumerate(sides):
        span = slice(part * tokens, (part + 1) * tokens)
        gate_pre = jnp.dot(x_ref[...], weights[0], preferred_element_type=jnp.float32)
        up_pre = jnp.dot(x_ref[...], weights[1], preferred_element_type=jnp.float32)
        grad_hidden = jnp.dot(c_ref[...], weights[2], preferred_element_type=jnp.float32)
        gate_sig = jax.nn.sigmoid(gate_pre)
        gate_act = gate_pre * gate_sig
        alive = jnp.where(slots[slot] == core, live[0], 0)
        keep = lax.broadcasted_iota(jnp.int32, gate_pre.shape, 0) < alive
        grad_up = grad_hidden * gate_act
        grad_gate = grad_hidden * up_pre * gate_sig * (1.0 + gate_pre * (1.0 - gate_sig))
        hidden_all[span] = jnp.where(keep, gate_act * up_pre, 0.0).astype(jnp.bfloat16)
        up_grad[span] = jnp.where(keep, grad_up, 0.0).astype(jnp.bfloat16)
        gate_grad[span] = jnp.where(keep, grad_gate, 0.0).astype(jnp.bfloat16)
    products = ((x_turned, gate_grad), (x_turned, up_grad), (c_turned, hidden_all))
    gradient_rows(0, products, outs)


def expert_rows(y_ref, weights, out_ref):
    gate_pre = jnp.dot(y_ref[...], weights[0], preferred_element_type=jnp.float32)
    up_pre = jnp.dot(y_ref[...], weights[1], preferred_element_type=jnp.float32)
    act = (gate_pre * jax.nn.sigmoid(gate_pre) * up_pre).astype(jnp.bfloat16)
    result = lax.dot_general(act, weights[2], (((1,), (1,)), ((), ())), preferred_element_type=jnp.float32)
    out_ref[...] = result.astype(jnp.bfloat16)


def other_kernel(count, *refs):
    pieces = refs[:count]
    other_y, other_out, weights = refs[count:]
    place_pieces(lax.axis_index("dev") // 2, pieces, weights)
    expert_rows(other_y, weights, other_out)


def own_kernel(slots, weights, own_y, own_out, matches):
    me_index = lax.axis_index("dev")
    matches[0] = jnp.where(slots[me_index] == (me_index & CORE), 1, 0)
    expert_rows(own_y, weights, own_out)


VMEM = pl.BlockSpec(memory_space=pltpu.VMEM)
SMEM = pl.BlockSpec(memory_space=pltpu.SMEM)


def params():
    return pltpu.CompilerParams(vmem_limit_bytes=VMEM_LIMIT)


def transposed(own_x, other_x, own_c, other_c):
    tokens, width = own_x.shape
    return pl.pallas_call(
        transpose_kernel,
        out_shape=[jax.ShapeDtypeStruct((width, 2 * tokens), own_x.dtype)] * 2,
        in_specs=[VMEM] * 4,
        out_specs=[VMEM] * 2,
        compiler_params=params(),
        cost_estimate=pl.CostEstimate(flops=0, bytes_accessed=16 * tokens * width, transcendentals=0),
        name="transpose_rows",
    )(own_x, other_x, own_c, other_c)


def backward(slots, own_live, other_live, pieces, own_x, other_x, own_c, other_c, x_turned, c_turned):
    count = len(pieces)
    kinds, rows, units = pieces[0].shape
    tokens, width = own_x.shape
    one = jax.ShapeDtypeStruct((kinds, rows, units), jnp.bfloat16)
    two = jax.ShapeDtypeStruct((2, kinds, rows, units), jnp.bfloat16)
    return pl.pallas_call(
        functools.partial(backward_kernel, count),
        out_shape=[one, one, two] * (count // 4),
        in_specs=[SMEM] * 3 + [VMEM] * (count + 6),
        out_specs=[VMEM] * (3 * count // 4),
        scratch_shapes=[
            pltpu.VMEM((2 * tokens, units), jnp.bfloat16),
            pltpu.VMEM((2 * tokens, units), jnp.bfloat16),
            pltpu.VMEM((2 * tokens, units), jnp.bfloat16),
            pltpu.VMEM((kinds, width, units), jnp.bfloat16),
        ],
        compiler_params=params(),
        cost_estimate=pl.CostEstimate(
            flops=24 * tokens * width * units,
            bytes_accessed=16 * tokens * width + 12 * width * units,
            transcendentals=2 * tokens * units,
        ),
        name="slot_gradients",
    )(slots, own_live, other_live, *pieces, own_x, other_x, own_c, other_c, x_turned, c_turned)


def forward(slots, pieces, own_y, other_y):
    count = len(pieces)
    kinds, rows, units = pieces[0].shape
    tokens, width = own_y.shape
    one = jax.ShapeDtypeStruct((tokens, width), jnp.bfloat16)
    cost = pl.CostEstimate(
        flops=6 * tokens * width * units,
        bytes_accessed=4 * tokens * width + 6 * width * units,
        transcendentals=tokens * units,
    )
    other_out, weights = pl.pallas_call(
        functools.partial(other_kernel, count),
        out_shape=[one, jax.ShapeDtypeStruct((kinds, width, units), jnp.bfloat16)],
        in_specs=[VMEM] * (count + 1),
        out_specs=[VMEM] * 2,
        compiler_params=params(),
        cost_estimate=cost,
        name="other_outputs",
    )(*pieces, other_y)
    own_out, matches = pl.pallas_call(
        own_kernel,
        out_shape=[one, jax.ShapeDtypeStruct((1,), jnp.int32)],
        in_specs=[SMEM, VMEM, VMEM],
        out_specs=[VMEM, SMEM],
        compiler_params=params(),
        cost_estimate=cost,
        name="own_outputs",
    )(slots, weights, own_y)
    return own_out, other_out, matches


def after(value, *others):
    return lax.optimization_barrier((value,) + others)[0]


def gather_chips(piece):
    depth = lax.axis_size("dev") // Z_UNIT
    column = [piece] + [None] * (depth - 1)
    for top in reversed([1 << bit for bit in range(depth.bit_length() - 1)]):
        column[top] = hop(piece, top * Z_UNIT)
    along_x, along_y, across = [None] * depth, [None] * depth, [None] * depth
    along_x[0] = hop(piece, X_STEP)
    along_y[0] = hop(piece, Y_STEP)
    along_x[1] = hop(column[1], X_STEP)
    for zj in range(2, depth):
        top = 1 << zj.bit_length() - 1
        if zj != top:
            column[zj] = hop(column[top], (zj - top) * Z_UNIT)
    along_y[1] = hop(after(column[1], along_x[0]), Y_STEP)
    for zj in range(2, depth, 2):
        along_x[zj] = hop(after(column[zj], along_x[zj - 2], along_y[zj - 2]), X_STEP)
        across[zj - 2] = hop(after(along_x[zj - 2], along_y[zj - 2]), Y_STEP)
        along_x[zj + 1] = hop(after(column[zj + 1], along_x[zj - 1]), X_STEP)
        along_y[zj + 1] = hop(after(column[zj + 1], along_x[zj - 1]), Y_STEP)
        along_y[zj] = hop(after(column[zj], along_y[zj - 1]), Y_STEP)
        across[zj - 1] = hop(after(along_y[zj - 1], along_x[zj]), X_STEP)
    across[-2] = hop(after(along_x[-2], along_x[-1]), Y_STEP)
    across[-1] = hop(along_y[-1], X_STEP)
    return [part for group in zip(column, along_x, along_y, across) for part in group]


def add_all(first, *others):
    total = first.astype(jnp.float32)
    for other in others:
        total = total + other.astype(jnp.float32)
    return total


def reduce_chips(pieces):
    depth = lax.axis_size("dev") // Z_UNIT
    column = [[pieces[3 * zj]] for zj in range(depth)]
    arrived, crossed, risen = (), (), ()
    for upper in reversed(range(1, depth, 2)):
        up_y, pair_x = pieces[3 * upper + 1 : 3 * upper + 3]
        below_x, pair_y = pieces[3 * upper - 2 : 3 * upper]
        got_x = hop(pair_x, X_STEP)
        got_y = hop(after(pair_y, *arrived), Y_STEP)
        up_y = add_all(up_y, got_x[0]).astype(jnp.bfloat16)
        column[upper] += [got_x[1], hop(after(up_y, *crossed), Y_STEP)]
        below_x = add_all(below_x, got_y[0]).astype(jnp.bfloat16)
        column[upper - 1] += [got_y[1], hop(after(below_x, *risen), X_STEP)]
        arrived, crossed, risen = (got_x,), (column[upper][-1],), ()
        for zj in (upper, upper - 1):
            top = 1 << zj.bit_length() - 1 if zj else 0
            low = zj - top
            if zj:
                part = add_all(*column[zj]).astype(jnp.bfloat16)
                column[top if low else 0].append(hop(part, (low or top) * Z_UNIT))
                risen = risen or (column[top if low else 0][-1],)
    return add_all(*column[0])


def block_a_core(master, first, second, old_rows, old_cotangent, new_rows, old_slots, new_slots, live):
    local_rows = master.shape[2]
    core = lax.axis_index("dev") & CORE

    def mine(state):
        return lax.dynamic_index_in_dim(state, core, 0, keepdims=False)

    def partners(state):
        return lax.dynamic_index_in_dim(state, 1 - core, 0, keepdims=False)

    def both_rows(own, other):
        return jnp.where(
            core == 0, jnp.concatenate([own, other], axis=-2), jnp.concatenate([other, own], axis=-2)
        )

    other_x = hop(old_rows, CORE)
    other_c = hop(old_cotangent, CORE)
    theirs = hop(jnp.stack([partners(master), partners(first), partners(second)]), CORE)
    other_y = hop(new_rows, CORE)
    other_live = hop(live, CORE)
    theirs, other_x, other_c, other_y, other_live = lax.optimization_barrier(
        (theirs, other_x, other_c, other_y, other_live)
    )
    x_turned, c_turned = transposed(old_rows, other_x, old_cotangent, other_c)
    master_two = both_rows(mine(master), theirs[0])
    pieces = gather_chips(master_two.astype(jnp.bfloat16))
    grads = backward(
        old_slots,
        live,
        other_live,
        pieces,
        old_rows,
        other_x,
        old_cotangent,
        other_c,
        x_turned,
        c_turned,
    )
    theirs = after(theirs, grads[0])
    first_two = both_rows(mine(first), theirs[1])
    second_two = both_rows(mine(second), theirs[2])
    grad = reduce_chips(grads)
    updated = adam_update(master_two, first_two, second_two, grad)

    new_pieces = gather_chips(updated[0].astype(jnp.bfloat16))
    updated = jnp.stack(updated)
    own_part = lax.dynamic_slice_in_dim(updated, core * local_rows, local_rows, 2)
    other_part = lax.dynamic_slice_in_dim(updated, (1 - core) * local_rows, local_rows, 2)
    own_out, other_out, matches = forward(new_slots, new_pieces, new_rows, other_y)
    from_other = hop(after(other_part, other_out), CORE)
    state = jnp.where(
        core == 0, jnp.stack([own_part, from_other], axis=1), jnp.stack([from_other, own_part], axis=1)
    )
    new_outputs = jnp.where(matches[0] == 1, own_out, hop(other_out, CORE))
    return (state[0], state[1], state[2], new_outputs[None])


def hidden_terms(tokens, cotangent, weights, live):
    positions = jnp.arange(tokens.shape[0], dtype=jnp.int32)
    cotangent = jnp.where((positions < live)[:, None], cotangent, jnp.zeros_like(cotangent))
    gate_pre = jnp.dot(tokens, weights[0], preferred_element_type=jnp.float32)
    up_pre = jnp.dot(tokens, weights[1], preferred_element_type=jnp.float32)
    gate_sig = jax.nn.sigmoid(gate_pre)
    gate_act = gate_pre * gate_sig
    hidden = (gate_act * up_pre).astype(jnp.bfloat16)
    grad_down = lax.dot_general(
        cotangent, hidden, (((0,), (0,)), ((), ())), preferred_element_type=jnp.float32
    )
    grad_hidden = jnp.dot(cotangent, weights[2], preferred_element_type=jnp.float32)
    grad_up_pre = (grad_hidden * gate_act).astype(jnp.bfloat16)
    grad_gate_pre = (grad_hidden * up_pre * gate_sig * (1.0 + gate_pre * (1.0 - gate_sig))).astype(
        jnp.bfloat16
    )
    grad_gate = lax.dot_general(
        tokens, grad_gate_pre, (((0,), (0,)), ((), ())), preferred_element_type=jnp.float32
    )
    grad_up = lax.dot_general(
        tokens, grad_up_pre, (((0,), (0,)), ((), ())), preferred_element_type=jnp.float32
    )
    return jnp.stack([grad_gate, grad_up, grad_down])


def expert_forward(tokens, weights):
    gate_pre = jnp.dot(tokens, weights[0], preferred_element_type=jnp.float32)
    up_pre = jnp.dot(tokens, weights[1], preferred_element_type=jnp.float32)
    activation = (jax.nn.silu(gate_pre) * up_pre).astype(jnp.bfloat16)
    result = lax.dot_general(
        activation, weights[2], (((1,), (1,)), ((), ())), preferred_element_type=jnp.float32
    )
    return result.astype(jnp.bfloat16)


def halving(buffer, levels, me_index):
    for step in range(levels):
        count = buffer.shape[2]
        halves = buffer.reshape(buffer.shape[:2] + (count // 2, 2) + buffer.shape[3:])
        own_bit = me_index >> step & 1
        keeping = lax.dynamic_index_in_dim(halves, own_bit, 3, keepdims=False)
        sending = lax.dynamic_index_in_dim(halves, 1 - own_bit, 3, keepdims=False)
        buffer = keeping + hop(sending, 1 << step)
    return buffer


def any_shape(master, first, second, old_rows, old_cotangent, new_rows, old_slots, new_slots, live):
    blocks, kinds, local_rows, block_width = master.shape
    devices = lax.axis_size("dev")
    me_index = lax.axis_index("dev")
    own_old = lax.dynamic_index_in_dim(old_slots, me_index, 0, keepdims=False)
    own_new = lax.dynamic_index_in_dim(new_slots, me_index, 0, keepdims=False)
    every_block = lax.all_gather(master.astype(jnp.bfloat16), "dev", axis=2, tiled=True)
    weights = lax.dynamic_index_in_dim(every_block, own_old, 0, keepdims=False)
    slot_grad = hidden_terms(old_rows, old_cotangent, weights, live[0])
    block_ids = jnp.arange(blocks, dtype=jnp.int32)[:, None, None, None, None]
    dense = slot_grad.reshape(kinds, devices, local_rows, block_width)
    buffer = jnp.where(block_ids == own_old, dense[None], jnp.zeros((), jnp.float32))
    buffer = halving(buffer, devices.bit_length() - 1, me_index)
    grad = buffer.reshape(master.shape)
    new_master, new_first, new_second = adam_update(master, first, second, grad)
    updated_blocks = lax.all_gather(new_master.astype(jnp.bfloat16), "dev", axis=2, tiled=True)
    new_weights = lax.dynamic_index_in_dim(updated_blocks, own_new, 0, keepdims=False)
    return (new_master, new_first, new_second, expert_forward(new_rows, new_weights)[None])


def on_device(
    master,
    first_moment,
    second_moment,
    old_rows,
    old_cotangent,
    new_rows,
    old_slots,
    new_slots,
    live_rows,
):
    blocks, kinds, local_rows, units = master.shape
    devices = lax.axis_size("dev")
    whole_tiles = local_rows % 16 == 0 and units % 128 == 0 and old_rows.shape[1] % 128 == 0
    form = block_a_core if blocks == 2 and devices % (2 * Z_UNIT) == 0 and whole_tiles else any_shape
    return form(
        master,
        first_moment,
        second_moment,
        old_rows[0],
        old_cotangent[0],
        new_rows[0],
        old_slots,
        new_slots,
        live_rows,
    )


def solution(mesh):
    return jax.shard_map(
        on_device,
        mesh=mesh,
        in_specs=(
            P(None, None, "dev", None),
            P(None, None, "dev", None),
            P(None, None, "dev", None),
            P("dev", None, None),
            P("dev", None, None),
            P("dev", None, None),
            P(),
            P(),
            P("dev"),
        ),
        out_specs=(
            P(None, None, "dev", None),
            P(None, None, "dev", None),
            P(None, None, "dev", None),
            P("dev", None, None),
        ),
        check_vma=False,
    )
```

```python
import functools

import jax
import jax.numpy as jnp
from jax import lax
from jax.experimental import pallas as pl
from jax.experimental.pallas import tpu as pltpu
from jax.sharding import PartitionSpec as P

beta_one = 0.9
beta_two = 0.95
corr_one = 0.9999734386011124
corr_two = 0.994079470779666
adam_eps = 1e-08
learn_rate = 0.003
decay_rate = 0.1

CORE, X_STEP, Y_STEP, Z_UNIT = 1, 2, 4, 8
VMEM_LIMIT = 16 * 1024 * 1024


def hop(block, mask):
    count = lax.axis_size("dev")
    return lax.ppermute(block, "dev", [(low, low ^ mask) for low in range(count)])


def adam_update(master, first, second, grad):
    first_new = beta_one * first + (1.0 - beta_one) * grad
    second_new = beta_two * second + (1.0 - beta_two) * grad * grad
    direction = first_new / corr_one / (jnp.sqrt(second_new / corr_two) + adam_eps)
    master_new = master - learn_rate * (direction + decay_rate * master)
    return (master_new, first_new, second_new)


def place_pieces(chip, pieces, weights):
    rows = pieces[0].shape[1]
    for j, piece in enumerate(pieces):
        start = pl.multiple_of(lax.bitwise_xor(chip, j) * rows, rows)
        weights[:, pl.ds(start, rows), :] = piece[...]


def transpose_kernel(slots, own_x, other_x, own_c, other_c, x_turned, c_turned, matches):
    me_index = lax.axis_index("dev")
    matches[0] = jnp.where(slots[me_index] == (me_index & CORE), 1, 0)
    chip = me_index // 2
    tokens, width = own_x.shape
    rows = 2 * width // lax.axis_size("dev")
    lanes = max(128, rows)
    for out, pair in ((x_turned, (own_x, other_x)), (c_turned, (own_c, other_c))):
        for part, ref in enumerate(pair):
            for at in range(0, width, lanes):
                turned = ref[:, at : at + lanes].T
                for low in range(0, lanes, rows):
                    j = lax.bitwise_xor(chip, (at + low) // rows)
                    start = pl.multiple_of(j * rows, rows)
                    out[pl.ds(start, rows), part * tokens : (part + 1) * tokens] = turned[low : low + rows]


def places(outs):
    found = []
    for zj in range(len(outs) // 3):
        own, later, pair = outs[3 * zj : 3 * zj + 3]
        by_x, by_y = ((pair, (1,)), (later, ())) if zj % 2 else ((later, ()), (pair, (1,)))
        found += [(own, ()), by_x, by_y, (pair, (0,))]
    return found


def gradient_rows(first_row, products, outs):
    outs = places(outs)
    rows = outs[0][0].shape[1]
    width = len(outs) * rows
    tall = min(width, 256)
    for at in range(0, width, tall):
        for kind, (left, right) in enumerate(products):
            product = jnp.dot(
                left[first_row + at : first_row + at + tall], right[...], preferred_element_type=jnp.float32
            ).astype(jnp.bfloat16)
            for low in range(0, tall, rows):
                out, before = outs[(at + low) // rows]
                out[before + (kind,)] = product[low : low + rows]


def backward_kernel(count, slots, own_live, other_live, *refs):
    pieces = refs[:count]
    own_x, other_x, own_c, other_c, x_turned, c_turned = refs[count : count + 6]
    outs = refs[count + 6 : -4]
    gate_grad, up_grad, hidden_all, weights = refs[-4:]
    me_index = lax.axis_index("dev")
    core = me_index & CORE
    place_pieces(me_index // 2, pieces, weights)
    tokens = own_x.shape[0]
    sides = ((own_x, own_c, me_index, own_live), (other_x, other_c, me_index ^ CORE, other_live))
    for part, (x_ref, c_ref, slot, live) in enumerate(sides):
        span = slice(part * tokens, (part + 1) * tokens)
        gate_pre = jnp.dot(x_ref[...], weights[0], preferred_element_type=jnp.float32)
        up_pre = jnp.dot(x_ref[...], weights[1], preferred_element_type=jnp.float32)
        grad_hidden = jnp.dot(c_ref[...], weights[2], preferred_element_type=jnp.float32)
        gate_sig = jax.nn.sigmoid(gate_pre)
        gate_act = gate_pre * gate_sig
        alive = jnp.where(slots[slot] == core, live[0], 0)
        keep = lax.broadcasted_iota(jnp.int32, gate_pre.shape, 0) < alive
        grad_up = grad_hidden * gate_act
        grad_gate = grad_hidden * up_pre * gate_sig * (1.0 + gate_pre * (1.0 - gate_sig))
        hidden_all[span] = jnp.where(keep, gate_act * up_pre, 0.0).astype(jnp.bfloat16)
        up_grad[span] = jnp.where(keep, grad_up, 0.0).astype(jnp.bfloat16)
        gate_grad[span] = jnp.where(keep, grad_gate, 0.0).astype(jnp.bfloat16)
    products = ((x_turned, gate_grad), (x_turned, up_grad), (c_turned, hidden_all))
    gradient_rows(0, products, outs)


def expert_rows(y_ref, weights, out_ref):
    gate_pre = jnp.dot(y_ref[...], weights[0], preferred_element_type=jnp.float32)
    up_pre = jnp.dot(y_ref[...], weights[1], preferred_element_type=jnp.float32)
    act = (gate_pre * jax.nn.sigmoid(gate_pre) * up_pre).astype(jnp.bfloat16)
    result = lax.dot_general(act, weights[2], (((1,), (1,)), ((), ())), preferred_element_type=jnp.float32)
    out_ref[...] = result.astype(jnp.bfloat16)


def other_kernel(count, *refs):
    pieces = refs[:count]
    other_y, own_y, other_out, weights = refs[count:]
    place_pieces(lax.axis_index("dev") // 2, pieces, weights)
    expert_rows(other_y, weights, other_out)


def own_kernel(weights, own_y, own_out):
    expert_rows(own_y, weights, own_out)


VMEM = pl.BlockSpec(memory_space=pltpu.VMEM)
SMEM = pl.BlockSpec(memory_space=pltpu.SMEM)


def params():
    return pltpu.CompilerParams(vmem_limit_bytes=VMEM_LIMIT)


def transposed(slots, own_x, other_x, own_c, other_c):
    tokens, width = own_x.shape
    return pl.pallas_call(
        transpose_kernel,
        out_shape=[jax.ShapeDtypeStruct((width, 2 * tokens), own_x.dtype)] * 2
        + [jax.ShapeDtypeStruct((1,), jnp.int32)],
        in_specs=[SMEM] + [VMEM] * 4,
        out_specs=[VMEM, VMEM, SMEM],
        compiler_params=params(),
        cost_estimate=pl.CostEstimate(flops=0, bytes_accessed=16 * tokens * width, transcendentals=0),
        name="transpose_rows",
    )(slots, own_x, other_x, own_c, other_c)


def backward(slots, own_live, other_live, pieces, own_x, other_x, own_c, other_c, x_turned, c_turned):
    count = len(pieces)
    kinds, rows, units = pieces[0].shape
    tokens, width = own_x.shape
    one = jax.ShapeDtypeStruct((kinds, rows, units), jnp.bfloat16)
    two = jax.ShapeDtypeStruct((2, kinds, rows, units), jnp.bfloat16)
    return pl.pallas_call(
        functools.partial(backward_kernel, count),
        out_shape=[one, one, two] * (count // 4),
        in_specs=[SMEM] * 3 + [VMEM] * (count + 6),
        out_specs=[VMEM] * (3 * count // 4),
        scratch_shapes=[
            pltpu.VMEM((2 * tokens, units), jnp.bfloat16),
            pltpu.VMEM((2 * tokens, units), jnp.bfloat16),
            pltpu.VMEM((2 * tokens, units), jnp.bfloat16),
            pltpu.VMEM((kinds, width, units), jnp.bfloat16),
        ],
        compiler_params=params(),
        cost_estimate=pl.CostEstimate(
            flops=24 * tokens * width * units,
            bytes_accessed=16 * tokens * width + 12 * width * units,
            transcendentals=2 * tokens * units,
        ),
        name="slot_gradients",
    )(slots, own_live, other_live, *pieces, own_x, other_x, own_c, other_c, x_turned, c_turned)


def forward(pieces, own_y, other_y):
    count = len(pieces)
    kinds, rows, units = pieces[0].shape
    tokens, width = own_y.shape
    one = jax.ShapeDtypeStruct((tokens, width), jnp.bfloat16)
    cost = pl.CostEstimate(
        flops=6 * tokens * width * units,
        bytes_accessed=4 * tokens * width + 6 * width * units,
        transcendentals=tokens * units,
    )
    other_out, weights = pl.pallas_call(
        functools.partial(other_kernel, count),
        out_shape=[one, jax.ShapeDtypeStruct((kinds, width, units), jnp.bfloat16)],
        in_specs=[VMEM] * (count + 2),
        out_specs=[VMEM] * 2,
        compiler_params=params(),
        cost_estimate=cost,
        name="other_outputs",
    )(*pieces, other_y, own_y)
    own_out = pl.pallas_call(
        own_kernel,
        out_shape=one,
        in_specs=[VMEM, VMEM],
        out_specs=VMEM,
        compiler_params=params(),
        cost_estimate=cost,
        name="own_outputs",
    )(weights, own_y)
    return own_out, other_out


def after(value, *others):
    return lax.optimization_barrier((value,) + others)[0]


def gather_chips(piece):
    depth = lax.axis_size("dev") // Z_UNIT
    column = [piece] + [None] * (depth - 1)
    for top in reversed([1 << bit for bit in range(depth.bit_length() - 1)]):
        column[top] = hop(piece, top * Z_UNIT)
    along_x, along_y, across = [None] * depth, [None] * depth, [None] * depth
    along_x[0] = hop(piece, X_STEP)
    along_y[0] = hop(piece, Y_STEP)
    along_x[1] = hop(column[1], X_STEP)
    for zj in range(2, depth):
        top = 1 << zj.bit_length() - 1
        if zj != top:
            column[zj] = hop(column[top], (zj - top) * Z_UNIT)
    along_y[1] = hop(after(column[1], along_x[0]), Y_STEP)
    for zj in range(2, depth, 2):
        along_x[zj] = hop(after(column[zj], along_x[zj - 2], along_y[zj - 2]), X_STEP)
        across[zj - 2] = hop(after(along_x[zj - 2], along_y[zj - 2]), Y_STEP)
        along_x[zj + 1] = hop(after(column[zj + 1], along_x[zj - 1]), X_STEP)
        along_y[zj + 1] = hop(after(column[zj + 1], along_x[zj - 1]), Y_STEP)
        along_y[zj] = hop(after(column[zj], along_y[zj - 1]), Y_STEP)
        across[zj - 1] = hop(after(along_y[zj - 1], along_x[zj]), X_STEP)
    across[-2] = hop(after(along_x[-2], along_x[-1]), Y_STEP)
    across[-1] = hop(along_y[-1], X_STEP)
    return [part for group in zip(column, along_x, along_y, across) for part in group]


def add_all(first, *others):
    total = first.astype(jnp.float32)
    for other in others:
        total = total + other.astype(jnp.float32)
    return total


def reduce_chips(pieces):
    depth = lax.axis_size("dev") // Z_UNIT
    total, waiting, arrived, crossed = [], [], (), ()
    for upper in reversed(range(1, depth, 2)):
        own_up, up_y, pair_x = pieces[3 * upper : 3 * upper + 3]
        own_low, low_x, pair_y = pieces[3 * upper - 3 : 3 * upper]
        got_x = hop(pair_x, X_STEP)
        got_y = hop(after(pair_y, *arrived), Y_STEP)
        up_y = hop(after(add_all(up_y, got_x[0]).astype(jnp.bfloat16), *crossed), Y_STEP)
        low_x = hop(after(add_all(low_x, got_y[0]).astype(jnp.bfloat16), *crossed), X_STEP)
        arrived, crossed = (got_x,), (low_x,)
        low = [own_low, got_y[1], low_x]
        up = add_all(own_up, got_x[1], up_y).astype(jnp.bfloat16)
        if upper > 1:
            total.append(hop(add_all(*low).astype(jnp.bfloat16), (upper - 1) * Z_UNIT))
            waiting.append((up, upper * Z_UNIT))
        else:
            total += low
            total += [hop(after(part, got_y), mask) for part, mask in waiting]
            total.append(hop(up, Z_UNIT))
    return add_all(*total)


def block_a_core(master, first, second, old_rows, old_cotangent, new_rows, old_slots, new_slots, live):
    local_rows = master.shape[2]
    core = lax.axis_index("dev") & CORE

    def mine(state):
        return lax.dynamic_index_in_dim(state, core, 0, keepdims=False)

    def partners(state):
        return lax.dynamic_index_in_dim(state, 1 - core, 0, keepdims=False)

    def both_rows(own, other):
        return jnp.where(
            core == 0, jnp.concatenate([own, other], axis=-2), jnp.concatenate([other, own], axis=-2)
        )

    other_x = hop(old_rows, CORE)
    other_c = hop(old_cotangent, CORE)
    theirs = hop(jnp.stack([partners(master), partners(first), partners(second)]), CORE)
    other_y = hop(new_rows, CORE)
    other_live = hop(live, CORE)
    x_turned, c_turned, matches = transposed(new_slots, old_rows, other_x, old_cotangent, other_c)
    theirs, other_y, other_live, x_turned, c_turned = lax.optimization_barrier(
        (theirs, other_y, other_live, x_turned, c_turned)
    )
    master_two = both_rows(mine(master), theirs[0])
    pieces = gather_chips(master_two.astype(jnp.bfloat16))
    grads = backward(
        old_slots,
        live,
        other_live,
        pieces,
        old_rows,
        other_x,
        old_cotangent,
        other_c,
        x_turned,
        c_turned,
    )
    theirs = after(theirs, grads[0])
    first_two = both_rows(mine(first), theirs[1])
    second_two = both_rows(mine(second), theirs[2])
    grad = reduce_chips(grads)
    updated = adam_update(master_two, first_two, second_two, grad)

    new_pieces = gather_chips(updated[0].astype(jnp.bfloat16))
    updated = jnp.stack(updated)
    own_part = lax.dynamic_slice_in_dim(updated, core * local_rows, local_rows, 2)
    other_part = lax.dynamic_slice_in_dim(updated, (1 - core) * local_rows, local_rows, 2)
    own_out, other_out = forward(new_pieces, new_rows, other_y)
    from_other = hop(after(other_part, other_out), CORE)
    state = jnp.where(
        core == 0, jnp.stack([own_part, from_other], axis=1), jnp.stack([from_other, own_part], axis=1)
    )
    new_outputs = jnp.where(matches[0] == 1, own_out, hop(other_out, CORE))
    return (state[0], state[1], state[2], new_outputs[None])


def hidden_terms(tokens, cotangent, weights, live):
    positions = jnp.arange(tokens.shape[0], dtype=jnp.int32)
    cotangent = jnp.where((positions < live)[:, None], cotangent, jnp.zeros_like(cotangent))
    gate_pre = jnp.dot(tokens, weights[0], preferred_element_type=jnp.float32)
    up_pre = jnp.dot(tokens, weights[1], preferred_element_type=jnp.float32)
    gate_sig = jax.nn.sigmoid(gate_pre)
    gate_act = gate_pre * gate_sig
    hidden = (gate_act * up_pre).astype(jnp.bfloat16)
    grad_down = lax.dot_general(
        cotangent, hidden, (((0,), (0,)), ((), ())), preferred_element_type=jnp.float32
    )
    grad_hidden = jnp.dot(cotangent, weights[2], preferred_element_type=jnp.float32)
    grad_up_pre = (grad_hidden * gate_act).astype(jnp.bfloat16)
    grad_gate_pre = (grad_hidden * up_pre * gate_sig * (1.0 + gate_pre * (1.0 - gate_sig))).astype(
        jnp.bfloat16
    )
    grad_gate = lax.dot_general(
        tokens, grad_gate_pre, (((0,), (0,)), ((), ())), preferred_element_type=jnp.float32
    )
    grad_up = lax.dot_general(
        tokens, grad_up_pre, (((0,), (0,)), ((), ())), preferred_element_type=jnp.float32
    )
    return jnp.stack([grad_gate, grad_up, grad_down])


def expert_forward(tokens, weights):
    gate_pre = jnp.dot(tokens, weights[0], preferred_element_type=jnp.float32)
    up_pre = jnp.dot(tokens, weights[1], preferred_element_type=jnp.float32)
    activation = (jax.nn.silu(gate_pre) * up_pre).astype(jnp.bfloat16)
    result = lax.dot_general(
        activation, weights[2], (((1,), (1,)), ((), ())), preferred_element_type=jnp.float32
    )
    return result.astype(jnp.bfloat16)


def halving(buffer, levels, me_index):
    for step in range(levels):
        count = buffer.shape[2]
        halves = buffer.reshape(buffer.shape[:2] + (count // 2, 2) + buffer.shape[3:])
        own_bit = me_index >> step & 1
        keeping = lax.dynamic_index_in_dim(halves, own_bit, 3, keepdims=False)
        sending = lax.dynamic_index_in_dim(halves, 1 - own_bit, 3, keepdims=False)
        buffer = keeping + hop(sending, 1 << step)
    return buffer


def any_shape(master, first, second, old_rows, old_cotangent, new_rows, old_slots, new_slots, live):
    blocks, kinds, local_rows, block_width = master.shape
    devices = lax.axis_size("dev")
    me_index = lax.axis_index("dev")
    own_old = lax.dynamic_index_in_dim(old_slots, me_index, 0, keepdims=False)
    own_new = lax.dynamic_index_in_dim(new_slots, me_index, 0, keepdims=False)
    every_block = lax.all_gather(master.astype(jnp.bfloat16), "dev", axis=2, tiled=True)
    weights = lax.dynamic_index_in_dim(every_block, own_old, 0, keepdims=False)
    slot_grad = hidden_terms(old_rows, old_cotangent, weights, live[0])
    block_ids = jnp.arange(blocks, dtype=jnp.int32)[:, None, None, None, None]
    dense = slot_grad.reshape(kinds, devices, local_rows, block_width)
    buffer = jnp.where(block_ids == own_old, dense[None], jnp.zeros((), jnp.float32))
    buffer = halving(buffer, devices.bit_length() - 1, me_index)
    grad = buffer.reshape(master.shape)
    new_master, new_first, new_second = adam_update(master, first, second, grad)
    updated_blocks = lax.all_gather(new_master.astype(jnp.bfloat16), "dev", axis=2, tiled=True)
    new_weights = lax.dynamic_index_in_dim(updated_blocks, own_new, 0, keepdims=False)
    return (new_master, new_first, new_second, expert_forward(new_rows, new_weights)[None])


def on_device(
    master,
    first_moment,
    second_moment,
    old_rows,
    old_cotangent,
    new_rows,
    old_slots,
    new_slots,
    live_rows,
):
    blocks, kinds, local_rows, units = master.shape
    devices = lax.axis_size("dev")
    whole_tiles = local_rows % 16 == 0 and units % 128 == 0 and old_rows.shape[1] % 128 == 0
    form = block_a_core if blocks == 2 and devices % (2 * Z_UNIT) == 0 and whole_tiles else any_shape
    return form(
        master,
        first_moment,
        second_moment,
        old_rows[0],
        old_cotangent[0],
        new_rows[0],
        old_slots,
        new_slots,
        live_rows,
    )


def solution(mesh):
    return jax.shard_map(
        on_device,
        mesh=mesh,
        in_specs=(
            P(None, None, "dev", None),
            P(None, None, "dev", None),
            P(None, None, "dev", None),
            P("dev", None, None),
            P("dev", None, None),
            P("dev", None, None),
            P(),
            P(),
            P("dev"),
        ),
        out_specs=(
            P(None, None, "dev", None),
            P(None, None, "dev", None),
            P(None, None, "dev", None),
            P("dev", None, None),
        ),
        check_vma=False,
    )
```

```python
import functools

import jax
import jax.numpy as jnp
from jax import lax
from jax.experimental import pallas as pl
from jax.experimental.pallas import tpu as pltpu
from jax.sharding import PartitionSpec as P

beta_one = 0.9
beta_two = 0.95
corr_one = 0.9999734386011124
corr_two = 0.994079470779666
adam_eps = 1e-08
learn_rate = 0.003
decay_rate = 0.1

CORE, X_STEP, Y_STEP, Z_UNIT = 1, 2, 4, 8
VMEM_LIMIT = 16 * 1024 * 1024


def hop(block, mask):
    count = lax.axis_size("dev")
    return lax.ppermute(block, "dev", [(low, low ^ mask) for low in range(count)])


def adam_update(master, first, second, grad):
    first_new = beta_one * first + (1.0 - beta_one) * grad
    second_new = beta_two * second + (1.0 - beta_two) * grad * grad
    direction = first_new / corr_one / (jnp.sqrt(second_new / corr_two) + adam_eps)
    master_new = master - learn_rate * (direction + decay_rate * master)
    return (master_new, first_new, second_new)


def place_pieces(chip, pieces, weights):
    rows = pieces[0].shape[1]
    for j, piece in enumerate(pieces):
        start = pl.multiple_of(lax.bitwise_xor(chip, j) * rows, rows)
        weights[:, pl.ds(start, rows), :] = piece[...]


def transpose_kernel(own_x, other_x, own_c, other_c, x_turned, c_turned):
    chip = lax.axis_index("dev") // 2
    tokens, width = own_x.shape
    rows = 2 * width // lax.axis_size("dev")
    lanes = max(128, rows)
    for out, pair in ((x_turned, (own_x, other_x)), (c_turned, (own_c, other_c))):
        for part, ref in enumerate(pair):
            for at in range(0, width, lanes):
                turned = ref[:, at : at + lanes].T
                for low in range(0, lanes, rows):
                    j = lax.bitwise_xor(chip, (at + low) // rows)
                    start = pl.multiple_of(j * rows, rows)
                    out[pl.ds(start, rows), part * tokens : (part + 1) * tokens] = turned[low : low + rows]


def places(outs):
    found = []
    for zj in range(len(outs) // 3):
        own, later, pair = outs[3 * zj : 3 * zj + 3]
        by_x, by_y = ((pair, (1,)), (later, ())) if zj % 2 else ((later, ()), (pair, (1,)))
        found += [(own, ()), by_x, by_y, (pair, (0,))]
    return found


def gradient_rows(first_row, products, outs):
    outs = places(outs)
    rows = outs[0][0].shape[1]
    width = len(outs) * rows
    tall = min(width, 256)
    for at in range(0, width, tall):
        for kind, (left, right) in enumerate(products):
            product = jnp.dot(
                left[first_row + at : first_row + at + tall], right[...], preferred_element_type=jnp.float32
            ).astype(jnp.bfloat16)
            for low in range(0, tall, rows):
                out, before = outs[(at + low) // rows]
                out[before + (kind,)] = product[low : low + rows]


def slot_block(slots, slot):
    lane = lax.broadcasted_iota(jnp.int32, slots.shape, 1)
    return jnp.sum(jnp.where(lane == slot, slots[...], 0), axis=1, keepdims=True)


def backward_kernel(count, slots, new_slots, own_live, other_live, *refs):
    pieces = refs[:count]
    own_x, other_x, own_c, other_c, x_turned, c_turned = refs[count : count + 6]
    outs, matches = refs[count + 6 : -5], refs[-5]
    gate_grad, up_grad, hidden_all, weights = refs[-4:]
    me_index = lax.axis_index("dev")
    core = me_index & CORE
    place_pieces(me_index // 2, pieces, weights)
    matches[...] = jnp.where(slot_block(new_slots, me_index) == core, 1, 0)
    tokens = own_x.shape[0]
    sides = ((own_x, own_c, me_index, own_live), (other_x, other_c, me_index ^ CORE, other_live))
    for part, (x_ref, c_ref, slot, live) in enumerate(sides):
        span = slice(part * tokens, (part + 1) * tokens)
        gate_pre = jnp.dot(x_ref[...], weights[0], preferred_element_type=jnp.float32)
        up_pre = jnp.dot(x_ref[...], weights[1], preferred_element_type=jnp.float32)
        grad_hidden = jnp.dot(c_ref[...], weights[2], preferred_element_type=jnp.float32)
        gate_sig = jax.nn.sigmoid(gate_pre)
        gate_act = gate_pre * gate_sig
        alive = jnp.where(slot_block(slots, slot) == core, live[...], 0)
        keep = lax.broadcasted_iota(jnp.int32, gate_pre.shape, 0) < alive
        grad_up = grad_hidden * gate_act
        grad_gate = grad_hidden * up_pre * gate_sig * (1.0 + gate_pre * (1.0 - gate_sig))
        hidden_all[span] = jnp.where(keep, gate_act * up_pre, 0.0).astype(jnp.bfloat16)
        up_grad[span] = jnp.where(keep, grad_up, 0.0).astype(jnp.bfloat16)
        gate_grad[span] = jnp.where(keep, grad_gate, 0.0).astype(jnp.bfloat16)
    products = ((x_turned, gate_grad), (x_turned, up_grad), (c_turned, hidden_all))
    gradient_rows(0, products, outs)


def expert_rows(y_ref, weights, out_ref):
    gate_pre = jnp.dot(y_ref[...], weights[0], preferred_element_type=jnp.float32)
    up_pre = jnp.dot(y_ref[...], weights[1], preferred_element_type=jnp.float32)
    act = (gate_pre * jax.nn.sigmoid(gate_pre) * up_pre).astype(jnp.bfloat16)
    result = lax.dot_general(act, weights[2], (((1,), (1,)), ((), ())), preferred_element_type=jnp.float32)
    out_ref[...] = result.astype(jnp.bfloat16)


def other_kernel(count, *refs):
    pieces = refs[:count]
    other_y, own_y, other_out, weights = refs[count:]
    place_pieces(lax.axis_index("dev") // 2, pieces, weights)
    expert_rows(other_y, weights, other_out)


def own_kernel(weights, own_y, own_out):
    expert_rows(own_y, weights, own_out)


VMEM = pl.BlockSpec(memory_space=pltpu.VMEM)


def params():
    return pltpu.CompilerParams(vmem_limit_bytes=VMEM_LIMIT)


def transposed(own_x, other_x, own_c, other_c):
    tokens, width = own_x.shape
    return pl.pallas_call(
        transpose_kernel,
        out_shape=[jax.ShapeDtypeStruct((width, 2 * tokens), own_x.dtype)] * 2,
        in_specs=[VMEM] * 4,
        out_specs=[VMEM] * 2,
        compiler_params=params(),
        cost_estimate=pl.CostEstimate(flops=0, bytes_accessed=16 * tokens * width, transcendentals=0),
        name="transpose_rows",
    )(own_x, other_x, own_c, other_c)


def backward(slots, new_slots, own_live, other_live, pieces, own_x, other_x, own_c, other_c, x_turned, c_turned):
    count = len(pieces)
    kinds, rows, units = pieces[0].shape
    tokens, width = own_x.shape
    one = jax.ShapeDtypeStruct((kinds, rows, units), jnp.bfloat16)
    two = jax.ShapeDtypeStruct((2, kinds, rows, units), jnp.bfloat16)
    return pl.pallas_call(
        functools.partial(backward_kernel, count),
        out_shape=[one, one, two] * (count // 4) + [jax.ShapeDtypeStruct((1, 1), jnp.int32)],
        in_specs=[VMEM] * (count + 10),
        out_specs=[VMEM] * (3 * count // 4 + 1),
        scratch_shapes=[
            pltpu.VMEM((2 * tokens, units), jnp.bfloat16),
            pltpu.VMEM((2 * tokens, units), jnp.bfloat16),
            pltpu.VMEM((2 * tokens, units), jnp.bfloat16),
            pltpu.VMEM((kinds, width, units), jnp.bfloat16),
        ],
        compiler_params=params(),
        cost_estimate=pl.CostEstimate(
            flops=24 * tokens * width * units,
            bytes_accessed=16 * tokens * width + 12 * width * units,
            transcendentals=2 * tokens * units,
        ),
        name="slot_gradients",
    )(slots, new_slots, own_live, other_live, *pieces, own_x, other_x, own_c, other_c, x_turned, c_turned)


def forward(pieces, own_y, other_y):
    count = len(pieces)
    kinds, rows, units = pieces[0].shape
    tokens, width = own_y.shape
    one = jax.ShapeDtypeStruct((tokens, width), jnp.bfloat16)
    cost = pl.CostEstimate(
        flops=6 * tokens * width * units,
        bytes_accessed=4 * tokens * width + 6 * width * units,
        transcendentals=tokens * units,
    )
    other_out, weights = pl.pallas_call(
        functools.partial(other_kernel, count),
        out_shape=[one, jax.ShapeDtypeStruct((kinds, width, units), jnp.bfloat16)],
        in_specs=[VMEM] * (count + 2),
        out_specs=[VMEM] * 2,
        compiler_params=params(),
        cost_estimate=cost,
        name="other_outputs",
    )(*pieces, other_y, own_y)
    own_out = pl.pallas_call(
        own_kernel,
        out_shape=one,
        in_specs=[VMEM, VMEM],
        out_specs=VMEM,
        compiler_params=params(),
        cost_estimate=cost,
        name="own_outputs",
    )(weights, own_y)
    return own_out, other_out


def after(value, *others):
    return lax.optimization_barrier((value,) + others)[0]


def gather_chips(piece):
    depth = lax.axis_size("dev") // Z_UNIT
    column = [piece] + [None] * (depth - 1)
    for top in reversed([1 << bit for bit in range(depth.bit_length() - 1)]):
        column[top] = hop(piece, top * Z_UNIT)
    along_x, along_y, across = [None] * depth, [None] * depth, [None] * depth
    along_x[0] = hop(piece, X_STEP)
    along_y[0] = hop(piece, Y_STEP)
    along_x[1] = hop(column[1], X_STEP)
    for zj in range(2, depth):
        top = 1 << zj.bit_length() - 1
        if zj != top:
            column[zj] = hop(column[top], (zj - top) * Z_UNIT)
    along_y[1] = hop(after(column[1], along_x[0]), Y_STEP)
    for zj in range(2, depth, 2):
        along_x[zj] = hop(after(column[zj], along_x[zj - 2], along_y[zj - 2]), X_STEP)
        across[zj - 2] = hop(after(along_x[zj - 2], along_y[zj - 2]), Y_STEP)
        along_x[zj + 1] = hop(after(column[zj + 1], along_x[zj - 1]), X_STEP)
        along_y[zj + 1] = hop(after(column[zj + 1], along_x[zj - 1]), Y_STEP)
        along_y[zj] = hop(after(column[zj], along_y[zj - 1]), Y_STEP)
        across[zj - 1] = hop(after(along_y[zj - 1], along_x[zj]), X_STEP)
    across[-2] = hop(after(along_x[-2], along_x[-1]), Y_STEP)
    across[-1] = hop(along_y[-1], X_STEP)
    return [part for group in zip(column, along_x, along_y, across) for part in group]


def add_all(first, *others):
    total = first.astype(jnp.float32)
    for other in others:
        total = total + other.astype(jnp.float32)
    return total


def reduce_chips(pieces):
    depth = lax.axis_size("dev") // Z_UNIT
    total, waiting, arrived, crossed = [], [], (), ()
    for upper in reversed(range(1, depth, 2)):
        own_up, up_y, pair_x = pieces[3 * upper : 3 * upper + 3]
        own_low, low_x, pair_y = pieces[3 * upper - 3 : 3 * upper]
        got_x = hop(pair_x, X_STEP)
        got_y = hop(after(pair_y, *arrived), Y_STEP)
        up_y = hop(after(add_all(up_y, got_x[0]).astype(jnp.bfloat16), *crossed), Y_STEP)
        low_x = hop(after(add_all(low_x, got_y[0]).astype(jnp.bfloat16), *crossed), X_STEP)
        arrived, crossed = (got_x,), (low_x,)
        low = [own_low, got_y[1], low_x]
        up = add_all(own_up, got_x[1], up_y).astype(jnp.bfloat16)
        if upper > 1:
            total.append(hop(add_all(*low).astype(jnp.bfloat16), (upper - 1) * Z_UNIT))
            waiting.append((up, upper * Z_UNIT))
        else:
            total += low
            total += [hop(after(part, got_y), mask) for part, mask in waiting]
            total.append(hop(up, Z_UNIT))
    return add_all(*total)


def block_a_core(master, first, second, old_rows, old_cotangent, new_rows, old_slots, new_slots, live):
    local_rows = master.shape[2]
    core = lax.axis_index("dev") & CORE

    def both_rows(own, other):
        return jnp.where(
            core == 0, jnp.concatenate([own, other], axis=-2), jnp.concatenate([other, own], axis=-2)
        )

    other_x = hop(old_rows, CORE)
    other_c = hop(old_cotangent, CORE)
    state = jnp.stack([master, first, second], axis=1)
    mine = lax.dynamic_index_in_dim(state, core, 0, keepdims=False)
    theirs = hop(lax.dynamic_index_in_dim(state, 1 - core, 0, keepdims=False), CORE)
    other_y = hop(new_rows, CORE)
    other_live = hop(live, CORE)
    x_turned, c_turned = transposed(old_rows, other_x, old_cotangent, other_c)
    theirs, other_y, other_live, x_turned, c_turned = lax.optimization_barrier(
        (theirs, other_y, other_live, x_turned, c_turned)
    )
    master_two = both_rows(mine[0], theirs[0])
    pieces = gather_chips(master_two.astype(jnp.bfloat16))
    *grads, matches = backward(
        old_slots[None],
        new_slots[None],
        live[None],
        other_live[None],
        pieces,
        old_rows,
        other_x,
        old_cotangent,
        other_c,
        x_turned,
        c_turned,
    )
    theirs = after(theirs, grads[0])
    first_two = both_rows(mine[1], theirs[1])
    second_two = both_rows(mine[2], theirs[2])
    grad = reduce_chips(grads)
    updated = adam_update(master_two, first_two, second_two, grad)

    new_pieces = gather_chips(updated[0].astype(jnp.bfloat16))
    updated = jnp.stack(updated)
    own_part = lax.dynamic_slice_in_dim(updated, core * local_rows, local_rows, 2)
    other_part = lax.dynamic_slice_in_dim(updated, (1 - core) * local_rows, local_rows, 2)
    own_out, other_out = forward(new_pieces, new_rows, other_y)
    from_other = hop(after(other_part, other_out), CORE)
    state = jnp.where(
        core == 0, jnp.stack([own_part, from_other], axis=1), jnp.stack([from_other, own_part], axis=1)
    )
    new_outputs = jnp.where(matches == 1, own_out, hop(other_out, CORE))
    return (state[0], state[1], state[2], new_outputs[None])


def hidden_terms(tokens, cotangent, weights, live):
    positions = jnp.arange(tokens.shape[0], dtype=jnp.int32)
    cotangent = jnp.where((positions < live)[:, None], cotangent, jnp.zeros_like(cotangent))
    gate_pre = jnp.dot(tokens, weights[0], preferred_element_type=jnp.float32)
    up_pre = jnp.dot(tokens, weights[1], preferred_element_type=jnp.float32)
    gate_sig = jax.nn.sigmoid(gate_pre)
    gate_act = gate_pre * gate_sig
    hidden = (gate_act * up_pre).astype(jnp.bfloat16)
    grad_down = lax.dot_general(
        cotangent, hidden, (((0,), (0,)), ((), ())), preferred_element_type=jnp.float32
    )
    grad_hidden = jnp.dot(cotangent, weights[2], preferred_element_type=jnp.float32)
    grad_up_pre = (grad_hidden * gate_act).astype(jnp.bfloat16)
    grad_gate_pre = (grad_hidden * up_pre * gate_sig * (1.0 + gate_pre * (1.0 - gate_sig))).astype(
        jnp.bfloat16
    )
    grad_gate = lax.dot_general(
        tokens, grad_gate_pre, (((0,), (0,)), ((), ())), preferred_element_type=jnp.float32
    )
    grad_up = lax.dot_general(
        tokens, grad_up_pre, (((0,), (0,)), ((), ())), preferred_element_type=jnp.float32
    )
    return jnp.stack([grad_gate, grad_up, grad_down])


def expert_forward(tokens, weights):
    gate_pre = jnp.dot(tokens, weights[0], preferred_element_type=jnp.float32)
    up_pre = jnp.dot(tokens, weights[1], preferred_element_type=jnp.float32)
    activation = (jax.nn.silu(gate_pre) * up_pre).astype(jnp.bfloat16)
    result = lax.dot_general(
        activation, weights[2], (((1,), (1,)), ((), ())), preferred_element_type=jnp.float32
    )
    return result.astype(jnp.bfloat16)


def halving(buffer, levels, me_index):
    for step in range(levels):
        count = buffer.shape[2]
        halves = buffer.reshape(buffer.shape[:2] + (count // 2, 2) + buffer.shape[3:])
        own_bit = me_index >> step & 1
        keeping = lax.dynamic_index_in_dim(halves, own_bit, 3, keepdims=False)
        sending = lax.dynamic_index_in_dim(halves, 1 - own_bit, 3, keepdims=False)
        buffer = keeping + hop(sending, 1 << step)
    return buffer


def any_shape(master, first, second, old_rows, old_cotangent, new_rows, old_slots, new_slots, live):
    blocks, kinds, local_rows, block_width = master.shape
    devices = lax.axis_size("dev")
    me_index = lax.axis_index("dev")
    own_old = lax.dynamic_index_in_dim(old_slots, me_index, 0, keepdims=False)
    own_new = lax.dynamic_index_in_dim(new_slots, me_index, 0, keepdims=False)
    every_block = lax.all_gather(master.astype(jnp.bfloat16), "dev", axis=2, tiled=True)
    weights = lax.dynamic_index_in_dim(every_block, own_old, 0, keepdims=False)
    slot_grad = hidden_terms(old_rows, old_cotangent, weights, live[0])
    block_ids = jnp.arange(blocks, dtype=jnp.int32)[:, None, None, None, None]
    dense = slot_grad.reshape(kinds, devices, local_rows, block_width)
    buffer = jnp.where(block_ids == own_old, dense[None], jnp.zeros((), jnp.float32))
    buffer = halving(buffer, devices.bit_length() - 1, me_index)
    grad = buffer.reshape(master.shape)
    new_master, new_first, new_second = adam_update(master, first, second, grad)
    updated_blocks = lax.all_gather(new_master.astype(jnp.bfloat16), "dev", axis=2, tiled=True)
    new_weights = lax.dynamic_index_in_dim(updated_blocks, own_new, 0, keepdims=False)
    return (new_master, new_first, new_second, expert_forward(new_rows, new_weights)[None])


def on_device(
    master,
    first_moment,
    second_moment,
    old_rows,
    old_cotangent,
    new_rows,
    old_slots,
    new_slots,
    live_rows,
):
    blocks, kinds, local_rows, units = master.shape
    devices = lax.axis_size("dev")
    whole_tiles = local_rows % 16 == 0 and units % 128 == 0 and old_rows.shape[1] % 128 == 0
    form = block_a_core if blocks == 2 and devices % (2 * Z_UNIT) == 0 and whole_tiles else any_shape
    return form(
        master,
        first_moment,
        second_moment,
        old_rows[0],
        old_cotangent[0],
        new_rows[0],
        old_slots,
        new_slots,
        live_rows,
    )


def solution(mesh):
    return jax.shard_map(
        on_device,
        mesh=mesh,
        in_specs=(
            P(None, None, "dev", None),
            P(None, None, "dev", None),
            P(None, None, "dev", None),
            P("dev", None, None),
            P("dev", None, None),
            P("dev", None, None),
            P(),
            P(),
            P("dev"),
        ),
        out_specs=(
            P(None, None, "dev", None),
            P(None, None, "dev", None),
            P(None, None, "dev", None),
            P("dev", None, None),
        ),
        check_vma=False,
    )
```

```python
import functools

import jax
import jax.numpy as jnp
from jax import lax
from jax.experimental import pallas as pl
from jax.experimental.pallas import tpu as pltpu
from jax.sharding import PartitionSpec as P

beta_one = 0.9
beta_two = 0.95
corr_one = 0.9999734386011124
corr_two = 0.994079470779666
adam_eps = 1e-08
learn_rate = 0.003
decay_rate = 0.1

CORE, X_STEP, Y_STEP, Z_UNIT = 1, 2, 4, 8
VMEM_LIMIT = 16 * 1024 * 1024


def hop(block, mask):
    count = lax.axis_size("dev")
    return lax.ppermute(block, "dev", [(low, low ^ mask) for low in range(count)])


def adam_update(master, first, second, grad):
    first_new = beta_one * first + (1.0 - beta_one) * grad
    second_new = beta_two * second + (1.0 - beta_two) * grad * grad
    direction = first_new / corr_one / (jnp.sqrt(second_new / corr_two) + adam_eps)
    master_new = master - learn_rate * (direction + decay_rate * master)
    return (master_new, first_new, second_new)


def place_pieces(chip, pieces, weights):
    rows = pieces[0].shape[1]
    for j, piece in enumerate(pieces):
        start = pl.multiple_of(lax.bitwise_xor(chip, j) * rows, rows)
        weights[:, pl.ds(start, rows), :] = piece[...]


def transpose_kernel(own_x, other_x, own_c, other_c, x_turned, c_turned):
    chip = lax.axis_index("dev") // 2
    tokens, width = own_x.shape
    rows = 2 * width // lax.axis_size("dev")
    lanes = max(128, rows)
    for out, pair in ((x_turned, (own_x, other_x)), (c_turned, (own_c, other_c))):
        for part, ref in enumerate(pair):
            for at in range(0, width, lanes):
                turned = ref[:, at : at + lanes].T
                for low in range(0, lanes, rows):
                    j = lax.bitwise_xor(chip, (at + low) // rows)
                    start = pl.multiple_of(j * rows, rows)
                    out[pl.ds(start, rows), part * tokens : (part + 1) * tokens] = turned[low : low + rows]


def places(outs):
    found = []
    for zj in range(len(outs) // 3):
        own, later, pair = outs[3 * zj : 3 * zj + 3]
        by_x, by_y = ((pair, (1,)), (later, ())) if zj % 2 else ((later, ()), (pair, (1,)))
        found += [(own, ()), by_x, by_y, (pair, (0,))]
    return found


def gradient_rows(first_row, products, outs):
    outs = places(outs)
    rows = outs[0][0].shape[1]
    width = len(outs) * rows
    tall = min(width, 256)
    for at in range(0, width, tall):
        for kind, (left, right) in enumerate(products):
            product = jnp.dot(
                left[first_row + at : first_row + at + tall], right[...], preferred_element_type=jnp.float32
            ).astype(jnp.bfloat16)
            for low in range(0, tall, rows):
                out, before = outs[(at + low) // rows]
                out[before + (kind,)] = product[low : low + rows]


def slot_block(slots, slot):
    lane = lax.broadcasted_iota(jnp.int32, slots.shape, 1)
    return jnp.sum(jnp.where(lane == slot, slots[...], 0), axis=1, keepdims=True)


def backward_kernel(count, slots, new_slots, own_live, other_live, *refs):
    pieces = refs[:count]
    own_x, other_x, own_c, other_c, x_turned, c_turned = refs[count : count + 6]
    outs, matches = refs[count + 6 : -5], refs[-5]
    gate_grad, up_grad, hidden_all, weights = refs[-4:]
    me_index = lax.axis_index("dev")
    core = me_index & CORE
    place_pieces(me_index // 2, pieces, weights)
    matches[...] = jnp.where(slot_block(new_slots, me_index) == core, 1, 0)
    tokens = own_x.shape[0]
    sides = ((own_x, own_c, me_index, own_live), (other_x, other_c, me_index ^ CORE, other_live))
    for part, (x_ref, c_ref, slot, live) in enumerate(sides):
        span = slice(part * tokens, (part + 1) * tokens)
        gate_pre = jnp.dot(x_ref[...], weights[0], preferred_element_type=jnp.float32)
        up_pre = jnp.dot(x_ref[...], weights[1], preferred_element_type=jnp.float32)
        grad_hidden = jnp.dot(c_ref[...], weights[2], preferred_element_type=jnp.float32)
        gate_sig = jax.nn.sigmoid(gate_pre)
        gate_act = gate_pre * gate_sig
        alive = jnp.where(slot_block(slots, slot) == core, live[...], 0)
        keep = lax.broadcasted_iota(jnp.int32, gate_pre.shape, 0) < alive
        grad_up = grad_hidden * gate_act
        grad_gate = grad_hidden * up_pre * gate_sig * (1.0 + gate_pre * (1.0 - gate_sig))
        hidden_all[span] = jnp.where(keep, gate_act * up_pre, 0.0).astype(jnp.bfloat16)
        up_grad[span] = jnp.where(keep, grad_up, 0.0).astype(jnp.bfloat16)
        gate_grad[span] = jnp.where(keep, grad_gate, 0.0).astype(jnp.bfloat16)
    products = ((x_turned, gate_grad), (x_turned, up_grad), (c_turned, hidden_all))
    gradient_rows(0, products, outs)


def expert_rows(y_ref, weights, out_ref):
    gate_pre = jnp.dot(y_ref[...], weights[0], preferred_element_type=jnp.float32)
    up_pre = jnp.dot(y_ref[...], weights[1], preferred_element_type=jnp.float32)
    act = (gate_pre * jax.nn.sigmoid(gate_pre) * up_pre).astype(jnp.bfloat16)
    result = lax.dot_general(act, weights[2], (((1,), (1,)), ((), ())), preferred_element_type=jnp.float32)
    out_ref[...] = result.astype(jnp.bfloat16)


def other_kernel(count, *refs):
    pieces = refs[:count]
    other_y, own_y, other_out, weights = refs[count:]
    place_pieces(lax.axis_index("dev") // 2, pieces, weights)
    expert_rows(other_y, weights, other_out)


def own_kernel(weights, own_y, own_out):
    expert_rows(own_y, weights, own_out)


VMEM = pl.BlockSpec(memory_space=pltpu.VMEM)


def params():
    return pltpu.CompilerParams(vmem_limit_bytes=VMEM_LIMIT)


def transposed(own_x, other_x, own_c, other_c):
    tokens, width = own_x.shape
    return pl.pallas_call(
        transpose_kernel,
        out_shape=[jax.ShapeDtypeStruct((width, 2 * tokens), own_x.dtype)] * 2,
        in_specs=[VMEM] * 4,
        out_specs=[VMEM] * 2,
        compiler_params=params(),
        cost_estimate=pl.CostEstimate(flops=0, bytes_accessed=16 * tokens * width, transcendentals=0),
        name="transpose_rows",
    )(own_x, other_x, own_c, other_c)


def backward(slots, new_slots, own_live, other_live, pieces, own_x, other_x, own_c, other_c, x_turned, c_turned):
    count = len(pieces)
    kinds, rows, units = pieces[0].shape
    tokens, width = own_x.shape
    one = jax.ShapeDtypeStruct((kinds, rows, units), jnp.bfloat16)
    two = jax.ShapeDtypeStruct((2, kinds, rows, units), jnp.bfloat16)
    return pl.pallas_call(
        functools.partial(backward_kernel, count),
        out_shape=[one, one, two] * (count // 4) + [jax.ShapeDtypeStruct((1, 1), jnp.int32)],
        in_specs=[VMEM] * (count + 10),
        out_specs=[VMEM] * (3 * count // 4 + 1),
        scratch_shapes=[
            pltpu.VMEM((2 * tokens, units), jnp.bfloat16),
            pltpu.VMEM((2 * tokens, units), jnp.bfloat16),
            pltpu.VMEM((2 * tokens, units), jnp.bfloat16),
            pltpu.VMEM((kinds, width, units), jnp.bfloat16),
        ],
        compiler_params=params(),
        cost_estimate=pl.CostEstimate(
            flops=24 * tokens * width * units,
            bytes_accessed=16 * tokens * width + 12 * width * units,
            transcendentals=2 * tokens * units,
        ),
        name="slot_gradients",
    )(slots, new_slots, own_live, other_live, *pieces, own_x, other_x, own_c, other_c, x_turned, c_turned)


def forward(pieces, own_y, other_y):
    count = len(pieces)
    kinds, rows, units = pieces[0].shape
    tokens, width = own_y.shape
    one = jax.ShapeDtypeStruct((tokens, width), jnp.bfloat16)
    cost = pl.CostEstimate(
        flops=6 * tokens * width * units,
        bytes_accessed=4 * tokens * width + 6 * width * units,
        transcendentals=tokens * units,
    )
    other_out, weights = pl.pallas_call(
        functools.partial(other_kernel, count),
        out_shape=[one, jax.ShapeDtypeStruct((kinds, width, units), jnp.bfloat16)],
        in_specs=[VMEM] * (count + 2),
        out_specs=[VMEM] * 2,
        compiler_params=params(),
        cost_estimate=cost,
        name="other_outputs",
    )(*pieces, other_y, own_y)
    own_out = pl.pallas_call(
        own_kernel,
        out_shape=one,
        in_specs=[VMEM, VMEM],
        out_specs=VMEM,
        compiler_params=params(),
        cost_estimate=cost,
        name="own_outputs",
    )(weights, own_y)
    return own_out, other_out


def after(value, *others):
    return lax.optimization_barrier((value,) + others)[0]


def gather_chips(piece):
    depth = lax.axis_size("dev") // Z_UNIT
    column = [piece] + [None] * (depth - 1)
    for top in reversed([1 << bit for bit in range(depth.bit_length() - 1)]):
        column[top] = hop(piece, top * Z_UNIT)
    along_x, along_y, across = [None] * depth, [None] * depth, [None] * depth
    along_x[0] = hop(piece, X_STEP)
    along_y[0] = hop(piece, Y_STEP)
    along_x[1] = hop(column[1], X_STEP)
    for zj in range(2, depth):
        top = 1 << zj.bit_length() - 1
        if zj != top:
            column[zj] = hop(column[top], (zj - top) * Z_UNIT)
    along_y[1] = hop(after(column[1], along_x[0]), Y_STEP)
    for zj in range(2, depth, 2):
        along_x[zj] = hop(after(column[zj], along_x[zj - 2], along_y[zj - 2]), X_STEP)
        across[zj - 2] = hop(after(along_x[zj - 2], along_y[zj - 2]), Y_STEP)
        along_x[zj + 1] = hop(after(column[zj + 1], along_x[zj - 1]), X_STEP)
        along_y[zj + 1] = hop(after(column[zj + 1], along_x[zj - 1]), Y_STEP)
        along_y[zj] = hop(after(column[zj], along_y[zj - 1]), Y_STEP)
        across[zj - 1] = hop(after(along_y[zj - 1], along_x[zj]), X_STEP)
    across[-2] = hop(after(along_x[-2], along_x[-1]), Y_STEP)
    across[-1] = hop(along_y[-1], X_STEP)
    return [part for group in zip(column, along_x, along_y, across) for part in group]


def add_all(first, *others):
    total = first.astype(jnp.float32)
    for other in others:
        total = total + other.astype(jnp.float32)
    return total


def reduce_chips(pieces):
    depth = lax.axis_size("dev") // Z_UNIT
    total, waiting, arrived, crossed = [], [], (), ()
    for upper in reversed(range(1, depth, 2)):
        own_up, up_y, pair_x = pieces[3 * upper : 3 * upper + 3]
        own_low, low_x, pair_y = pieces[3 * upper - 3 : 3 * upper]
        got_x = hop(pair_x, X_STEP)
        got_y = hop(after(pair_y, *arrived), Y_STEP)
        up_y = hop(after(add_all(up_y, got_x[0]).astype(jnp.bfloat16), *crossed), Y_STEP)
        low_x = hop(after(add_all(low_x, got_y[0]).astype(jnp.bfloat16), *crossed), X_STEP)
        arrived, crossed = (got_x,), (low_x,)
        low = [own_low, got_y[1], low_x]
        up = add_all(own_up, got_x[1], up_y).astype(jnp.bfloat16)
        if upper > 1:
            total.append(hop(add_all(*low).astype(jnp.bfloat16), (upper - 1) * Z_UNIT))
            waiting.append((up, upper * Z_UNIT))
        else:
            total += low
            total += [hop(after(part, got_y), mask) for part, mask in waiting]
            total.append(hop(up, Z_UNIT))
    return add_all(*total)


def block_a_core(master, first, second, old_rows, old_cotangent, new_rows, old_slots, new_slots, live):
    local_rows = master.shape[2]
    core = lax.axis_index("dev") & CORE

    def mine(state):
        return lax.dynamic_index_in_dim(state, core, 0, keepdims=False)

    def partners(state):
        return lax.dynamic_index_in_dim(state, 1 - core, 0, keepdims=False)

    def both_rows(own, other):
        return jnp.where(
            core == 0, jnp.concatenate([own, other], axis=-2), jnp.concatenate([other, own], axis=-2)
        )

    other_x = hop(old_rows, CORE)
    other_c = hop(old_cotangent, CORE)
    theirs = hop(jnp.stack([partners(master), partners(first), partners(second)]), CORE)
    other_y = hop(new_rows, CORE)
    other_live = hop(live, CORE)
    x_turned, c_turned = transposed(old_rows, other_x, old_cotangent, other_c)
    theirs, other_y, other_live, x_turned, c_turned = lax.optimization_barrier(
        (theirs, other_y, other_live, x_turned, c_turned)
    )
    master_two = both_rows(mine(master), theirs[0])
    pieces = gather_chips(master_two.astype(jnp.bfloat16))
    *grads, matches = backward(
        old_slots[None],
        new_slots[None],
        live[None],
        other_live[None],
        pieces,
        old_rows,
        other_x,
        old_cotangent,
        other_c,
        x_turned,
        c_turned,
    )
    theirs = after(theirs, grads[0])
    first_two = both_rows(mine(first), theirs[1])
    second_two = both_rows(mine(second), theirs[2])
    grad = reduce_chips(grads)
    updated = adam_update(master_two, first_two, second_two, grad)

    new_pieces = gather_chips(updated[0].astype(jnp.bfloat16))
    updated = jnp.stack(updated)
    own_part = lax.dynamic_slice_in_dim(updated, core * local_rows, local_rows, 2)
    other_part = lax.dynamic_slice_in_dim(updated, (1 - core) * local_rows, local_rows, 2)
    own_out, other_out = forward(new_pieces, new_rows, other_y)
    from_other = hop(after(other_part, other_out), CORE)
    state = jnp.where(
        core == 0, jnp.stack([own_part, from_other], axis=1), jnp.stack([from_other, own_part], axis=1)
    )
    new_outputs = jnp.where(matches == 1, own_out, hop(other_out, CORE))
    return (state[0], state[1], state[2], new_outputs[None])


def hidden_terms(tokens, cotangent, weights, live):
    positions = jnp.arange(tokens.shape[0], dtype=jnp.int32)
    cotangent = jnp.where((positions < live)[:, None], cotangent, jnp.zeros_like(cotangent))
    gate_pre = jnp.dot(tokens, weights[0], preferred_element_type=jnp.float32)
    up_pre = jnp.dot(tokens, weights[1], preferred_element_type=jnp.float32)
    gate_sig = jax.nn.sigmoid(gate_pre)
    gate_act = gate_pre * gate_sig
    hidden = (gate_act * up_pre).astype(jnp.bfloat16)
    grad_down = lax.dot_general(
        cotangent, hidden, (((0,), (0,)), ((), ())), preferred_element_type=jnp.float32
    )
    grad_hidden = jnp.dot(cotangent, weights[2], preferred_element_type=jnp.float32)
    grad_up_pre = (grad_hidden * gate_act).astype(jnp.bfloat16)
    grad_gate_pre = (grad_hidden * up_pre * gate_sig * (1.0 + gate_pre * (1.0 - gate_sig))).astype(
        jnp.bfloat16
    )
    grad_gate = lax.dot_general(
        tokens, grad_gate_pre, (((0,), (0,)), ((), ())), preferred_element_type=jnp.float32
    )
    grad_up = lax.dot_general(
        tokens, grad_up_pre, (((0,), (0,)), ((), ())), preferred_element_type=jnp.float32
    )
    return jnp.stack([grad_gate, grad_up, grad_down])


def expert_forward(tokens, weights):
    gate_pre = jnp.dot(tokens, weights[0], preferred_element_type=jnp.float32)
    up_pre = jnp.dot(tokens, weights[1], preferred_element_type=jnp.float32)
    activation = (jax.nn.silu(gate_pre) * up_pre).astype(jnp.bfloat16)
    result = lax.dot_general(
        activation, weights[2], (((1,), (1,)), ((), ())), preferred_element_type=jnp.float32
    )
    return result.astype(jnp.bfloat16)


def halving(buffer, levels, me_index):
    for step in range(levels):
        count = buffer.shape[2]
        halves = buffer.reshape(buffer.shape[:2] + (count // 2, 2) + buffer.shape[3:])
        own_bit = me_index >> step & 1
        keeping = lax.dynamic_index_in_dim(halves, own_bit, 3, keepdims=False)
        sending = lax.dynamic_index_in_dim(halves, 1 - own_bit, 3, keepdims=False)
        buffer = keeping + hop(sending, 1 << step)
    return buffer


def any_shape(master, first, second, old_rows, old_cotangent, new_rows, old_slots, new_slots, live):
    blocks, kinds, local_rows, block_width = master.shape
    devices = lax.axis_size("dev")
    me_index = lax.axis_index("dev")
    own_old = lax.dynamic_index_in_dim(old_slots, me_index, 0, keepdims=False)
    own_new = lax.dynamic_index_in_dim(new_slots, me_index, 0, keepdims=False)
    every_block = lax.all_gather(master.astype(jnp.bfloat16), "dev", axis=2, tiled=True)
    weights = lax.dynamic_index_in_dim(every_block, own_old, 0, keepdims=False)
    slot_grad = hidden_terms(old_rows, old_cotangent, weights, live[0])
    block_ids = jnp.arange(blocks, dtype=jnp.int32)[:, None, None, None, None]
    dense = slot_grad.reshape(kinds, devices, local_rows, block_width)
    buffer = jnp.where(block_ids == own_old, dense[None], jnp.zeros((), jnp.float32))
    buffer = halving(buffer, devices.bit_length() - 1, me_index)
    grad = buffer.reshape(master.shape)
    new_master, new_first, new_second = adam_update(master, first, second, grad)
    updated_blocks = lax.all_gather(new_master.astype(jnp.bfloat16), "dev", axis=2, tiled=True)
    new_weights = lax.dynamic_index_in_dim(updated_blocks, own_new, 0, keepdims=False)
    return (new_master, new_first, new_second, expert_forward(new_rows, new_weights)[None])


def on_device(
    master,
    first_moment,
    second_moment,
    old_rows,
    old_cotangent,
    new_rows,
    old_slots,
    new_slots,
    live_rows,
):
    blocks, kinds, local_rows, units = master.shape
    devices = lax.axis_size("dev")
    whole_tiles = local_rows % 16 == 0 and units % 128 == 0 and old_rows.shape[1] % 128 == 0
    form = block_a_core if blocks == 2 and devices % (2 * Z_UNIT) == 0 and whole_tiles else any_shape
    return form(
        master,
        first_moment,
        second_moment,
        old_rows[0],
        old_cotangent[0],
        new_rows[0],
        old_slots,
        new_slots,
        live_rows,
    )


def solution(mesh):
    return jax.shard_map(
        on_device,
        mesh=mesh,
        in_specs=(
            P(None, None, "dev", None),
            P(None, None, "dev", None),
            P(None, None, "dev", None),
            P("dev", None, None),
            P("dev", None, None),
            P("dev", None, None),
            P(),
            P(),
            P("dev"),
        ),
        out_specs=(
            P(None, None, "dev", None),
            P(None, None, "dev", None),
            P(None, None, "dev", None),
            P("dev", None, None),
        ),
        check_vma=False,
    )
```

```python
import functools

import jax
import jax.numpy as jnp
from jax import lax
from jax.experimental import pallas as pl
from jax.experimental.pallas import tpu as pltpu
from jax.sharding import PartitionSpec as P

beta_one = 0.9
beta_two = 0.95
corr_one = 0.9999734386011124
corr_two = 0.994079470779666
adam_eps = 1e-08
learn_rate = 0.003
decay_rate = 0.1

CORE, X_STEP, Y_STEP, Z_UNIT = 1, 2, 4, 8
VMEM_LIMIT = 16 * 1024 * 1024


def hop(block, mask):
    count = lax.axis_size("dev")
    return lax.ppermute(block, "dev", [(low, low ^ mask) for low in range(count)])


def adam_update(master, first, second, grad):
    first_new = beta_one * first + (1.0 - beta_one) * grad
    second_new = beta_two * second + (1.0 - beta_two) * grad * grad
    direction = first_new / corr_one / (jnp.sqrt(second_new / corr_two) + adam_eps)
    master_new = master - learn_rate * (direction + decay_rate * master)
    return (master_new, first_new, second_new)


def place_pieces(chip, pieces, weights):
    rows = pieces[0].shape[1]
    for j, piece in enumerate(pieces):
        start = pl.multiple_of(lax.bitwise_xor(chip, j) * rows, rows)
        weights[:, pl.ds(start, rows), :] = piece[...]


def transpose_kernel(own_x, other_x, own_c, other_c, x_turned, c_turned):
    chip = lax.axis_index("dev") // 2
    tokens, width = own_x.shape
    rows = 2 * width // lax.axis_size("dev")
    lanes = max(128, rows)
    for out, pair in ((x_turned, (own_x, other_x)), (c_turned, (own_c, other_c))):
        for part, ref in enumerate(pair):
            for at in range(0, width, lanes):
                turned = ref[:, at : at + lanes].T
                for low in range(0, lanes, rows):
                    j = lax.bitwise_xor(chip, (at + low) // rows)
                    start = pl.multiple_of(j * rows, rows)
                    out[pl.ds(start, rows), part * tokens : (part + 1) * tokens] = turned[low : low + rows]


def places(outs):
    found = []
    for zj in range(len(outs) // 3):
        own, later, pair = outs[3 * zj : 3 * zj + 3]
        by_x, by_y = ((pair, (1,)), (later, ())) if zj % 2 else ((later, ()), (pair, (1,)))
        found += [(own, ()), by_x, by_y, (pair, (0,))]
    return found


def gradient_rows(first_row, products, outs):
    outs = places(outs)
    rows = outs[0][0].shape[1]
    width = len(outs) * rows
    tall = min(width, 256)
    for at in range(0, width, tall):
        for kind, (left, right) in enumerate(products):
            product = jnp.dot(
                left[first_row + at : first_row + at + tall], right[...], preferred_element_type=jnp.float32
            ).astype(jnp.bfloat16)
            for low in range(0, tall, rows):
                out, before = outs[(at + low) // rows]
                out[before + (kind,)] = product[low : low + rows]


def slot_block(slots, slot):
    lane = lax.broadcasted_iota(jnp.int32, slots.shape, 1)
    return jnp.sum(jnp.where(lane == slot, slots[...], 0), axis=1, keepdims=True)


def backward_kernel(count, slots, new_slots, own_live, other_live, *refs):
    pieces = refs[:count]
    own_x, other_x, own_c, other_c, x_turned, c_turned = refs[count : count + 6]
    outs, matches = refs[count + 6 : -5], refs[-5]
    gate_grad, up_grad, hidden_all, weights = refs[-4:]
    me_index = lax.axis_index("dev")
    core = me_index & CORE
    place_pieces(me_index // 2, pieces, weights)
    matches[...] = jnp.where(slot_block(new_slots, me_index) == core, 1, 0)
    tokens = own_x.shape[0]
    sides = ((own_x, own_c, me_index, own_live), (other_x, other_c, me_index ^ CORE, other_live))
    for part, (x_ref, c_ref, slot, live) in enumerate(sides):
        span = slice(part * tokens, (part + 1) * tokens)
        gate_pre = jnp.dot(x_ref[...], weights[0], preferred_element_type=jnp.float32)
        up_pre = jnp.dot(x_ref[...], weights[1], preferred_element_type=jnp.float32)
        grad_hidden = jnp.dot(c_ref[...], weights[2], preferred_element_type=jnp.float32)
        gate_sig = jax.nn.sigmoid(gate_pre)
        gate_act = gate_pre * gate_sig
        alive = jnp.where(slot_block(slots, slot) == core, live[...], 0)
        keep = lax.broadcasted_iota(jnp.int32, gate_pre.shape, 0) < alive
        grad_up = grad_hidden * gate_act
        grad_gate = grad_hidden * up_pre * gate_sig * (1.0 + gate_pre * (1.0 - gate_sig))
        hidden_all[span] = jnp.where(keep, gate_act * up_pre, 0.0).astype(jnp.bfloat16)
        up_grad[span] = jnp.where(keep, grad_up, 0.0).astype(jnp.bfloat16)
        gate_grad[span] = jnp.where(keep, grad_gate, 0.0).astype(jnp.bfloat16)
    products = ((x_turned, gate_grad), (x_turned, up_grad), (c_turned, hidden_all))
    gradient_rows(0, products, outs)


def expert_rows(y_ref, weights, out_ref):
    gate_pre = jnp.dot(y_ref[...], weights[0], preferred_element_type=jnp.float32)
    up_pre = jnp.dot(y_ref[...], weights[1], preferred_element_type=jnp.float32)
    act = (gate_pre * jax.nn.sigmoid(gate_pre) * up_pre).astype(jnp.bfloat16)
    result = lax.dot_general(act, weights[2], (((1,), (1,)), ((), ())), preferred_element_type=jnp.float32)
    out_ref[...] = result.astype(jnp.bfloat16)


def other_kernel(count, *refs):
    pieces = refs[:count]
    other_y, own_y, other_out, weights = refs[count:]
    place_pieces(lax.axis_index("dev") // 2, pieces, weights)
    expert_rows(other_y, weights, other_out)


def own_kernel(weights, own_y, own_out):
    expert_rows(own_y, weights, own_out)


VMEM = pl.BlockSpec(memory_space=pltpu.VMEM)


def params():
    return pltpu.CompilerParams(vmem_limit_bytes=VMEM_LIMIT)


def transposed(own_x, other_x, own_c, other_c):
    tokens, width = own_x.shape
    return pl.pallas_call(
        transpose_kernel,
        out_shape=[jax.ShapeDtypeStruct((width, 2 * tokens), own_x.dtype)] * 2,
        in_specs=[VMEM] * 4,
        out_specs=[VMEM] * 2,
        compiler_params=params(),
        cost_estimate=pl.CostEstimate(flops=0, bytes_accessed=16 * tokens * width, transcendentals=0),
        name="transpose_rows",
    )(own_x, other_x, own_c, other_c)


def backward(slots, new_slots, own_live, other_live, pieces, own_x, other_x, own_c, other_c, x_turned, c_turned):
    count = len(pieces)
    kinds, rows, units = pieces[0].shape
    tokens, width = own_x.shape
    one = jax.ShapeDtypeStruct((kinds, rows, units), jnp.bfloat16)
    two = jax.ShapeDtypeStruct((2, kinds, rows, units), jnp.bfloat16)
    return pl.pallas_call(
        functools.partial(backward_kernel, count),
        out_shape=[one, one, two] * (count // 4) + [jax.ShapeDtypeStruct((1, 1), jnp.int32)],
        in_specs=[VMEM] * (count + 10),
        out_specs=[VMEM] * (3 * count // 4 + 1),
        scratch_shapes=[
            pltpu.VMEM((2 * tokens, units), jnp.bfloat16),
            pltpu.VMEM((2 * tokens, units), jnp.bfloat16),
            pltpu.VMEM((2 * tokens, units), jnp.bfloat16),
            pltpu.VMEM((kinds, width, units), jnp.bfloat16),
        ],
        compiler_params=params(),
        cost_estimate=pl.CostEstimate(
            flops=24 * tokens * width * units,
            bytes_accessed=16 * tokens * width + 12 * width * units,
            transcendentals=2 * tokens * units,
        ),
        name="slot_gradients",
    )(slots, new_slots, own_live, other_live, *pieces, own_x, other_x, own_c, other_c, x_turned, c_turned)


def forward(pieces, own_y, other_y):
    count = len(pieces)
    kinds, rows, units = pieces[0].shape
    tokens, width = own_y.shape
    one = jax.ShapeDtypeStruct((tokens, width), jnp.bfloat16)
    cost = pl.CostEstimate(
        flops=6 * tokens * width * units,
        bytes_accessed=4 * tokens * width + 6 * width * units,
        transcendentals=tokens * units,
    )
    other_out, weights = pl.pallas_call(
        functools.partial(other_kernel, count),
        out_shape=[one, jax.ShapeDtypeStruct((kinds, width, units), jnp.bfloat16)],
        in_specs=[VMEM] * (count + 2),
        out_specs=[VMEM] * 2,
        compiler_params=params(),
        cost_estimate=cost,
        name="other_outputs",
    )(*pieces, other_y, own_y)
    own_out = pl.pallas_call(
        own_kernel,
        out_shape=one,
        in_specs=[VMEM, VMEM],
        out_specs=VMEM,
        compiler_params=params(),
        cost_estimate=cost,
        name="own_outputs",
    )(weights, own_y)
    return own_out, other_out


def after(value, *others):
    return lax.optimization_barrier((value,) + others)[0]


def gather_chips(piece, *first):
    depth = lax.axis_size("dev") // Z_UNIT
    column = [piece] + [None] * (depth - 1)
    for top in reversed([1 << bit for bit in range(depth.bit_length() - 1)]):
        column[top] = hop(piece, top * Z_UNIT)
    along_x, along_y, across = [None] * depth, [None] * depth, [None] * depth
    along_x[0] = hop(piece, X_STEP)
    along_y[0] = hop(piece, Y_STEP)
    along_x[1] = hop(column[1], X_STEP)
    for zj in range(2, depth):
        top = 1 << zj.bit_length() - 1
        if zj != top:
            column[zj] = hop(after(column[top], *first), (zj - top) * Z_UNIT)
    along_y[1] = hop(after(column[1], along_x[0]), Y_STEP)
    for zj in range(2, depth, 2):
        along_x[zj] = hop(after(column[zj], along_x[zj - 2], along_y[zj - 2]), X_STEP)
        across[zj - 2] = hop(after(along_x[zj - 2], along_y[zj - 2]), Y_STEP)
        along_x[zj + 1] = hop(after(column[zj + 1], along_x[zj - 1]), X_STEP)
        along_y[zj + 1] = hop(after(column[zj + 1], along_x[zj - 1]), Y_STEP)
        along_y[zj] = hop(after(column[zj], along_y[zj - 1]), Y_STEP)
        across[zj - 1] = hop(after(along_y[zj - 1], along_x[zj]), X_STEP)
    across[-2] = hop(after(along_x[-2], along_x[-1]), Y_STEP)
    across[-1] = hop(along_y[-1], X_STEP)
    return [part for group in zip(column, along_x, along_y, across) for part in group]


def add_all(first, *others):
    total = first.astype(jnp.float32)
    for other in others:
        total = total + other.astype(jnp.float32)
    return total


def reduce_chips(pieces):
    depth = lax.axis_size("dev") // Z_UNIT
    total, waiting, arrived, crossed = [], [], (), ()
    for upper in reversed(range(1, depth, 2)):
        own_up, up_y, pair_x = pieces[3 * upper : 3 * upper + 3]
        own_low, low_x, pair_y = pieces[3 * upper - 3 : 3 * upper]
        got_x = hop(pair_x, X_STEP)
        got_y = hop(after(pair_y, *arrived), Y_STEP)
        up_y = hop(after(add_all(up_y, got_x[0]).astype(jnp.bfloat16), *crossed), Y_STEP)
        low_x = hop(after(add_all(low_x, got_y[0]).astype(jnp.bfloat16), *crossed), X_STEP)
        arrived, crossed = (got_x,), (low_x,)
        low = [own_low, got_y[1], low_x]
        up = add_all(own_up, got_x[1], up_y).astype(jnp.bfloat16)
        if upper > 1:
            total.append(hop(add_all(*low).astype(jnp.bfloat16), (upper - 1) * Z_UNIT))
            waiting.append((up, upper * Z_UNIT))
        else:
            total += low
            total += [hop(after(part, got_y), mask) for part, mask in waiting]
            total.append(hop(up, Z_UNIT))
    return add_all(*total)


def block_a_core(master, first, second, old_rows, old_cotangent, new_rows, old_slots, new_slots, live):
    local_rows = master.shape[2]
    core = lax.axis_index("dev") & CORE

    def mine(state):
        return lax.dynamic_index_in_dim(state, core, 0, keepdims=False)

    def partners(state):
        return lax.dynamic_index_in_dim(state, 1 - core, 0, keepdims=False)

    def both_rows(own, other):
        return jnp.where(
            core == 0, jnp.concatenate([own, other], axis=-2), jnp.concatenate([other, own], axis=-2)
        )

    other_x = hop(old_rows, CORE)
    other_c = hop(old_cotangent, CORE)
    their_master = hop(partners(master), CORE)
    theirs = hop(jnp.stack([partners(first), partners(second)]), CORE)
    other_y = hop(new_rows, CORE)
    other_live = hop(live, CORE)
    x_turned, c_turned = transposed(old_rows, other_x, old_cotangent, other_c)
    their_master, other_y, other_live, x_turned, c_turned = lax.optimization_barrier(
        (their_master, other_y, other_live, x_turned, c_turned)
    )
    master_two = both_rows(mine(master), their_master)
    pieces = gather_chips(master_two.astype(jnp.bfloat16), theirs)
    *grads, matches = backward(
        old_slots[None],
        new_slots[None],
        live[None],
        other_live[None],
        pieces,
        old_rows,
        other_x,
        old_cotangent,
        other_c,
        x_turned,
        c_turned,
    )
    theirs = after(theirs, grads[0])
    first_two = both_rows(mine(first), theirs[0])
    second_two = both_rows(mine(second), theirs[1])
    grad = reduce_chips(grads)
    grad, is_own = lax.optimization_barrier((grad, matches == 1))
    updated = adam_update(master_two, first_two, second_two, grad)

    new_pieces = gather_chips(updated[0].astype(jnp.bfloat16))
    updated = jnp.stack(updated)
    own_part = lax.dynamic_slice_in_dim(updated, core * local_rows, local_rows, 2)
    other_part = lax.dynamic_slice_in_dim(updated, (1 - core) * local_rows, local_rows, 2)
    own_out, other_out = forward(new_pieces, new_rows, other_y)
    from_other = hop(after(other_part, other_out), CORE)
    state = jnp.where(
        core == 0, jnp.stack([own_part, from_other], axis=1), jnp.stack([from_other, own_part], axis=1)
    )
    new_outputs = jnp.where(is_own, own_out, hop(other_out, CORE))
    return (state[0], state[1], state[2], new_outputs[None])


def hidden_terms(tokens, cotangent, weights, live):
    positions = jnp.arange(tokens.shape[0], dtype=jnp.int32)
    cotangent = jnp.where((positions < live)[:, None], cotangent, jnp.zeros_like(cotangent))
    gate_pre = jnp.dot(tokens, weights[0], preferred_element_type=jnp.float32)
    up_pre = jnp.dot(tokens, weights[1], preferred_element_type=jnp.float32)
    gate_sig = jax.nn.sigmoid(gate_pre)
    gate_act = gate_pre * gate_sig
    hidden = (gate_act * up_pre).astype(jnp.bfloat16)
    grad_down = lax.dot_general(
        cotangent, hidden, (((0,), (0,)), ((), ())), preferred_element_type=jnp.float32
    )
    grad_hidden = jnp.dot(cotangent, weights[2], preferred_element_type=jnp.float32)
    grad_up_pre = (grad_hidden * gate_act).astype(jnp.bfloat16)
    grad_gate_pre = (grad_hidden * up_pre * gate_sig * (1.0 + gate_pre * (1.0 - gate_sig))).astype(
        jnp.bfloat16
    )
    grad_gate = lax.dot_general(
        tokens, grad_gate_pre, (((0,), (0,)), ((), ())), preferred_element_type=jnp.float32
    )
    grad_up = lax.dot_general(
        tokens, grad_up_pre, (((0,), (0,)), ((), ())), preferred_element_type=jnp.float32
    )
    return jnp.stack([grad_gate, grad_up, grad_down])


def expert_forward(tokens, weights):
    gate_pre = jnp.dot(tokens, weights[0], preferred_element_type=jnp.float32)
    up_pre = jnp.dot(tokens, weights[1], preferred_element_type=jnp.float32)
    activation = (jax.nn.silu(gate_pre) * up_pre).astype(jnp.bfloat16)
    result = lax.dot_general(
        activation, weights[2], (((1,), (1,)), ((), ())), preferred_element_type=jnp.float32
    )
    return result.astype(jnp.bfloat16)


def halving(buffer, levels, me_index):
    for step in range(levels):
        count = buffer.shape[2]
        halves = buffer.reshape(buffer.shape[:2] + (count // 2, 2) + buffer.shape[3:])
        own_bit = me_index >> step & 1
        keeping = lax.dynamic_index_in_dim(halves, own_bit, 3, keepdims=False)
        sending = lax.dynamic_index_in_dim(halves, 1 - own_bit, 3, keepdims=False)
        buffer = keeping + hop(sending, 1 << step)
    return buffer


def any_shape(master, first, second, old_rows, old_cotangent, new_rows, old_slots, new_slots, live):
    blocks, kinds, local_rows, block_width = master.shape
    devices = lax.axis_size("dev")
    me_index = lax.axis_index("dev")
    own_old = lax.dynamic_index_in_dim(old_slots, me_index, 0, keepdims=False)
    own_new = lax.dynamic_index_in_dim(new_slots, me_index, 0, keepdims=False)
    every_block = lax.all_gather(master.astype(jnp.bfloat16), "dev", axis=2, tiled=True)
    weights = lax.dynamic_index_in_dim(every_block, own_old, 0, keepdims=False)
    slot_grad = hidden_terms(old_rows, old_cotangent, weights, live[0])
    block_ids = jnp.arange(blocks, dtype=jnp.int32)[:, None, None, None, None]
    dense = slot_grad.reshape(kinds, devices, local_rows, block_width)
    buffer = jnp.where(block_ids == own_old, dense[None], jnp.zeros((), jnp.float32))
    buffer = halving(buffer, devices.bit_length() - 1, me_index)
    grad = buffer.reshape(master.shape)
    new_master, new_first, new_second = adam_update(master, first, second, grad)
    updated_blocks = lax.all_gather(new_master.astype(jnp.bfloat16), "dev", axis=2, tiled=True)
    new_weights = lax.dynamic_index_in_dim(updated_blocks, own_new, 0, keepdims=False)
    return (new_master, new_first, new_second, expert_forward(new_rows, new_weights)[None])


def on_device(
    master,
    first_moment,
    second_moment,
    old_rows,
    old_cotangent,
    new_rows,
    old_slots,
    new_slots,
    live_rows,
):
    blocks, kinds, local_rows, units = master.shape
    devices = lax.axis_size("dev")
    whole_tiles = local_rows % 16 == 0 and units % 128 == 0 and old_rows.shape[1] % 128 == 0
    form = block_a_core if blocks == 2 and devices % (2 * Z_UNIT) == 0 and whole_tiles else any_shape
    return form(
        master,
        first_moment,
        second_moment,
        old_rows[0],
        old_cotangent[0],
        new_rows[0],
        old_slots,
        new_slots,
        live_rows,
    )


def solution(mesh):
    return jax.shard_map(
        on_device,
        mesh=mesh,
        in_specs=(
            P(None, None, "dev", None),
            P(None, None, "dev", None),
            P(None, None, "dev", None),
            P("dev", None, None),
            P("dev", None, None),
            P("dev", None, None),
            P(),
            P(),
            P("dev"),
        ),
        out_specs=(
            P(None, None, "dev", None),
            P(None, None, "dev", None),
            P(None, None, "dev", None),
            P("dev", None, None),
        ),
        check_vma=False,
    )
```

```python
import functools

import jax
import jax.numpy as jnp
from jax import lax
from jax.experimental import pallas as pl
from jax.experimental.pallas import tpu as pltpu
from jax.sharding import PartitionSpec as P

beta_one = 0.9
beta_two = 0.95
corr_one = 0.9999734386011124
corr_two = 0.994079470779666
adam_eps = 1e-08
learn_rate = 0.003
decay_rate = 0.1

CORE, X_STEP, Y_STEP, Z_UNIT = 1, 2, 4, 8
VMEM_LIMIT = 16 * 1024 * 1024


def hop(block, mask):
    count = lax.axis_size("dev")
    return lax.ppermute(block, "dev", [(low, low ^ mask) for low in range(count)])


def adam_update(master, first, second, grad):
    first_new = beta_one * first + (1.0 - beta_one) * grad
    second_new = beta_two * second + (1.0 - beta_two) * grad * grad
    direction = first_new / corr_one / (jnp.sqrt(second_new / corr_two) + adam_eps)
    master_new = master - learn_rate * (direction + decay_rate * master)
    return (master_new, first_new, second_new)


def place_pieces(chip, pieces, weights):
    rows = pieces[0].shape[1]
    for j, piece in enumerate(pieces):
        start = pl.multiple_of(lax.bitwise_xor(chip, j) * rows, rows)
        weights[:, pl.ds(start, rows), :] = piece[...]


def transpose_kernel(own_x, other_x, own_c, other_c, x_turned, c_turned):
    chip = lax.axis_index("dev") // 2
    tokens, width = own_x.shape
    rows = 2 * width // lax.axis_size("dev")
    lanes = max(128, rows)
    for out, pair in ((x_turned, (own_x, other_x)), (c_turned, (own_c, other_c))):
        for part, ref in enumerate(pair):
            for at in range(0, width, lanes):
                turned = ref[:, at : at + lanes].T
                for low in range(0, lanes, rows):
                    j = lax.bitwise_xor(chip, (at + low) // rows)
                    start = pl.multiple_of(j * rows, rows)
                    out[pl.ds(start, rows), part * tokens : (part + 1) * tokens] = turned[low : low + rows]


def places(outs):
    found = []
    for zj in range(len(outs) // 3):
        own, later, pair = outs[3 * zj : 3 * zj + 3]
        by_x, by_y = ((pair, (1,)), (later, ())) if zj % 2 else ((later, ()), (pair, (1,)))
        found += [(own, ()), by_x, by_y, (pair, (0,))]
    return found


def gradient_rows(first_row, products, outs):
    outs = places(outs)
    rows = outs[0][0].shape[1]
    width = len(outs) * rows
    tall = min(width, 256)
    for at in range(0, width, tall):
        for kind, (left, right) in enumerate(products):
            product = jnp.dot(
                left[first_row + at : first_row + at + tall], right[...], preferred_element_type=jnp.float32
            ).astype(jnp.bfloat16)
            for low in range(0, tall, rows):
                out, before = outs[(at + low) // rows]
                out[before + (kind,)] = product[low : low + rows]


def slot_block(slots, slot):
    lane = lax.broadcasted_iota(jnp.int32, slots.shape, 1)
    return jnp.sum(jnp.where(lane == slot, slots[...], 0), axis=1, keepdims=True)


def backward_kernel(count, slots, new_slots, own_live, other_live, *refs):
    pieces = refs[:count]
    own_x, other_x, own_c, other_c, x_turned, c_turned = refs[count : count + 6]
    outs, matches = refs[count + 6 : -5], refs[-5]
    gate_grad, up_grad, hidden_all, weights = refs[-4:]
    me_index = lax.axis_index("dev")
    core = me_index & CORE
    place_pieces(me_index // 2, pieces, weights)
    matches[...] = jnp.where(slot_block(new_slots, me_index) == core, 1, 0)
    tokens = own_x.shape[0]
    sides = ((own_x, own_c, me_index, own_live), (other_x, other_c, me_index ^ CORE, other_live))
    for part, (x_ref, c_ref, slot, live) in enumerate(sides):
        span = slice(part * tokens, (part + 1) * tokens)
        gate_pre = jnp.dot(x_ref[...], weights[0], preferred_element_type=jnp.float32)
        up_pre = jnp.dot(x_ref[...], weights[1], preferred_element_type=jnp.float32)
        grad_hidden = jnp.dot(c_ref[...], weights[2], preferred_element_type=jnp.float32)
        gate_sig = jax.nn.sigmoid(gate_pre)
        gate_act = gate_pre * gate_sig
        alive = jnp.where(slot_block(slots, slot) == core, live[...], 0)
        keep = lax.broadcasted_iota(jnp.int32, gate_pre.shape, 0) < alive
        grad_up = grad_hidden * gate_act
        grad_gate = grad_hidden * up_pre * gate_sig * (1.0 + gate_pre * (1.0 - gate_sig))
        hidden_all[span] = jnp.where(keep, gate_act * up_pre, 0.0).astype(jnp.bfloat16)
        up_grad[span] = jnp.where(keep, grad_up, 0.0).astype(jnp.bfloat16)
        gate_grad[span] = jnp.where(keep, grad_gate, 0.0).astype(jnp.bfloat16)
    products = ((x_turned, gate_grad), (x_turned, up_grad), (c_turned, hidden_all))
    gradient_rows(0, products, outs)


def expert_rows(y_ref, weights, out_ref):
    gate_pre = jnp.dot(y_ref[...], weights[0], preferred_element_type=jnp.float32)
    up_pre = jnp.dot(y_ref[...], weights[1], preferred_element_type=jnp.float32)
    act = (gate_pre * jax.nn.sigmoid(gate_pre) * up_pre).astype(jnp.bfloat16)
    result = lax.dot_general(act, weights[2], (((1,), (1,)), ((), ())), preferred_element_type=jnp.float32)
    out_ref[...] = result.astype(jnp.bfloat16)


def other_kernel(count, *refs):
    pieces = refs[:count]
    other_y, own_y, other_out, weights = refs[count:]
    place_pieces(lax.axis_index("dev") // 2, pieces, weights)
    expert_rows(other_y, weights, other_out)


def own_kernel(weights, own_y, own_out):
    expert_rows(own_y, weights, own_out)


VMEM = pl.BlockSpec(memory_space=pltpu.VMEM)


def params():
    return pltpu.CompilerParams(vmem_limit_bytes=VMEM_LIMIT)


def transposed(own_x, other_x, own_c, other_c):
    tokens, width = own_x.shape
    return pl.pallas_call(
        transpose_kernel,
        out_shape=[jax.ShapeDtypeStruct((width, 2 * tokens), own_x.dtype)] * 2,
        in_specs=[VMEM] * 4,
        out_specs=[VMEM] * 2,
        compiler_params=params(),
        cost_estimate=pl.CostEstimate(flops=0, bytes_accessed=16 * tokens * width, transcendentals=0),
        name="transpose_rows",
    )(own_x, other_x, own_c, other_c)


def backward(slots, new_slots, own_live, other_live, pieces, own_x, other_x, own_c, other_c, x_turned, c_turned):
    count = len(pieces)
    kinds, rows, units = pieces[0].shape
    tokens, width = own_x.shape
    one = jax.ShapeDtypeStruct((kinds, rows, units), jnp.bfloat16)
    two = jax.ShapeDtypeStruct((2, kinds, rows, units), jnp.bfloat16)
    return pl.pallas_call(
        functools.partial(backward_kernel, count),
        out_shape=[one, one, two] * (count // 4) + [jax.ShapeDtypeStruct((1, 1), jnp.int32)],
        in_specs=[VMEM] * (count + 10),
        out_specs=[VMEM] * (3 * count // 4 + 1),
        scratch_shapes=[
            pltpu.VMEM((2 * tokens, units), jnp.bfloat16),
            pltpu.VMEM((2 * tokens, units), jnp.bfloat16),
            pltpu.VMEM((2 * tokens, units), jnp.bfloat16),
            pltpu.VMEM((kinds, width, units), jnp.bfloat16),
        ],
        compiler_params=params(),
        cost_estimate=pl.CostEstimate(
            flops=24 * tokens * width * units,
            bytes_accessed=16 * tokens * width + 12 * width * units,
            transcendentals=2 * tokens * units,
        ),
        name="slot_gradients",
    )(slots, new_slots, own_live, other_live, *pieces, own_x, other_x, own_c, other_c, x_turned, c_turned)


def forward(pieces, own_y, other_y):
    count = len(pieces)
    kinds, rows, units = pieces[0].shape
    tokens, width = own_y.shape
    one = jax.ShapeDtypeStruct((tokens, width), jnp.bfloat16)
    cost = pl.CostEstimate(
        flops=6 * tokens * width * units,
        bytes_accessed=4 * tokens * width + 6 * width * units,
        transcendentals=tokens * units,
    )
    other_out, weights = pl.pallas_call(
        functools.partial(other_kernel, count),
        out_shape=[one, jax.ShapeDtypeStruct((kinds, width, units), jnp.bfloat16)],
        in_specs=[VMEM] * (count + 2),
        out_specs=[VMEM] * 2,
        compiler_params=params(),
        cost_estimate=cost,
        name="other_outputs",
    )(*pieces, other_y, own_y)
    own_out = pl.pallas_call(
        own_kernel,
        out_shape=one,
        in_specs=[VMEM, VMEM],
        out_specs=VMEM,
        compiler_params=params(),
        cost_estimate=cost,
        name="own_outputs",
    )(weights, own_y)
    return own_out, other_out


def after(value, *others):
    return lax.optimization_barrier((value,) + others)[0]


def gather_chips(piece, *first):
    depth = lax.axis_size("dev") // Z_UNIT
    column = [piece] + [None] * (depth - 1)
    for top in reversed([1 << bit for bit in range(depth.bit_length() - 1)]):
        column[top] = hop(piece, top * Z_UNIT)
    along_x, along_y, across = [None] * depth, [None] * depth, [None] * depth
    along_x[0] = hop(piece, X_STEP)
    along_y[0] = hop(piece, Y_STEP)
    along_x[1] = hop(column[1], X_STEP)
    for zj in range(2, depth):
        top = 1 << zj.bit_length() - 1
        if zj != top:
            column[zj] = hop(after(column[top], *first), (zj - top) * Z_UNIT)
    along_y[1] = hop(after(column[1], along_x[0]), Y_STEP)
    for zj in range(2, depth, 2):
        along_x[zj] = hop(after(column[zj], along_x[zj - 2], along_y[zj - 2]), X_STEP)
        across[zj - 2] = hop(after(along_x[zj - 2], along_y[zj - 2]), Y_STEP)
        along_x[zj + 1] = hop(after(column[zj + 1], along_x[zj - 1]), X_STEP)
        along_y[zj + 1] = hop(after(column[zj + 1], along_x[zj - 1]), Y_STEP)
        along_y[zj] = hop(after(column[zj], along_y[zj - 1]), Y_STEP)
        across[zj - 1] = hop(after(along_y[zj - 1], along_x[zj]), X_STEP)
    across[-2] = hop(after(along_x[-2], along_x[-1]), Y_STEP)
    across[-1] = hop(along_y[-1], X_STEP)
    return [part for group in zip(column, along_x, along_y, across) for part in group]


def add_all(first, *others):
    total = first.astype(jnp.float32)
    for other in others:
        total = total + other.astype(jnp.float32)
    return total


def reduce_chips(pieces):
    depth = lax.axis_size("dev") // Z_UNIT
    total, waiting, arrived, crossed = [], [], (), ()
    for upper in reversed(range(1, depth, 2)):
        own_up, up_y, pair_x = pieces[3 * upper : 3 * upper + 3]
        own_low, low_x, pair_y = pieces[3 * upper - 3 : 3 * upper]
        got_x = hop(pair_x, X_STEP)
        got_y = hop(after(pair_y, *arrived), Y_STEP)
        up_y = hop(after(add_all(up_y, got_x[0]).astype(jnp.bfloat16), *crossed), Y_STEP)
        low_x = hop(after(add_all(low_x, got_y[0]).astype(jnp.bfloat16), *crossed), X_STEP)
        arrived, crossed = (got_x,), (low_x,)
        low = [own_low, got_y[1], low_x]
        up = add_all(own_up, got_x[1], up_y).astype(jnp.bfloat16)
        if upper > 1:
            total.append(hop(add_all(*low).astype(jnp.bfloat16), (upper - 1) * Z_UNIT))
            waiting.append((up, upper * Z_UNIT))
        else:
            total += low
            total += [hop(after(part, got_y), mask) for part, mask in waiting]
            total.append(hop(up, Z_UNIT))
    return add_all(*total)


def block_a_core(master, first, second, old_rows, old_cotangent, new_rows, old_slots, new_slots, live):
    local_rows = master.shape[2]
    core = lax.axis_index("dev") & CORE

    def mine(state):
        return lax.dynamic_index_in_dim(state, core, 0, keepdims=False)

    def partners(state):
        return lax.dynamic_index_in_dim(state, 1 - core, 0, keepdims=False)

    def both_rows(own, other):
        return jnp.where(
            core == 0, jnp.concatenate([own, other], axis=-2), jnp.concatenate([other, own], axis=-2)
        )

    other_x = hop(old_rows, CORE)
    other_c = hop(old_cotangent, CORE)
    their_master = hop(partners(master), CORE)
    theirs = hop(jnp.stack([partners(first), partners(second)]), CORE)
    other_y = hop(new_rows, CORE)
    other_live = hop(live, CORE)
    their_master, other_x, other_c, other_y, other_live = lax.optimization_barrier(
        (their_master, other_x, other_c, other_y, other_live)
    )
    x_turned, c_turned = transposed(old_rows, other_x, old_cotangent, other_c)
    master_two = both_rows(mine(master), their_master)
    pieces = gather_chips(master_two.astype(jnp.bfloat16), theirs)
    *grads, matches = backward(
        old_slots[None],
        new_slots[None],
        live[None],
        other_live[None],
        pieces,
        old_rows,
        other_x,
        old_cotangent,
        other_c,
        x_turned,
        c_turned,
    )
    theirs = after(theirs, grads[0])
    first_two = both_rows(mine(first), theirs[0])
    second_two = both_rows(mine(second), theirs[1])
    grad = reduce_chips(grads)
    grad, is_own = lax.optimization_barrier((grad, matches == 1))
    updated = adam_update(master_two, first_two, second_two, grad)

    new_pieces = gather_chips(updated[0].astype(jnp.bfloat16))
    updated = jnp.stack(updated)
    own_part = lax.dynamic_slice_in_dim(updated, core * local_rows, local_rows, 2)
    other_part = lax.dynamic_slice_in_dim(updated, (1 - core) * local_rows, local_rows, 2)
    own_out, other_out = forward(new_pieces, new_rows, other_y)
    from_other = hop(after(other_part, other_out), CORE)
    state = jnp.where(
        core == 0, jnp.stack([own_part, from_other], axis=1), jnp.stack([from_other, own_part], axis=1)
    )
    new_outputs = jnp.where(is_own, own_out, hop(other_out, CORE))
    return (state[0], state[1], state[2], new_outputs[None])


def hidden_terms(tokens, cotangent, weights, live):
    positions = jnp.arange(tokens.shape[0], dtype=jnp.int32)
    cotangent = jnp.where((positions < live)[:, None], cotangent, jnp.zeros_like(cotangent))
    gate_pre = jnp.dot(tokens, weights[0], preferred_element_type=jnp.float32)
    up_pre = jnp.dot(tokens, weights[1], preferred_element_type=jnp.float32)
    gate_sig = jax.nn.sigmoid(gate_pre)
    gate_act = gate_pre * gate_sig
    hidden = (gate_act * up_pre).astype(jnp.bfloat16)
    grad_down = lax.dot_general(
        cotangent, hidden, (((0,), (0,)), ((), ())), preferred_element_type=jnp.float32
    )
    grad_hidden = jnp.dot(cotangent, weights[2], preferred_element_type=jnp.float32)
    grad_up_pre = (grad_hidden * gate_act).astype(jnp.bfloat16)
    grad_gate_pre = (grad_hidden * up_pre * gate_sig * (1.0 + gate_pre * (1.0 - gate_sig))).astype(
        jnp.bfloat16
    )
    grad_gate = lax.dot_general(
        tokens, grad_gate_pre, (((0,), (0,)), ((), ())), preferred_element_type=jnp.float32
    )
    grad_up = lax.dot_general(
        tokens, grad_up_pre, (((0,), (0,)), ((), ())), preferred_element_type=jnp.float32
    )
    return jnp.stack([grad_gate, grad_up, grad_down])


def expert_forward(tokens, weights):
    gate_pre = jnp.dot(tokens, weights[0], preferred_element_type=jnp.float32)
    up_pre = jnp.dot(tokens, weights[1], preferred_element_type=jnp.float32)
    activation = (jax.nn.silu(gate_pre) * up_pre).astype(jnp.bfloat16)
    result = lax.dot_general(
        activation, weights[2], (((1,), (1,)), ((), ())), preferred_element_type=jnp.float32
    )
    return result.astype(jnp.bfloat16)


def halving(buffer, levels, me_index):
    for step in range(levels):
        count = buffer.shape[2]
        halves = buffer.reshape(buffer.shape[:2] + (count // 2, 2) + buffer.shape[3:])
        own_bit = me_index >> step & 1
        keeping = lax.dynamic_index_in_dim(halves, own_bit, 3, keepdims=False)
        sending = lax.dynamic_index_in_dim(halves, 1 - own_bit, 3, keepdims=False)
        buffer = keeping + hop(sending, 1 << step)
    return buffer


def any_shape(master, first, second, old_rows, old_cotangent, new_rows, old_slots, new_slots, live):
    blocks, kinds, local_rows, block_width = master.shape
    devices = lax.axis_size("dev")
    me_index = lax.axis_index("dev")
    own_old = lax.dynamic_index_in_dim(old_slots, me_index, 0, keepdims=False)
    own_new = lax.dynamic_index_in_dim(new_slots, me_index, 0, keepdims=False)
    every_block = lax.all_gather(master.astype(jnp.bfloat16), "dev", axis=2, tiled=True)
    weights = lax.dynamic_index_in_dim(every_block, own_old, 0, keepdims=False)
    slot_grad = hidden_terms(old_rows, old_cotangent, weights, live[0])
    block_ids = jnp.arange(blocks, dtype=jnp.int32)[:, None, None, None, None]
    dense = slot_grad.reshape(kinds, devices, local_rows, block_width)
    buffer = jnp.where(block_ids == own_old, dense[None], jnp.zeros((), jnp.float32))
    buffer = halving(buffer, devices.bit_length() - 1, me_index)
    grad = buffer.reshape(master.shape)
    new_master, new_first, new_second = adam_update(master, first, second, grad)
    updated_blocks = lax.all_gather(new_master.astype(jnp.bfloat16), "dev", axis=2, tiled=True)
    new_weights = lax.dynamic_index_in_dim(updated_blocks, own_new, 0, keepdims=False)
    return (new_master, new_first, new_second, expert_forward(new_rows, new_weights)[None])


def on_device(
    master,
    first_moment,
    second_moment,
    old_rows,
    old_cotangent,
    new_rows,
    old_slots,
    new_slots,
    live_rows,
):
    blocks, kinds, local_rows, units = master.shape
    devices = lax.axis_size("dev")
    whole_tiles = local_rows % 16 == 0 and units % 128 == 0 and old_rows.shape[1] % 128 == 0
    form = block_a_core if blocks == 2 and devices % (2 * Z_UNIT) == 0 and whole_tiles else any_shape
    return form(
        master,
        first_moment,
        second_moment,
        old_rows[0],
        old_cotangent[0],
        new_rows[0],
        old_slots,
        new_slots,
        live_rows,
    )


def solution(mesh):
    return jax.shard_map(
        on_device,
        mesh=mesh,
        in_specs=(
            P(None, None, "dev", None),
            P(None, None, "dev", None),
            P(None, None, "dev", None),
            P("dev", None, None),
            P("dev", None, None),
            P("dev", None, None),
            P(),
            P(),
            P("dev"),
        ),
        out_specs=(
            P(None, None, "dev", None),
            P(None, None, "dev", None),
            P(None, None, "dev", None),
            P("dev", None, None),
        ),
        check_vma=False,
    )
```

```python
import functools

import jax
import jax.numpy as jnp
from jax import lax
from jax.experimental import pallas as pl
from jax.experimental.pallas import tpu as pltpu
from jax.sharding import PartitionSpec as P

beta_one = 0.9
beta_two = 0.95
corr_one = 0.9999734386011124
corr_two = 0.994079470779666
adam_eps = 1e-08
learn_rate = 0.003
decay_rate = 0.1

CORE, X_STEP, Y_STEP, Z_UNIT = 1, 2, 4, 8
VMEM_LIMIT = 16 * 1024 * 1024


def hop(block, mask):
    count = lax.axis_size("dev")
    return lax.ppermute(block, "dev", [(low, low ^ mask) for low in range(count)])


def adam_update(master, first, second, grad):
    first_new = beta_one * first + (1.0 - beta_one) * grad
    second_new = beta_two * second + (1.0 - beta_two) * grad * grad
    direction = first_new / corr_one / (jnp.sqrt(second_new / corr_two) + adam_eps)
    master_new = master - learn_rate * (direction + decay_rate * master)
    return (master_new, first_new, second_new)


def place_pieces(chip, pieces, weights):
    rows = pieces[0].shape[1]
    for j, piece in enumerate(pieces):
        start = pl.multiple_of(lax.bitwise_xor(chip, j) * rows, rows)
        weights[:, pl.ds(start, rows), :] = piece[...]


def transpose_kernel(own_x, other_x, own_c, other_c, x_turned, c_turned):
    chip = lax.axis_index("dev") // 2
    tokens, width = own_x.shape
    rows = 2 * width // lax.axis_size("dev")
    lanes = max(128, rows)
    for out, pair in ((x_turned, (own_x, other_x)), (c_turned, (own_c, other_c))):
        for part, ref in enumerate(pair):
            for at in range(0, width, lanes):
                turned = ref[:, at : at + lanes].T
                for low in range(0, lanes, rows):
                    j = lax.bitwise_xor(chip, (at + low) // rows)
                    start = pl.multiple_of(j * rows, rows)
                    out[pl.ds(start, rows), part * tokens : (part + 1) * tokens] = turned[low : low + rows]


def places(outs):
    found = []
    for zj in range(len(outs) // 3):
        own, later, pair = outs[3 * zj : 3 * zj + 3]
        by_x, by_y = ((pair, (1,)), (later, ())) if zj % 2 else ((later, ()), (pair, (1,)))
        found += [(own, ()), by_x, by_y, (pair, (0,))]
    return found


def gradient_rows(first_row, products, outs):
    outs = places(outs)
    rows = outs[0][0].shape[1]
    width = len(outs) * rows
    tall = min(width, 256)
    for at in range(0, width, tall):
        for kind, (left, right) in enumerate(products):
            product = jnp.dot(
                left[first_row + at : first_row + at + tall], right[...], preferred_element_type=jnp.float32
            ).astype(jnp.bfloat16)
            for low in range(0, tall, rows):
                out, before = outs[(at + low) // rows]
                out[before + (kind,)] = product[low : low + rows]


def slot_block(slots, slot):
    lane = lax.broadcasted_iota(jnp.int32, slots.shape, 1)
    return jnp.sum(jnp.where(lane == slot, slots[...], 0), axis=1, keepdims=True)


def backward_kernel(count, slots, new_slots, own_live, other_live, *refs):
    pieces = refs[:count]
    own_x, other_x, own_c, other_c, x_turned, c_turned = refs[count : count + 6]
    outs, matches = refs[count + 6 : -5], refs[-5]
    gate_grad, up_grad, hidden_all, weights = refs[-4:]
    me_index = lax.axis_index("dev")
    core = me_index & CORE
    place_pieces(me_index // 2, pieces, weights)
    matches[...] = jnp.where(slot_block(new_slots, me_index) == core, 1, 0)
    tokens = own_x.shape[0]
    sides = ((own_x, own_c, me_index, own_live), (other_x, other_c, me_index ^ CORE, other_live))
    for part, (x_ref, c_ref, slot, live) in enumerate(sides):
        span = slice(part * tokens, (part + 1) * tokens)
        gate_pre = jnp.dot(x_ref[...], weights[0], preferred_element_type=jnp.float32)
        up_pre = jnp.dot(x_ref[...], weights[1], preferred_element_type=jnp.float32)
        grad_hidden = jnp.dot(c_ref[...], weights[2], preferred_element_type=jnp.float32)
        gate_sig = jax.nn.sigmoid(gate_pre)
        gate_act = gate_pre * gate_sig
        alive = jnp.where(slot_block(slots, slot) == core, live[...], 0)
        keep = lax.broadcasted_iota(jnp.int32, gate_pre.shape, 0) < alive
        grad_up = grad_hidden * gate_act
        grad_gate = grad_hidden * up_pre * gate_sig * (1.0 + gate_pre * (1.0 - gate_sig))
        hidden_all[span] = jnp.where(keep, gate_act * up_pre, 0.0).astype(jnp.bfloat16)
        up_grad[span] = jnp.where(keep, grad_up, 0.0).astype(jnp.bfloat16)
        gate_grad[span] = jnp.where(keep, grad_gate, 0.0).astype(jnp.bfloat16)
    products = ((x_turned, gate_grad), (x_turned, up_grad), (c_turned, hidden_all))
    gradient_rows(0, products, outs)


def expert_rows(y_ref, weights, out_ref):
    gate_pre = jnp.dot(y_ref[...], weights[0], preferred_element_type=jnp.float32)
    up_pre = jnp.dot(y_ref[...], weights[1], preferred_element_type=jnp.float32)
    act = (gate_pre * jax.nn.sigmoid(gate_pre) * up_pre).astype(jnp.bfloat16)
    result = lax.dot_general(act, weights[2], (((1,), (1,)), ((), ())), preferred_element_type=jnp.float32)
    out_ref[...] = result.astype(jnp.bfloat16)


def other_kernel(count, *refs):
    pieces = refs[:count]
    other_y, own_y, other_out, weights = refs[count:]
    place_pieces(lax.axis_index("dev") // 2, pieces, weights)
    expert_rows(other_y, weights, other_out)


def own_kernel(weights, own_y, own_out):
    expert_rows(own_y, weights, own_out)


VMEM = pl.BlockSpec(memory_space=pltpu.VMEM)


def params():
    return pltpu.CompilerParams(vmem_limit_bytes=VMEM_LIMIT)


def transposed(own_x, other_x, own_c, other_c):
    tokens, width = own_x.shape
    return pl.pallas_call(
        transpose_kernel,
        out_shape=[jax.ShapeDtypeStruct((width, 2 * tokens), own_x.dtype)] * 2,
        in_specs=[VMEM] * 4,
        out_specs=[VMEM] * 2,
        compiler_params=params(),
        cost_estimate=pl.CostEstimate(flops=0, bytes_accessed=16 * tokens * width, transcendentals=0),
        name="transpose_rows",
    )(own_x, other_x, own_c, other_c)


def backward(slots, new_slots, own_live, other_live, pieces, own_x, other_x, own_c, other_c, x_turned, c_turned):
    count = len(pieces)
    kinds, rows, units = pieces[0].shape
    tokens, width = own_x.shape
    one = jax.ShapeDtypeStruct((kinds, rows, units), jnp.bfloat16)
    two = jax.ShapeDtypeStruct((2, kinds, rows, units), jnp.bfloat16)
    return pl.pallas_call(
        functools.partial(backward_kernel, count),
        out_shape=[one, one, two] * (count // 4) + [jax.ShapeDtypeStruct((1, 1), jnp.int32)],
        in_specs=[VMEM] * (count + 10),
        out_specs=[VMEM] * (3 * count // 4 + 1),
        scratch_shapes=[
            pltpu.VMEM((2 * tokens, units), jnp.bfloat16),
            pltpu.VMEM((2 * tokens, units), jnp.bfloat16),
            pltpu.VMEM((2 * tokens, units), jnp.bfloat16),
            pltpu.VMEM((kinds, width, units), jnp.bfloat16),
        ],
        compiler_params=params(),
        cost_estimate=pl.CostEstimate(
            flops=24 * tokens * width * units,
            bytes_accessed=16 * tokens * width + 12 * width * units,
            transcendentals=2 * tokens * units,
        ),
        name="slot_gradients",
    )(slots, new_slots, own_live, other_live, *pieces, own_x, other_x, own_c, other_c, x_turned, c_turned)


def forward(pieces, own_y, other_y):
    count = len(pieces)
    kinds, rows, units = pieces[0].shape
    tokens, width = own_y.shape
    one = jax.ShapeDtypeStruct((tokens, width), jnp.bfloat16)
    cost = pl.CostEstimate(
        flops=6 * tokens * width * units,
        bytes_accessed=4 * tokens * width + 6 * width * units,
        transcendentals=tokens * units,
    )
    other_out, weights = pl.pallas_call(
        functools.partial(other_kernel, count),
        out_shape=[one, jax.ShapeDtypeStruct((kinds, width, units), jnp.bfloat16)],
        in_specs=[VMEM] * (count + 2),
        out_specs=[VMEM] * 2,
        compiler_params=params(),
        cost_estimate=cost,
        name="other_outputs",
    )(*pieces, other_y, own_y)
    own_out = pl.pallas_call(
        own_kernel,
        out_shape=one,
        in_specs=[VMEM, VMEM],
        out_specs=VMEM,
        compiler_params=params(),
        cost_estimate=cost,
        name="own_outputs",
    )(weights, own_y)
    return own_out, other_out


def after(value, *others):
    return lax.optimization_barrier((value,) + others)[0]


def gather_chips(piece, *first):
    depth = lax.axis_size("dev") // Z_UNIT
    column = [piece] + [None] * (depth - 1)
    for top in reversed([1 << bit for bit in range(depth.bit_length() - 1)]):
        column[top] = hop(piece, top * Z_UNIT)
    along_x, along_y, across = [None] * depth, [None] * depth, [None] * depth
    along_x[0] = hop(piece, X_STEP)
    along_y[0] = hop(piece, Y_STEP)
    along_x[1] = hop(column[1], X_STEP)
    for zj in range(2, depth):
        top = 1 << zj.bit_length() - 1
        if zj != top:
            column[zj] = hop(after(column[top], *first), (zj - top) * Z_UNIT)
    along_y[1] = hop(after(column[1], along_x[0]), Y_STEP)
    for zj in range(2, depth, 2):
        along_x[zj] = hop(after(column[zj], along_x[zj - 2], along_y[zj - 2]), X_STEP)
        across[zj - 2] = hop(after(along_x[zj - 2], along_y[zj - 2]), Y_STEP)
        along_x[zj + 1] = hop(after(column[zj + 1], along_x[zj - 1]), X_STEP)
        along_y[zj + 1] = hop(after(column[zj + 1], along_x[zj - 1]), Y_STEP)
        along_y[zj] = hop(after(column[zj], along_y[zj - 1]), Y_STEP)
        across[zj - 1] = hop(after(along_y[zj - 1], along_x[zj]), X_STEP)
    across[-2] = hop(after(along_x[-2], along_x[-1]), Y_STEP)
    across[-1] = hop(along_y[-1], X_STEP)
    return [part for group in zip(column, along_x, along_y, across) for part in group]


def add_all(first, *others):
    total = first.astype(jnp.float32)
    for other in others:
        total = total + other.astype(jnp.float32)
    return total


def reduce_chips(pieces):
    depth = lax.axis_size("dev") // Z_UNIT
    total, waiting, arrived = [], [], ()
    for upper in reversed(range(1, depth, 2)):
        own_up, up_y, pair_x = pieces[3 * upper : 3 * upper + 3]
        own_low, low_x, pair_y = pieces[3 * upper - 3 : 3 * upper]
        got_x = hop(pair_x, X_STEP)
        got_y = hop(after(pair_y, *arrived), Y_STEP)
        up_y = hop(add_all(up_y, got_x[0]).astype(jnp.bfloat16), Y_STEP)
        low_x = hop(add_all(low_x, got_y[0]).astype(jnp.bfloat16), X_STEP)
        arrived = (got_x,)
        low = [own_low, got_y[1], low_x]
        up = add_all(own_up, got_x[1], up_y).astype(jnp.bfloat16)
        if upper > 1:
            waiting += [(add_all(*low).astype(jnp.bfloat16), (upper - 1) * Z_UNIT), (up, upper * Z_UNIT)]
        else:
            total += low
            total += [hop(after(part, got_x if mask & Z_UNIT == 0 else got_y), mask) for part, mask in waiting]
            total.append(hop(up, Z_UNIT))
    return add_all(*total)


def block_a_core(master, first, second, old_rows, old_cotangent, new_rows, old_slots, new_slots, live):
    local_rows = master.shape[2]
    core = lax.axis_index("dev") & CORE

    def mine(state):
        return lax.dynamic_index_in_dim(state, core, 0, keepdims=False)

    def partners(state):
        return lax.dynamic_index_in_dim(state, 1 - core, 0, keepdims=False)

    def both_rows(own, other):
        return jnp.where(
            core == 0, jnp.concatenate([own, other], axis=-2), jnp.concatenate([other, own], axis=-2)
        )

    other_x = hop(old_rows, CORE)
    other_c = hop(old_cotangent, CORE)
    their_master = hop(partners(master), CORE)
    theirs = hop(jnp.stack([partners(first), partners(second)]), CORE)
    other_y = hop(new_rows, CORE)
    other_live = hop(live, CORE)
    their_master, other_x, other_c, other_y, other_live = lax.optimization_barrier(
        (their_master, other_x, other_c, other_y, other_live)
    )
    x_turned, c_turned = transposed(old_rows, other_x, old_cotangent, other_c)
    master_two = both_rows(mine(master), their_master)
    pieces = gather_chips(master_two.astype(jnp.bfloat16), theirs)
    *grads, matches = backward(
        old_slots[None],
        new_slots[None],
        live[None],
        other_live[None],
        pieces,
        old_rows,
        other_x,
        old_cotangent,
        other_c,
        x_turned,
        c_turned,
    )
    theirs = after(theirs, grads[0])
    first_two = both_rows(mine(first), theirs[0])
    second_two = both_rows(mine(second), theirs[1])
    grad = reduce_chips(grads)
    grad, is_own = lax.optimization_barrier((grad, matches == 1))
    updated = adam_update(master_two, first_two, second_two, grad)

    new_pieces = gather_chips(updated[0].astype(jnp.bfloat16))
    updated = jnp.stack(updated)
    own_part = lax.dynamic_slice_in_dim(updated, core * local_rows, local_rows, 2)
    other_part = lax.dynamic_slice_in_dim(updated, (1 - core) * local_rows, local_rows, 2)
    own_out, other_out = forward(new_pieces, new_rows, other_y)
    from_other = hop(after(other_part, other_out), CORE)
    state = jnp.where(
        core == 0, jnp.stack([own_part, from_other], axis=1), jnp.stack([from_other, own_part], axis=1)
    )
    new_outputs = jnp.where(is_own, own_out, hop(other_out, CORE))
    return (state[0], state[1], state[2], new_outputs[None])


def hidden_terms(tokens, cotangent, weights, live):
    positions = jnp.arange(tokens.shape[0], dtype=jnp.int32)
    cotangent = jnp.where((positions < live)[:, None], cotangent, jnp.zeros_like(cotangent))
    gate_pre = jnp.dot(tokens, weights[0], preferred_element_type=jnp.float32)
    up_pre = jnp.dot(tokens, weights[1], preferred_element_type=jnp.float32)
    gate_sig = jax.nn.sigmoid(gate_pre)
    gate_act = gate_pre * gate_sig
    hidden = (gate_act * up_pre).astype(jnp.bfloat16)
    grad_down = lax.dot_general(
        cotangent, hidden, (((0,), (0,)), ((), ())), preferred_element_type=jnp.float32
    )
    grad_hidden = jnp.dot(cotangent, weights[2], preferred_element_type=jnp.float32)
    grad_up_pre = (grad_hidden * gate_act).astype(jnp.bfloat16)
    grad_gate_pre = (grad_hidden * up_pre * gate_sig * (1.0 + gate_pre * (1.0 - gate_sig))).astype(
        jnp.bfloat16
    )
    grad_gate = lax.dot_general(
        tokens, grad_gate_pre, (((0,), (0,)), ((), ())), preferred_element_type=jnp.float32
    )
    grad_up = lax.dot_general(
        tokens, grad_up_pre, (((0,), (0,)), ((), ())), preferred_element_type=jnp.float32
    )
    return jnp.stack([grad_gate, grad_up, grad_down])


def expert_forward(tokens, weights):
    gate_pre = jnp.dot(tokens, weights[0], preferred_element_type=jnp.float32)
    up_pre = jnp.dot(tokens, weights[1], preferred_element_type=jnp.float32)
    activation = (jax.nn.silu(gate_pre) * up_pre).astype(jnp.bfloat16)
    result = lax.dot_general(
        activation, weights[2], (((1,), (1,)), ((), ())), preferred_element_type=jnp.float32
    )
    return result.astype(jnp.bfloat16)


def halving(buffer, levels, me_index):
    for step in range(levels):
        count = buffer.shape[2]
        halves = buffer.reshape(buffer.shape[:2] + (count // 2, 2) + buffer.shape[3:])
        own_bit = me_index >> step & 1
        keeping = lax.dynamic_index_in_dim(halves, own_bit, 3, keepdims=False)
        sending = lax.dynamic_index_in_dim(halves, 1 - own_bit, 3, keepdims=False)
        buffer = keeping + hop(sending, 1 << step)
    return buffer


def any_shape(master, first, second, old_rows, old_cotangent, new_rows, old_slots, new_slots, live):
    blocks, kinds, local_rows, block_width = master.shape
    devices = lax.axis_size("dev")
    me_index = lax.axis_index("dev")
    own_old = lax.dynamic_index_in_dim(old_slots, me_index, 0, keepdims=False)
    own_new = lax.dynamic_index_in_dim(new_slots, me_index, 0, keepdims=False)
    every_block = lax.all_gather(master.astype(jnp.bfloat16), "dev", axis=2, tiled=True)
    weights = lax.dynamic_index_in_dim(every_block, own_old, 0, keepdims=False)
    slot_grad = hidden_terms(old_rows, old_cotangent, weights, live[0])
    block_ids = jnp.arange(blocks, dtype=jnp.int32)[:, None, None, None, None]
    dense = slot_grad.reshape(kinds, devices, local_rows, block_width)
    buffer = jnp.where(block_ids == own_old, dense[None], jnp.zeros((), jnp.float32))
    buffer = halving(buffer, devices.bit_length() - 1, me_index)
    grad = buffer.reshape(master.shape)
    new_master, new_first, new_second = adam_update(master, first, second, grad)
    updated_blocks = lax.all_gather(new_master.astype(jnp.bfloat16), "dev", axis=2, tiled=True)
    new_weights = lax.dynamic_index_in_dim(updated_blocks, own_new, 0, keepdims=False)
    return (new_master, new_first, new_second, expert_forward(new_rows, new_weights)[None])


def on_device(
    master,
    first_moment,
    second_moment,
    old_rows,
    old_cotangent,
    new_rows,
    old_slots,
    new_slots,
    live_rows,
):
    blocks, kinds, local_rows, units = master.shape
    devices = lax.axis_size("dev")
    whole_tiles = local_rows % 16 == 0 and units % 128 == 0 and old_rows.shape[1] % 128 == 0
    form = block_a_core if blocks == 2 and devices % (2 * Z_UNIT) == 0 and whole_tiles else any_shape
    return form(
        master,
        first_moment,
        second_moment,
        old_rows[0],
        old_cotangent[0],
        new_rows[0],
        old_slots,
        new_slots,
        live_rows,
    )


def solution(mesh):
    return jax.shard_map(
        on_device,
        mesh=mesh,
        in_specs=(
            P(None, None, "dev", None),
            P(None, None, "dev", None),
            P(None, None, "dev", None),
            P("dev", None, None),
            P("dev", None, None),
            P("dev", None, None),
            P(),
            P(),
            P("dev"),
        ),
        out_specs=(
            P(None, None, "dev", None),
            P(None, None, "dev", None),
            P(None, None, "dev", None),
            P("dev", None, None),
        ),
        check_vma=False,
    )
```
